128 devices in a mesh: ga: 16 (over z, y_hi, core), ba: 8 (over y_lo, x).
Axes of the slice: x: 4, y: 4 (y_hi: 2, y_lo: 2; y = y_hi * 2 + y_lo), z: 4, core: 2. Of those that a mesh axis runs over, the one named last changes fastest.
Arguments:
- psi_val: bfloat16 [32, 32768], P('ba', 'ga'), may hold values from -6 to 6
- psi_con: bfloat16 [64, 32768], P(None, 'ga'), may hold values from -6 to 6
- e_val: float32 [32], P('ba'), may hold values from -12 to -1
- e_con: float32 [64], replicated, may hold values from 1 to 20
- occ: int32 [32], P('ba'), may hold values 0 or 1
- omega: float32 [8], replicated, may hold values from 0.5 to 20
- g_index: int32 [6144], replicated, may hold values from 0 to 16383
Outputs:
- chi: float32 [8, 6144, 6144], P('ba', 'ga')
The draws below stay inside these ranges and needn't reach their ends.
All inputs are finite; a program needn't handle non-finite values. No bound on the sum of `occ` on one device may be relied on, other than what follows from the above.
Results may differ from the reference program's by a relative error of at most 0.0058.
Values may be sent and summed in bfloat16 or wider, within the bound.
No kernel may reach another device: no remote copies, remote signals or barrier semaphores. Data moves between devices by JAX's collectives and lax.ppermute only.
A program may use at most 128 MiB of HBM per device.

```python
import math
import jax
import jax.numpy as jnp
from jax import lax

NG = 6144
NV = 32
NC = 64
RTOT = 32768
NFREQ = 8


def place_ends(drawn, own_key, smallest, largest):
    longest = drawn.shape.index(max(drawn.shape))
    spots = []
    for shift in (0, 1):
        where = [jax.random.randint(jax.random.fold_in(own_key, axis), (), 0, length) for axis, length in enumerate(drawn.shape)]
        where[longest] = (where[longest] + shift) % drawn.shape[longest]
        spots.append(tuple(where))
    return drawn.at[spots[0]].set(smallest).at[spots[1]].set(largest)


def block_levels(stream_key, dims, pieces, low, top_value):
    gain = 1.0
    for axis_at, shards_of in pieces:
        heights = jax.random.uniform(jax.random.fold_in(jax.random.fold_in(stream_key, 6), axis_at), (shards_of,), jnp.float32, low / len(pieces), top_value / len(pieces))
        gain = gain * jnp.repeat(jnp.exp(heights), dims[axis_at] // shards_of).reshape((-1,) + (1,) * (len(dims) - 1 - axis_at))
    return gain


def bell_draw(key, dims, deviation, limit, split=(), held_as=jnp.bfloat16):
    array = deviation * jax.random.normal(key, dims, jnp.float32)
    if split:
        array = array * block_levels(key, dims, split, -0.22, 0.18)
    return jnp.clip(array, -limit, limit).astype(held_as)


def setup_inputs(seed: int = 0) -> dict:
    key_list = jax.random.split(jax.random.key(seed), 8)
    psi_val = bell_draw(key_list[0], (NV, RTOT), 1.0, 6.0, ((0, 8), (1, 16)))
    psi_con = bell_draw(key_list[1], (NC, RTOT), 1.0, 6.0, ((1, 16),))
    e_val = jnp.clip(-12.0 + 11.0 * jax.random.uniform(key_list[2], (NV,), jnp.float32) ** block_levels(key_list[2], (NV,), ((0, 8),), -0.2, 0.2), -12.0, -1.0)
    e_con = jnp.clip(jax.random.uniform(key_list[3], (NC,), jnp.float32, 1.0, 20.0), 1.0, 20.0)
    occ = place_ends((jax.random.randint(key_list[4], (NV,), 0, 4) < 3).astype(jnp.int32), jax.random.fold_in(key_list[4], 1), 0, 1)
    omega = jnp.clip(jnp.exp(jax.random.uniform(key_list[5], (NFREQ,), jnp.float32, math.log(0.5), math.log(20.0))), 0.5, 20.0)
    g_index = place_ends(jax.random.randint(key_list[6], (NG,), 0, RTOT // 2), jax.random.fold_in(key_list[6], 1), 0, (RTOT // 2) - 1).astype(jnp.int32)
    return {"psi_val": psi_val, "psi_con": psi_con, "e_val": e_val, "e_con": e_con, "occ": occ, "omega": omega, "g_index": g_index}


def reference(psi_val, psi_con, e_val, e_con, occ, omega, g_index):
    grid_total = psi_val.shape[1]
    density = (psi_val.astype(jnp.float32)[:, None, :] * psi_con.astype(jnp.float32)[None, :, :]).astype(jnp.bfloat16)
    density = lax.optimization_barrier(density).reshape(NV * NC, grid_total).astype(jnp.float32)
    positions = jnp.arange(grid_total, dtype=jnp.int32)
    row_block = math.gcd(NG, 512)
    norm_factor = math.sqrt(2.0 / grid_total)
    two_pi = 2.0 * math.pi

    def one_block(kvals):
        phase = kvals[:, None] * positions[None, :] % grid_total
        table = (jnp.cos(phase.astype(jnp.float32) * (two_pi / grid_total)) * norm_factor).astype(jnp.bfloat16)
        table = lax.optimization_barrier(table).astype(jnp.float32)
        return jnp.dot(table, density.T, preferred_element_type=jnp.float32)
    rho = lax.map(one_block, g_index.reshape(NG // row_block, row_block)).reshape(NG, NV * NC)
    delta = e_con[None, :] - e_val[:, None]
    occf = occ.astype(jnp.float32)[:, None]
    root = jnp.sqrt(4.0 * occf[None] * delta[None] / (delta[None] * delta[None] + omega[:, None, None] * omega[:, None, None]) / math.sqrt(NV * NC))
    root = root.reshape(omega.shape[0], NV * NC)

    def one_freq(weights):
        scaled = (rho * weights[None, :]).astype(jnp.bfloat16)
        scaled = lax.optimization_barrier(scaled).astype(jnp.float32)
        return -jnp.dot(scaled, scaled.T, preferred_element_type=jnp.float32)
    return lax.map(one_freq, root)
```

```python
import functools
import math

import jax
import jax.numpy as jnp
import numpy as np
from jax import lax
from jax.experimental import pallas as pl
from jax.experimental.pallas import tpu as pltpu
from jax.sharding import PartitionSpec as P

NV = 32
NC = 64
N = 32768
NA = 128
NB = 256
NG = 6144
LANES = 128
PAIRS = 16
PARTS = (2048, 2048, 2176)
BLOCK = 512
AXES = ("z", "y", "x")
ORDERS = (("x", "y", "z"), ("y", "z", "x"), ("z", "x", "y"))
STRIDES = tuple({o[0]: 16, o[1]: 64, o[2]: 256} for o in ORDERS)


def split_bf16(a):
    hi = a.astype(np.float32).astype(jnp.bfloat16)
    lo = (a - hi.astype(np.float64)).astype(np.float32).astype(jnp.bfloat16)
    return hi, lo


def dft_constants():
    k1 = np.arange(NA)[:, None]
    ang = 2.0 * math.pi * ((k1 * np.arange(NA)[None, :]) % NA) / NA
    fh, fl = split_bf16(np.concatenate([np.cos(ang), np.sin(ang)], 0))
    first = np.concatenate([fh, fl], 1)
    tw = 2.0 * math.pi * ((k1 * np.arange(NB)[None, :]) % N) / N
    norm = math.sqrt(2.0 / N)
    tcos = (np.cos(tw) * norm).astype(np.float32)
    tsin = (np.sin(tw) * norm).astype(np.float32)
    b2 = 2.0 * math.pi * ((np.arange(NB)[:, None] * np.arange(NA)[None, :]) % NB) / NB
    sh, sl = split_bf16(np.concatenate([np.cos(b2), -np.sin(b2)], 0))
    second = np.concatenate([sh, sl, sh], 0)
    return first, tcos, tsin, second


def rho_kernel(psi, gidx, meta, first, tcos, tsin, second, out0, out1, out2, spec):
    bands = [psi[:, i].astype(jnp.float32).reshape(NA, NB) for i in range(8)]
    ca = tcos[...]
    sa = tsin[...]
    for p in range(PAIRS):
        d = (bands[p // 4] * bands[4 + p % 4]).astype(jnp.bfloat16)
        y = jnp.dot(first[...], jnp.concatenate([d, d], 0), preferred_element_type=jnp.float32)
        a, b = y[:NA], y[NA:]
        uv = jnp.concatenate([a * ca - b * sa, a * sa + b * ca], 1)
        hi = uv.astype(jnp.bfloat16)
        lo = (uv - hi.astype(jnp.float32)).astype(jnp.bfloat16)
        x = jnp.dot(
            jnp.concatenate([hi, hi, lo], 1), second[...], preferred_element_type=jnp.float32
        ).astype(jnp.bfloat16)
        spec[p * 64 : p * 64 + 64, 0:128] = x[:64]
        spec[p * 64 : p * 64 + 64, 128:256] = x[64:]
    width = 256
    base = 0
    for out, cols in ((out0, 2048), (out1, 2048), (out2, 2048)):

        def pick(i, carry, out=out, base=base):
            g = gidx[:, pl.ds(pl.multiple_of(base + i * width, width), width)]
            k1 = lax.bitwise_and(g, 127)
            k2 = lax.shift_right_logical(g, 7)
            kk = lax.shift_right_logical(k1, 6) * 128 + k2
            hot = jnp.where(
                lax.broadcasted_iota(jnp.int32, (256, width), 0) == kk, 1.0, 0.0
            ).astype(jnp.bfloat16)
            o = jnp.dot(spec[...], hot, preferred_element_type=jnp.float32)
            m = lax.broadcasted_iota(jnp.int32, (64, width), 0) == lax.bitwise_and(k1, 63)
            picked = jnp.sum(jnp.where(m[None], o.reshape(PAIRS, 64, width), 0.0), axis=1)
            out[:, pl.ds(pl.multiple_of(i * width, width), width)] = picked.astype(jnp.bfloat16)
            return carry

        lax.fori_loop(0, cols // width, pick, 0)
        base += cols
    out2[:, 2048:2176] = meta[...]


def rho_parts(psi, gidx, meta):
    first, tcos, tsin, second = dft_constants()
    vm = pl.BlockSpec(memory_space=pltpu.VMEM)
    return pl.pallas_call(
        rho_kernel,
        out_shape=[jax.ShapeDtypeStruct((PAIRS, c), jnp.bfloat16) for c in PARTS],
        in_specs=[vm] * 7,
        out_specs=[vm] * 3,
        scratch_shapes=[pltpu.VMEM((PAIRS * 64, 256), jnp.bfloat16)],
        compiler_params=pltpu.CompilerParams(vmem_limit_bytes=32 * 1024 * 1024),
        name="rho_pairs",
    )(psi, gidx, meta, *(jnp.asarray(c) for c in (first, tcos, tsin, second)))


def device_index(z, y, x, c):
    return (z * 4 + (y >> 1) * 2 + c) * 8 + (y & 1) * 4 + x


@functools.cache
def ring_pairs(axis, way):
    pairs = []
    for z in range(4):
        for y in range(4):
            for x in range(4):
                for c in range(2):
                    to = {"z": z, "y": y, "x": x}
                    to[axis] = (to[axis] + (way if c == 0 else -way)) % 4
                    pairs.append((device_index(z, y, x, c), device_index(to["z"], to["y"], to["x"], c)))
    return tuple(pairs)


@functools.cache
def core_pairs():
    return tuple(
        (device_index(z, y, x, c), device_index(z, y, x, 1 - c))
        for z in range(4) for y in range(4) for x in range(4) for c in range(2)
    )


def send(a, pairs):
    return lax.ppermute(a, ("ga", "ba"), pairs)


def ring_gather(a, axis):
    near = send(a, ring_pairs(axis, 1))
    other = send(a, ring_pairs(axis, -1))
    far = send(near, ring_pairs(axis, 1))
    return [a, near, other, far]


def chi_kernel(*refs):
    place, omega = refs[0], refs[1]
    pieces = [[refs[2 + t * 8 + q] for q in range(8)] for t in range(3)]
    out = refs[26]
    raw, meta, weight, left, left_t, right, result, sem_raw, sem_meta, sem_right, sem_out = refs[27:]
    block0 = place[0] * 3

    def right_copies(t, i, slot):
        return [
            pltpu.make_async_copy(
                pieces[t][q].at[:, pl.ds(pl.multiple_of(i * BLOCK, BLOCK), BLOCK)],
                right.at[slot, pl.ds(q * 256, 256), :],
                sem_right.at[slot, q],
            )
            for q in range(8)
        ]

    def raw_copy(e, t, q):
        lane = (block0 + e - 16 * t) * LANES
        return pltpu.make_async_copy(
            pieces[t][q].at[:, pl.ds(pl.multiple_of(lane, LANES), LANES)],
            raw.at[e, pl.ds(q * 256, 256), :],
            sem_raw.at[e, q],
        )

    meta_copies = [
        pltpu.make_async_copy(
            pieces[2][q].at[:, pl.ds(2048, LANES)], meta.at[pl.ds(q * 256, 256), :], sem_meta.at[q]
        )
        for q in range(8)
    ]
    for copy in meta_copies:
        copy.start()
    for e in range(3):
        for t in range(3):

            @pl.when((block0 + e) // 16 == t)
            def _(e=e, t=t):
                for q in range(8):
                    raw_copy(e, t, q).start()

    for copy in right_copies(0, 0, 0):
        copy.start()

    for copy in meta_copies:
        copy.wait()
    w2 = omega[0] * omega[0]
    for q in range(8):
        m = meta[q * 256 : q * 256 + 256, :].astype(jnp.float32)
        delta = m[:, 0:1] + m[:, 1:2] + m[:, 2:3]
        w = -4.0 * m[:, 3:4] * delta / (delta * delta + w2) / math.sqrt(NV * NC)
        weight[q * 256 : q * 256 + 256, :] = jnp.broadcast_to(w, (256, LANES))

    for e in range(3):
        for t in range(3):

            @pl.when((block0 + e) // 16 == t)
            def _(e=e, t=t):
                for q in range(8):
                    raw_copy(e, t, q).wait()

        part = (block0 + e) // 16
        sz, sy, sx = (
            jnp.where(part == 0, STRIDES[0][a], jnp.where(part == 1, STRIDES[1][a], STRIDES[2][a]))
            for a in AXES
        )

        def reorder(n, carry, e=e, sz=sz, sy=sy, sx=sx):
            z, y, x = n // 16, (n // 4) % 4, n % 4
            for core in range(2):
                src = pl.multiple_of(core * 1024 + z * sz + y * sy + x * sx, 16)
                wsrc = pl.multiple_of(
                    core * 1024 + z * STRIDES[2]["z"] + y * STRIDES[2]["y"] + x * STRIDES[2]["x"], 16
                )
                dst = pl.multiple_of(core * 1024 + n * 16, 16)
                left[pl.ds(dst, 16), e * LANES : (e + 1) * LANES] = (
                    raw[e, pl.ds(src, 16), :].astype(jnp.float32) * weight[pl.ds(wsrc, 16), :]
                ).astype(jnp.bfloat16)
            return carry

        lax.fori_loop(0, 64, reorder, 0, unroll=4)

    for t in range(3):
        first, second, last = ORDERS[t]
        for core in range(2):
            for d3 in range(4):
                rows = []
                for d2 in range(4):
                    for d1 in range(4):
                        at = {first: d1, second: d2, last: d3}
                        src = core * 1024 + sum(STRIDES[0][a] * at[a] for a in AXES)
                        rows.append(left[src : src + 16, :])
                block = jnp.concatenate(rows, 0)
                k = core * 1024 + d3 * 256
                left_t[t, :, k : k + 256] = block.T

    steps = 2048 // BLOCK
    for t in range(3):

        def step(i, carry, t=t):
            n = t * steps + i
            slot = lax.rem(n, 2)
            for copy in right_copies(t, i, slot):
                copy.wait()

            @pl.when(i < steps - 1)
            def _():
                for copy in right_copies(t, i + 1, 1 - slot):
                    copy.start()

            if t < 2:

                @pl.when(i == steps - 1)
                def _():
                    for copy in right_copies(t + 1, 0, 1 - slot):
                        copy.start()

            def out_copy(n):
                s = lax.rem(n, 2)
                return pltpu.make_async_copy(
                    result.at[s],
                    out.at[:, pl.ds(pl.multiple_of(n * BLOCK, BLOCK), BLOCK)],
                    sem_out.at[s],
                )

            @pl.when(n >= 2)
            def _():
                out_copy(n - 2).wait()

            result[slot] = jnp.dot(left_t[t], right[slot], preferred_element_type=jnp.float32)
            out_copy(n).start()
            return carry

        lax.fori_loop(0, steps, step, 0)
    for n in (3 * steps - 2, 3 * steps - 1):
        pltpu.make_async_copy(
            result.at[n % 2], out.at[:, pl.ds(n * BLOCK, BLOCK)], sem_out.at[n % 2]
        ).wait()


def chi_rows(place, omega, pieces):
    smem = pl.BlockSpec(memory_space=pltpu.SMEM)
    hbm = pl.BlockSpec(memory_space=pl.ANY)
    return pl.pallas_call(
        chi_kernel,
        out_shape=jax.ShapeDtypeStruct((384, NG), jnp.float32),
        in_specs=[smem, smem] + [hbm] * 24,
        out_specs=hbm,
        scratch_shapes=[
            pltpu.VMEM((3, 2048, LANES), jnp.bfloat16),
            pltpu.VMEM((2048, LANES), jnp.bfloat16),
            pltpu.VMEM((2048, LANES), jnp.float32),
            pltpu.VMEM((2048, 384), jnp.bfloat16),
            pltpu.VMEM((3, 384, 2048), jnp.bfloat16),
            pltpu.VMEM((2, 2048, BLOCK), jnp.bfloat16),
            pltpu.VMEM((2, 384, BLOCK), jnp.float32),
            pltpu.SemaphoreType.DMA((3, 8)),
            pltpu.SemaphoreType.DMA((8,)),
            pltpu.SemaphoreType.DMA((2, 8)),
            pltpu.SemaphoreType.DMA((2,)),
        ],
        compiler_params=pltpu.CompilerParams(vmem_limit_bytes=32 * 1024 * 1024),
        cost_estimate=pl.CostEstimate(
            flops=2 * 384 * NG * 2048, bytes_accessed=35 * 1024 * 1024, transcendentals=0
        ),
        name="chi_rows",
    )(place, omega, *pieces)


def on_device(psi_val, psi_con, e_val, e_con, occ, omega, g_index):
    ga = lax.axis_index("ga")
    ba = lax.axis_index("ba")
    con = psi_con.reshape(16, 4, 8, NB)
    val = jnp.broadcast_to(psi_val.reshape(1, 4, 8, NB), (16, 4, 8, NB))
    psi = lax.all_to_all(jnp.concatenate([val, con], 1), "ga", 0, 0, tiled=True)

    delta = (lax.dynamic_slice(e_con, (ga * 4,), (4,))[None, :] - e_val[:, None]).reshape(PAIRS)
    taken = jnp.broadcast_to(occ.astype(jnp.float32)[:, None], (4, 4)).reshape(PAIRS)
    d1 = lax.reduce_precision(delta, 8, 7)
    d2 = lax.reduce_precision(delta - d1, 8, 7)
    d3 = delta - d1 - d2
    meta = jnp.stack([d1, d2, d3, taken], 1).astype(jnp.bfloat16)
    meta = jnp.pad(meta, ((0, 0), (0, LANES - 4)))

    parts = rho_parts(psi, g_index.reshape(1, NG), meta)

    pieces = []
    for t in range(3):
        first, second, last = ORDERS[t]
        a = jnp.concatenate(ring_gather(parts[t], first), 0)
        a = jnp.concatenate(ring_gather(a, second), 0)
        mine = ring_gather(a, last)
        pieces += mine + [send(b, core_pairs()) for b in mine]

    place = ga.astype(jnp.int32).reshape(1)
    mine_omega = lax.dynamic_slice(omega, (ba,), (1,))
    return chi_rows(place, mine_omega, pieces)[None]


def solution(mesh):
    placed = (P("ba", "ga"), P(None, "ga"), P("ba"), P(), P("ba"), P(), P())
    return jax.shard_map(
        on_device, mesh=mesh, in_specs=placed, out_specs=P("ba", "ga", None), check_vma=False
    )
```

```python
import functools
import math

import jax
import jax.numpy as jnp
import numpy as np
from jax import lax
from jax.experimental import pallas as pl
from jax.experimental.pallas import tpu as pltpu
from jax.sharding import PartitionSpec as P

NV = 32
NC = 64
N = 32768
NA = 128
NB = 256
NG = 6144
HALF = NG // 2
LANES = 128
PAIRS = 16
PARTS = (1024, 1024, 1152)
WIDE = HALF + LANES
AXES = ("z", "y", "x")
ORDERS = (("x", "y", "z"), ("y", "z", "x"), ("z", "x", "y"))
STRIDES = tuple({o[0]: 32, o[1]: 128, o[2]: 512} for o in ORDERS)
K = 2048
MIB = 1024 * 1024
VM = pl.BlockSpec(memory_space=pltpu.VMEM)
SM = pl.BlockSpec(memory_space=pltpu.SMEM)
HBM = pl.BlockSpec(memory_space=pltpu.HBM)


def split_bf16(a):
    hi = a.astype(np.float32).astype(jnp.bfloat16)
    lo = (a - hi.astype(np.float64)).astype(np.float32).astype(jnp.bfloat16)
    return hi, lo


def dft_constants():
    k1 = np.arange(NA)[:, None]
    ang = 2.0 * math.pi * ((k1 * np.arange(NA)[None, :]) % NA) / NA
    fh, fl = split_bf16(np.concatenate([np.cos(ang), np.sin(ang)], 0))
    first = np.concatenate([fh, fl], 1)
    tw = 2.0 * math.pi * ((k1 * np.arange(NB)[None, :]) % N) / N
    norm = math.sqrt(2.0 / N)
    tcos = (np.cos(tw) * norm).astype(np.float32)
    tsin = (np.sin(tw) * norm).astype(np.float32)
    b2 = 2.0 * math.pi * ((np.arange(NB)[:, None] * np.arange(NA)[None, :]) % NB) / NB
    sh, sl = split_bf16(np.concatenate([np.cos(b2), -np.sin(b2)], 0))
    second = np.concatenate([sh, sl, sh], 0)
    return first, tcos, tsin, second


def transform(psi, first, tcos, tsin, second, spec):
    bands = [psi[:, i].astype(jnp.float32).reshape(NA, NB) for i in range(8)]
    ca = tcos[...]
    sa = tsin[...]
    for p in range(PAIRS):
        d = (bands[p // 4] * bands[4 + p % 4]).astype(jnp.bfloat16)
        y = jnp.dot(first[...], jnp.concatenate([d, d], 0), preferred_element_type=jnp.float32)
        a, b = y[:NA], y[NA:]
        uv = jnp.concatenate([a * ca - b * sa, a * sa + b * ca], 1)
        hi = uv.astype(jnp.bfloat16)
        lo = (uv - hi.astype(jnp.float32)).astype(jnp.bfloat16)
        x = jnp.dot(
            jnp.concatenate([hi, hi, lo], 1), second[...], preferred_element_type=jnp.float32
        ).astype(jnp.bfloat16)
        spec[p * 64 : p * 64 + 64, 0:128] = x[:64]
        spec[p * 64 : p * 64 + 64, 128:256] = x[64:]


def pick(spec, gidx, meta, out):
    width = 256

    def step(i, carry):
        at = pl.ds(pl.multiple_of(i * width, width), width)
        g = gidx[:, at]
        k1 = lax.bitwise_and(g, 127)
        kk = lax.shift_right_logical(k1, 6) * 128 + lax.shift_right_logical(g, 7)
        hot = jnp.where(
            lax.broadcasted_iota(jnp.int32, (256, width), 0) == kk, 1.0, 0.0
        ).astype(jnp.bfloat16)
        o = jnp.dot(spec[...], hot, preferred_element_type=jnp.float32)
        m = lax.broadcasted_iota(jnp.int32, (64, width), 0) == lax.bitwise_and(k1, 63)
        picked = jnp.sum(jnp.where(m[None], o.reshape(PAIRS, 64, width), 0.0), axis=1)
        out[:, at] = picked.astype(jnp.bfloat16)
        return carry

    lax.fori_loop(0, HALF // width, step, 0)
    out[:, HALF:WIDE] = meta[...]


def transform_kernel(psi, gidx, meta, first, tcos, tsin, second, spec, out):
    transform(psi, first, tcos, tsin, second, spec)
    pick(spec, gidx, meta, out)


def rho_spectrum(psi, gidx, meta):
    return pl.pallas_call(
        transform_kernel,
        out_shape=[
            jax.ShapeDtypeStruct((PAIRS * 64, 256), jnp.bfloat16),
            jax.ShapeDtypeStruct((PAIRS, WIDE), jnp.bfloat16),
        ],
        in_specs=[VM] * 7,
        out_specs=[VM] * 2,
        compiler_params=pltpu.CompilerParams(vmem_limit_bytes=24 * MIB),
        name="rho_spectrum",
    )(psi, gidx, meta, *(jnp.asarray(c) for c in dft_constants()))


def rho_pick(spec, gidx, meta):
    return pl.pallas_call(
        pick,
        out_shape=jax.ShapeDtypeStruct((PAIRS, WIDE), jnp.bfloat16),
        in_specs=[VM] * 3,
        out_specs=VM,
        compiler_params=pltpu.CompilerParams(vmem_limit_bytes=24 * MIB),
        name="rho_pick",
    )(spec, gidx, meta)


def device_index(z, y, x, c):
    return (z * 4 + (y >> 1) * 2 + c) * 8 + (y & 1) * 4 + x


@functools.cache
def ring_pairs(axis, way):
    pairs = []
    for z in range(4):
        for y in range(4):
            for x in range(4):
                for c in range(2):
                    to = {"z": z, "y": y, "x": x}
                    to[axis] = (to[axis] + (way if c == 0 else -way)) % 4
                    pairs.append((device_index(z, y, x, c), device_index(to["z"], to["y"], to["x"], c)))
    return tuple(pairs)


@functools.cache
def core_pairs():
    return tuple(
        (device_index(z, y, x, c), device_index(z, y, x, 1 - c))
        for z in range(4) for y in range(4) for x in range(4) for c in range(2)
    )


def send(a, pairs):
    return lax.ppermute(a, ("ga", "ba"), pairs)


def ring_gather(a, axis):
    near = send(a, ring_pairs(axis, 1))
    other = send(a, ring_pairs(axis, -1))
    far = send(near, ring_pairs(axis, 1))
    return [a, near, other, far]


def in_vmem(a):
    return pltpu.with_memory_space_constraint(a, pltpu.VMEM)


def weighted_kernel(place, omega, *refs):
    pieces = [refs[4 * t : 4 * t + 4] for t in range(3)]
    left, weight = refs[12:]
    block0 = place[0] * 3
    w2 = omega[0] * omega[0]
    for d3 in range(4):
        m = pieces[2][d3][:, 1024:1152].astype(jnp.float32)
        delta = m[:, 0:1] + m[:, 1:2] + m[:, 2:3]
        w = -4.0 * m[:, 3:4] * delta / (delta * delta + w2) / math.sqrt(NV * NC)
        weight[d3 * 512 : d3 * 512 + 512, :] = jnp.broadcast_to(w, (512, LANES))
    for e in range(3):
        block = block0 + e
        for t in range(3):

            @pl.when(block // 8 == t)
            def _(e=e, t=t, block=block):
                lane = pl.ds(pl.multiple_of((block - 8 * t) * LANES, LANES), LANES)
                for n in range(64):
                    at = {"z": n // 16, "y": (n // 4) % 4, "x": n % 4}
                    src = sum(STRIDES[t][a] * at[a] for a in AXES)
                    wsrc = sum(STRIDES[2][a] * at[a] for a in AXES)
                    left[n * 32 : n * 32 + 32, e * LANES : (e + 1) * LANES] = (
                        pieces[t][src // 512][src % 512 : src % 512 + 32, lane].astype(jnp.float32)
                        * weight[wsrc : wsrc + 32, :]
                    ).astype(jnp.bfloat16)


def weighted(place, omega, pieces):
    return pl.pallas_call(
        weighted_kernel,
        out_shape=jax.ShapeDtypeStruct((K, 384), jnp.bfloat16),
        in_specs=[SM, SM] + [VM] * 12,
        out_specs=VM,
        scratch_shapes=[pltpu.VMEM((K, LANES), jnp.float32)],
        compiler_params=pltpu.CompilerParams(vmem_limit_bytes=24 * MIB),
        name="weighted",
    )(place, omega, *pieces)


SWAPPED = (0, 2, 1, 3)


def transposed(left, t, left_t, other):
    first, second, last = ORDERS[t]
    for d3 in range(4):
        rows = []
        for d2 in range(4):
            for d1 in range(4):
                at = {first: d1, second: d2, last: d3}
                if other:
                    src = sum(STRIDES[0][a] * SWAPPED[at[a]] for a in AXES)
                    rows += [left[src + 16 : src + 32, :], left[src : src + 16, :]]
                else:
                    src = sum(STRIDES[0][a] * at[a] for a in AXES)
                    rows.append(left[src : src + 32, :])
        left_t[:, d3 * 512 : d3 * 512 + 512] = jnp.concatenate(rows, 0).T


def product(left_t, pieces, cols):
    acc = jnp.dot(left_t[:, 0:512], pieces[0][:, cols], preferred_element_type=jnp.float32)
    for d3 in range(1, 4):
        acc += jnp.dot(
            left_t[:, d3 * 512 : d3 * 512 + 512], pieces[d3][:, cols], preferred_element_type=jnp.float32
        )
    return acc


def out_lane(block, half):
    return (block // 3) * 6 + half * 3 + lax.rem(block, 3)


def own_kernel(core, left, *refs):
    pieces = [refs[4 * t : 4 * t + 4] for t in range(3)]
    out, left_t, result, sem = refs[12:]
    half = core[0]

    def copies(n):
        slot = lax.rem(n, 2)
        return [
            pltpu.make_async_copy(
                result.at[slot, :, pl.ds(j * LANES, LANES)],
                out.at[:, pl.ds(pl.multiple_of(out_lane(n * 4 + j, half) * LANES, LANES), LANES)],
                sem.at[slot, j],
            )
            for j in range(4)
        ]

    for t in range(3):
        transposed(left, t, left_t, False)

        def step(i, carry, t=t):
            n = t * 2 + i

            @pl.when(n >= 2)
            def _():
                for copy in copies(n - 2):
                    copy.wait()

            for j in range(2):
                cols = pl.ds(pl.multiple_of(i * 512 + j * 256, 256), 256)
                result[lax.rem(n, 2), :, j * 256 : j * 256 + 256] = product(left_t, pieces[t], cols)
            for copy in copies(n):
                copy.start()
            return carry

        lax.fori_loop(0, 2, step, 0)
    for n in (4, 5):
        for copy in copies(n):
            copy.wait()


def own_half(core, left, pieces):
    return pl.pallas_call(
        own_kernel,
        out_shape=jax.ShapeDtypeStruct((384, NG), jnp.float32),
        in_specs=[SM, VM] + [VM] * 12,
        out_specs=HBM,
        scratch_shapes=[
            pltpu.VMEM((384, K), jnp.bfloat16),
            pltpu.VMEM((2, 384, 512), jnp.float32),
            pltpu.SemaphoreType.DMA((2, 4)),
        ],
        compiler_params=pltpu.CompilerParams(vmem_limit_bytes=24 * MIB),
        cost_estimate=pl.CostEstimate(flops=2 * 384 * HALF * K, bytes_accessed=20 * MIB, transcendentals=0),
        name="own_half",
    )(core, left, *pieces)


def other_kernel(t, left, p0, p1, p2, p3, out, left_t):
    transposed(left, t, left_t, True)

    def step(i, carry):
        cols = pl.ds(pl.multiple_of(i * 256, 256), 256)
        out[:, cols] = product(left_t, (p0, p1, p2, p3), cols).astype(jnp.bfloat16)
        return carry

    lax.fori_loop(0, 4, step, 0)


def other_rows(t, left, pieces):
    return pl.pallas_call(
        functools.partial(other_kernel, t),
        out_shape=jax.ShapeDtypeStruct((384, 1024), jnp.bfloat16),
        in_specs=[VM] * 5,
        out_specs=VM,
        scratch_shapes=[pltpu.VMEM((384, K), jnp.bfloat16)],
        compiler_params=pltpu.CompilerParams(vmem_limit_bytes=24 * MIB),
        cost_estimate=pl.CostEstimate(flops=2 * 384 * 1024 * K, bytes_accessed=6 * MIB, transcendentals=0),
        name="other_rows",
    )(left, *pieces)


def finish_kernel(core, r0, r1, r2, _, out, wide, sem):
    half = 1 - core[0]

    def copies(t):
        return [
            pltpu.make_async_copy(
                wide.at[t, :, pl.ds(j * LANES, LANES)],
                out.at[:, pl.ds(pl.multiple_of(out_lane(t * 8 + j, half) * LANES, LANES), LANES)],
                sem.at[t, j],
            )
            for j in range(8)
        ]

    for t, r in enumerate((r0, r1, r2)):
        for j, copy in enumerate(copies(t)):
            at = slice(j * LANES, j * LANES + LANES)
            wide[t, :, at] = r[:, at].astype(jnp.float32)
            copy.start()
    for t in range(3):
        for copy in copies(t):
            copy.wait()


def finish(core, rows, out):
    return pl.pallas_call(
        finish_kernel,
        out_shape=jax.ShapeDtypeStruct((384, NG), jnp.float32),
        in_specs=[SM, VM, VM, VM, HBM],
        out_specs=HBM,
        scratch_shapes=[pltpu.VMEM((3, 384, 1024), jnp.float32), pltpu.SemaphoreType.DMA((3, 8))],
        input_output_aliases={4: 0},
        compiler_params=pltpu.CompilerParams(vmem_limit_bytes=24 * MIB),
        name="finish",
    )(core, *rows, out)


def on_device(psi_val, psi_con, e_val, e_con, occ, omega, g_index):
    ga = lax.axis_index("ga")
    ba = lax.axis_index("ba")
    core = lax.rem(ga, 2).astype(jnp.int32)
    con = psi_con.reshape(16, 4, 8, NB)
    val = jnp.broadcast_to(psi_val.reshape(1, 4, 8, NB), (16, 4, 8, NB))
    psi = lax.all_to_all(jnp.concatenate([val, con], 1), "ga", 0, 0, tiled=True)

    delta = (lax.dynamic_slice(e_con, (ga * 4,), (4,))[None, :] - e_val[:, None]).reshape(PAIRS)
    taken = jnp.broadcast_to(occ.astype(jnp.float32)[:, None], (4, 4)).reshape(PAIRS)
    d1 = lax.reduce_precision(delta, 8, 7)
    d2 = lax.reduce_precision(delta - d1, 8, 7)
    d3 = delta - d1 - d2
    meta = jnp.stack([d1, d2, d3, taken], 1).astype(jnp.bfloat16)
    meta = jnp.pad(meta, ((0, 0), (0, LANES - 4)))

    halves = g_index.reshape(8, 2, 384).transpose(1, 0, 2).reshape(2, HALF)
    kept = lax.dynamic_slice(halves, (core, 0), (1, HALF))
    given = lax.dynamic_slice(halves, (1 - core, 0), (1, HALF))
    spec, give = rho_spectrum(psi, given, meta)
    got = send(give, core_pairs())
    keep = rho_pick(spec, kept, meta)

    pieces = []
    start = 0
    for t in range(3):
        first, second, last = ORDERS[t]
        cols = slice(start, start + PARTS[t])
        start += PARTS[t]
        a = jnp.concatenate([keep[:, cols], got[:, cols]], 0)
        a = jnp.concatenate(ring_gather(a, first), 0)
        a = jnp.concatenate(ring_gather(a, second), 0)
        pieces.append([in_vmem(b) for b in ring_gather(a, last)])
    everything = pieces[0] + pieces[1] + pieces[2]

    place = lax.div(ga, 2).astype(jnp.int32).reshape(1)
    mine_omega = lax.dynamic_slice(omega, (ba,), (1,))
    left = weighted(place, mine_omega, everything)
    left_other = send(left, core_pairs())
    out = own_half(core.reshape(1), left, everything)
    rows = [send(other_rows(t, left_other, pieces[t]), core_pairs()) for t in range(3)]
    return finish(core.reshape(1), rows, out)[None]


def solution(mesh):
    placed = (P("ba", "ga"), P(None, "ga"), P("ba"), P(), P("ba"), P(), P())
    return jax.shard_map(
        on_device, mesh=mesh, in_specs=placed, out_specs=P("ba", "ga", None), check_vma=False
    )
```

```python
import functools
import math

import jax
import jax.numpy as jnp
import numpy as np
from jax import lax
from jax.experimental import pallas as pl
from jax.experimental.pallas import tpu as pltpu
from jax.sharding import PartitionSpec as P

NV = 32
NC = 64
N = 32768
NA = 128
NB = 256
NG = 6144
HALF = NG // 2
LANES = 128
PAIRS = 16
PARTS = (1024, 1024, 1152)
WIDE = HALF + LANES
AXES = ("z", "y", "x")
ORDERS = (("x", "y", "z"), ("y", "z", "x"), ("z", "x", "y"))
STRIDES = tuple({o[0]: 32, o[1]: 128, o[2]: 512} for o in ORDERS)
K = 2048
MIB = 1024 * 1024
VM = pl.BlockSpec(memory_space=pltpu.VMEM)
SM = pl.BlockSpec(memory_space=pltpu.SMEM)
HBM = pl.BlockSpec(memory_space=pltpu.HBM)


def split_bf16(a):
    hi = a.astype(np.float32).astype(jnp.bfloat16)
    lo = (a - hi.astype(np.float64)).astype(np.float32).astype(jnp.bfloat16)
    return hi, lo


def dft_constants():
    k1 = np.arange(NA)[:, None]
    ang = 2.0 * math.pi * ((k1 * np.arange(NA)[None, :]) % NA) / NA
    fh, fl = split_bf16(np.concatenate([np.cos(ang), np.sin(ang)], 0))
    first = np.concatenate([fh, fl], 1)
    tw = 2.0 * math.pi * ((k1 * np.arange(NB)[None, :]) % N) / N
    norm = math.sqrt(2.0 / N)
    tcos = (np.cos(tw) * norm).astype(np.float32)
    tsin = (np.sin(tw) * norm).astype(np.float32)
    b2 = 2.0 * math.pi * ((np.arange(NB)[:, None] * np.arange(NA)[None, :]) % NB) / NB
    sh, sl = split_bf16(np.concatenate([np.cos(b2), -np.sin(b2)], 0))
    second = np.concatenate([sh, sl, sh], 0)
    return first, tcos, tsin, second


def transform(psi, first, tcos, tsin, second, spec):
    bands = [psi[:, i].astype(jnp.float32).reshape(NA, NB) for i in range(8)]
    ca = tcos[...]
    sa = tsin[...]
    for p in range(PAIRS):
        d = (bands[p // 4] * bands[4 + p % 4]).astype(jnp.bfloat16)
        y = jnp.dot(first[...], jnp.concatenate([d, d], 0), preferred_element_type=jnp.float32)
        a, b = y[:NA], y[NA:]
        uv = jnp.concatenate([a * ca - b * sa, a * sa + b * ca], 1)
        hi = uv.astype(jnp.bfloat16)
        lo = (uv - hi.astype(jnp.float32)).astype(jnp.bfloat16)
        x = jnp.dot(
            jnp.concatenate([hi, hi, lo], 1), second[...], preferred_element_type=jnp.float32
        ).astype(jnp.bfloat16)
        spec[p * 64 : p * 64 + 64, 0:128] = x[:64]
        spec[p * 64 : p * 64 + 64, 128:256] = x[64:]


def pick(spec, gidx, meta, out):
    width = 256

    def step(i, carry):
        at = pl.ds(pl.multiple_of(i * width, width), width)
        g = gidx[:, at]
        k1 = lax.bitwise_and(g, 127)
        kk = lax.shift_right_logical(k1, 6) * 128 + lax.shift_right_logical(g, 7)
        hot = jnp.where(
            lax.broadcasted_iota(jnp.int32, (256, width), 0) == kk, 1.0, 0.0
        ).astype(jnp.bfloat16)
        o = jnp.dot(spec[...], hot, preferred_element_type=jnp.float32)
        m = lax.broadcasted_iota(jnp.int32, (64, width), 0) == lax.bitwise_and(k1, 63)
        picked = jnp.sum(jnp.where(m[None], o.reshape(PAIRS, 64, width), 0.0), axis=1)
        out[:, at] = picked.astype(jnp.bfloat16)
        return carry

    lax.fori_loop(0, HALF // width, step, 0)
    out[:, HALF:WIDE] = meta[...]


def transform_kernel(psi, gidx, meta, first, tcos, tsin, second, spec, out):
    transform(psi, first, tcos, tsin, second, spec)
    pick(spec, gidx, meta, out)


def rho_spectrum(psi, gidx, meta):
    return pl.pallas_call(
        transform_kernel,
        out_shape=[
            jax.ShapeDtypeStruct((PAIRS * 64, 256), jnp.bfloat16),
            jax.ShapeDtypeStruct((PAIRS, WIDE), jnp.bfloat16),
        ],
        in_specs=[VM] * 7,
        out_specs=[VM] * 2,
        compiler_params=pltpu.CompilerParams(vmem_limit_bytes=24 * MIB),
        name="rho_spectrum",
    )(psi, gidx, meta, *(jnp.asarray(c) for c in dft_constants()))


def rho_pick(spec, gidx, meta):
    return pl.pallas_call(
        pick,
        out_shape=jax.ShapeDtypeStruct((PAIRS, WIDE), jnp.bfloat16),
        in_specs=[VM] * 3,
        out_specs=VM,
        compiler_params=pltpu.CompilerParams(vmem_limit_bytes=24 * MIB),
        name="rho_pick",
    )(spec, gidx, meta)


def device_index(z, y, x, c):
    return (z * 4 + (y >> 1) * 2 + c) * 8 + (y & 1) * 4 + x


@functools.cache
def ring_pairs(axis, way):
    pairs = []
    for z in range(4):
        for y in range(4):
            for x in range(4):
                for c in range(2):
                    to = {"z": z, "y": y, "x": x}
                    to[axis] = (to[axis] + (way if c == 0 else -way)) % 4
                    pairs.append((device_index(z, y, x, c), device_index(to["z"], to["y"], to["x"], c)))
    return tuple(pairs)


@functools.cache
def core_pairs():
    return tuple(
        (device_index(z, y, x, c), device_index(z, y, x, 1 - c))
        for z in range(4) for y in range(4) for x in range(4) for c in range(2)
    )


def send(a, pairs):
    return lax.ppermute(a, ("ga", "ba"), pairs)


def far_pairs(axis):
    pairs = []
    for z in range(4):
        for y in range(4):
            for x in range(4):
                for c in range(2):
                    to = {"z": z, "y": y, "x": x}
                    to[axis] = (to[axis] + 2) % 4
                    pairs.append((device_index(z, y, x, c), device_index(to["z"], to["y"], to["x"], c)))
    return tuple(pairs)


def direct_gather(a, axis):
    pairs = (ring_pairs(axis, 1), ring_pairs(axis, -1), far_pairs(axis))
    return jnp.concatenate([a] + [send(a, p) for p in pairs], 0)


def ring_gather(a, axis):
    near = send(a, ring_pairs(axis, 1))
    other = send(a, ring_pairs(axis, -1))
    far = send(near, ring_pairs(axis, 1))
    return [a, near, other, far]


def in_vmem(a):
    return pltpu.with_memory_space_constraint(a, pltpu.VMEM)


def weighted_kernel(place, omega, *refs):
    pieces = [refs[4 * t : 4 * t + 4] for t in range(3)]
    left, weight = refs[12:]
    cols = pl.ds(pl.multiple_of(place[0] * LANES, LANES), LANES)
    w2 = omega[0] * omega[0]
    row = lax.broadcasted_iota(jnp.int32, (LANES, 2 * LANES), 0)
    lane = lax.broadcasted_iota(jnp.int32, (LANES, 2 * LANES), 1)
    spread = jnp.where((row < 3) & (lane < LANES) | (row == 3) & (lane >= LANES), 1.0, 0.0)
    spread = spread.astype(jnp.bfloat16)
    for d3 in range(4):
        m = jnp.dot(pieces[2][d3][:, 1024:1152], spread, preferred_element_type=jnp.float32)
        delta, taken = m[:, :LANES], m[:, LANES:]
        weight[d3 * 512 : d3 * 512 + 512, :] = (
            (-4.0 / math.sqrt(NV * NC)) * taken * delta / (delta * delta + w2)
        )
    for t in range(3):
        for n in range(64):
            at = {"z": n // 16, "y": (n // 4) % 4, "x": n % 4}
            src, dst, wsrc = (sum(STRIDES[o][a] * at[a] for a in AXES) for o in (t, 0, 2))
            block = pieces[t][src // 512][src % 512 : src % 512 + 32, cols].astype(jnp.float32)
            left[dst : dst + 32, t * LANES : (t + 1) * LANES] = (
                block * weight[wsrc : wsrc + 32, :]
            ).astype(jnp.bfloat16)


def weighted(place, omega, pieces):
    return pl.pallas_call(
        weighted_kernel,
        out_shape=jax.ShapeDtypeStruct((K, 384), jnp.bfloat16),
        in_specs=[SM, SM] + [VM] * 12,
        out_specs=VM,
        scratch_shapes=[pltpu.VMEM((K, LANES), jnp.float32)],
        compiler_params=pltpu.CompilerParams(vmem_limit_bytes=24 * MIB),
        name="weighted",
    )(place, omega, *pieces)


SWAPPED = (0, 2, 1, 3)


def product(left, pieces, t, other):
    first, second, last = ORDERS[t]
    acc = None
    for d3 in range(4):
        rows = []
        for d2 in range(4):
            for d1 in range(4):
                at = {first: d1, second: d2, last: d3}
                if other:
                    src = sum(STRIDES[0][a] * SWAPPED[at[a]] for a in AXES)
                    rows += [left[src + 16 : src + 32, :], left[src : src + 16, :]]
                else:
                    src = sum(STRIDES[0][a] * at[a] for a in AXES)
                    rows.append(left[src : src + 32, :])
        term = lax.dot_general(
            jnp.concatenate(rows, 0),
            pieces[d3][:, :1024],
            (((0,), (0,)), ((), ())),
            preferred_element_type=jnp.float32,
        )
        acc = term if acc is None else acc + term
    return acc


def part_copies(t, half, wide, out, sem):
    return [
        pltpu.make_async_copy(
            wide.at[:, pl.ds(j * LANES, LANES)],
            out.at[:, pl.ds(pl.multiple_of(((j * 2 + half) * 3 + t) * LANES, LANES), LANES)],
            sem.at[j],
        )
        for j in range(8)
    ]


def own_kernel(parts, core, left, *refs):
    n = len(parts)
    out, wide, sem = refs[-3:]
    for i, t in enumerate(parts):
        wide[i] = product(left, refs[4 * i : 4 * i + 4], t, False)
        for copy in part_copies(t, core[0], wide.at[i], out, sem.at[i]):
            copy.start()
    for i, t in enumerate(parts):
        for copy in part_copies(t, core[0], wide.at[i], out, sem.at[i]):
            copy.wait()


def own_rows(parts, core, left, pieces, out):
    n = len(parts)
    before = [] if out is None else [out]
    return pl.pallas_call(
        functools.partial(own_kernel, parts),
        out_shape=jax.ShapeDtypeStruct((384, NG), jnp.float32),
        in_specs=[SM, VM] + [VM] * (4 * n) + [HBM] * len(before),
        out_specs=HBM,
        scratch_shapes=[pltpu.VMEM((n, 384, 1024), jnp.float32), pltpu.SemaphoreType.DMA((n, 8))],
        input_output_aliases={2 + 4 * n: 0} if before else {},
        compiler_params=pltpu.CompilerParams(vmem_limit_bytes=24 * MIB),
        cost_estimate=pl.CostEstimate(
            flops=n * 2 * 384 * 1024 * K, bytes_accessed=n * 6 * MIB, transcendentals=0
        ),
        name="own_rows",
    )(core, left, *[p for t in parts for p in pieces[t]], *before)


def other_kernel(t, left, p0, p1, p2, p3, _, out):
    out[...] = product(left, (p0, p1, p2, p3), t, True).astype(jnp.bfloat16)


def other_rows(t, left, pieces, after):
    return pl.pallas_call(
        functools.partial(other_kernel, t),
        out_shape=jax.ShapeDtypeStruct((384, 1024), jnp.bfloat16),
        in_specs=[VM] * 5 + [HBM],
        out_specs=VM,
        compiler_params=pltpu.CompilerParams(vmem_limit_bytes=24 * MIB),
        cost_estimate=pl.CostEstimate(flops=2 * 384 * 1024 * K, bytes_accessed=6 * MIB, transcendentals=0),
        name="other_rows",
    )(left, *pieces, after)


def finish_kernel(core, r0, r1, r2, _, out, wide, sem):
    for t, r in enumerate((r0, r1, r2)):
        copies = part_copies(t, 1 - core[0], wide.at[t], out, sem.at[t])
        for j, copy in enumerate(copies):
            at = slice(j * LANES, j * LANES + LANES)
            wide[t, :, at] = r[:, at].astype(jnp.float32)
            copy.start()
    for t in range(3):
        for copy in part_copies(t, 1 - core[0], wide.at[t], out, sem.at[t]):
            copy.wait()


def finish(core, rows, out):
    return pl.pallas_call(
        finish_kernel,
        out_shape=jax.ShapeDtypeStruct((384, NG), jnp.float32),
        in_specs=[SM, VM, VM, VM, HBM],
        out_specs=HBM,
        scratch_shapes=[pltpu.VMEM((3, 384, 1024), jnp.float32), pltpu.SemaphoreType.DMA((3, 8))],
        input_output_aliases={4: 0},
        compiler_params=pltpu.CompilerParams(vmem_limit_bytes=24 * MIB),
        name="finish",
    )(core, *rows, out)


def on_device(psi_val, psi_con, e_val, e_con, occ, omega, g_index):
    ga = lax.axis_index("ga")
    ba = lax.axis_index("ba")
    core = lax.rem(ga, 2).astype(jnp.int32)
    con = psi_con.reshape(16, 4, 8, NB)
    val = jnp.broadcast_to(psi_val.reshape(1, 4, 8, NB), (16, 4, 8, NB))
    psi = lax.all_to_all(jnp.concatenate([val, con], 1), "ga", 0, 0, tiled=True)

    delta = (lax.dynamic_slice(e_con, (ga * 4,), (4,))[None, :] - e_val[:, None]).reshape(PAIRS)
    taken = jnp.broadcast_to(occ.astype(jnp.float32)[:, None], (4, 4)).reshape(PAIRS)
    d1 = lax.reduce_precision(delta, 8, 7)
    d2 = lax.reduce_precision(delta - d1, 8, 7)
    d3 = delta - d1 - d2
    meta = jnp.stack([d1, d2, d3, taken], 1).astype(jnp.bfloat16)
    meta = jnp.pad(meta, ((0, 0), (0, LANES - 4)))

    halves = g_index.reshape(8, 2, 3, LANES).transpose(1, 2, 0, 3).reshape(2, HALF)
    kept = lax.dynamic_slice(halves, (core, 0), (1, HALF))
    given = lax.dynamic_slice(halves, (1 - core, 0), (1, HALF))
    spec, give = rho_spectrum(psi, given, meta)
    got = send(give, core_pairs())
    keep = rho_pick(spec, kept, meta)

    pieces = []
    start = 0
    for t in range(3):
        first, second, last = ORDERS[t]
        cols = slice(start, start + PARTS[t])
        start += PARTS[t]
        a = jnp.concatenate([keep[:, cols], got[:, cols]], 0)
        a = direct_gather(direct_gather(a, first), second)
        pieces.append([in_vmem(b) for b in ring_gather(a, last)])
    everything = pieces[0] + pieces[1] + pieces[2]

    place = lax.div(ga, 2).astype(jnp.int32).reshape(1)
    mine_omega = lax.dynamic_slice(omega, (ba,), (1,))
    core = core.reshape(1)
    left = weighted(place, mine_omega, everything)
    left_other = send(left, core_pairs())
    out = own_rows((0,), core, left, pieces, None)
    rows = [send(other_rows(t, left_other, pieces[t], out), core_pairs()) for t in range(3)]
    out = own_rows((1, 2), core, left, pieces, out)
    return finish(core, rows, out)[None]


def solution(mesh):
    placed = (P("ba", "ga"), P(None, "ga"), P("ba"), P(), P("ba"), P(), P())
    return jax.shard_map(
        on_device, mesh=mesh, in_specs=placed, out_specs=P("ba", "ga", None), check_vma=False
    )
```

```python
import functools
import itertools
import math

import jax
import jax.numpy as jnp
import numpy as np
from jax import lax
from jax.experimental import pallas as pl
from jax.experimental.pallas import tpu as pltpu
from jax.sharding import PartitionSpec as P

NV = 32
NC = 64
N = 32768
NA = 128
NB = 256
NG = 6144
HALF = NG // 2
ROWS = 384
LANES = 128
PAIRS = 16
WIDE = HALF + LANES
BLOCK = 2 * PAIRS
CHUNK = 768
MIB = 1024 * 1024
VM = pl.BlockSpec(memory_space=pltpu.VMEM)
SM = pl.BlockSpec(memory_space=pltpu.SMEM)
HBM = pl.BlockSpec(memory_space=pltpu.HBM)
PARAMS = pltpu.CompilerParams(vmem_limit_bytes=14 * MIB)

NEAR = ((0, 0, 0), (2, 2, 2), (1, 1, 1), (3, 3, 3))
EVEN = ((0, 0, 0), (2, 0, 0), (0, 2, 0), (0, 0, 2))
STEP = ((0, 0, 0), (1, 0, 0), (0, 1, 0), (0, 0, 1))


def split_bf16(a):
    hi = a.astype(np.float32).astype(jnp.bfloat16)
    lo = (a - hi.astype(np.float64)).astype(np.float32).astype(jnp.bfloat16)
    return hi, lo


def dft_constants():
    k1 = np.arange(NA)[:, None]
    ang = 2.0 * math.pi * ((k1 * np.arange(NA)[None, :]) % NA) / NA
    fh, fl = split_bf16(np.concatenate([np.cos(ang), np.sin(ang)], 0))
    first = np.concatenate([fh, fl], 1)
    tw = 2.0 * math.pi * ((k1 * np.arange(NB)[None, :]) % N) / N
    norm = math.sqrt(2.0 / N)
    tcos = (np.cos(tw) * norm).astype(np.float32)
    tsin = (np.sin(tw) * norm).astype(np.float32)
    b2 = 2.0 * math.pi * ((np.arange(NB)[:, None] * np.arange(NA)[None, :]) % NB) / NB
    sh, sl = split_bf16(np.concatenate([np.cos(b2), -np.sin(b2)], 0))
    second = np.concatenate([sh, sl, sh], 0)
    return first, tcos, tsin, second


def transform(psi, first, tcos, tsin, second, spec):
    bands = [psi[:, i].astype(jnp.float32).reshape(NA, NB) for i in range(8)]
    ca = tcos[...]
    sa = tsin[...]
    for p in range(PAIRS):
        d = (bands[p // 4] * bands[4 + p % 4]).astype(jnp.bfloat16)
        y = jnp.dot(first[...], jnp.concatenate([d, d], 0), preferred_element_type=jnp.float32)
        a, b = y[:NA], y[NA:]
        uv = jnp.concatenate([a * ca - b * sa, a * sa + b * ca], 1)
        hi = uv.astype(jnp.bfloat16)
        lo = (uv - hi.astype(jnp.float32)).astype(jnp.bfloat16)
        x = jnp.dot(
            jnp.concatenate([hi, hi, lo], 1), second[...], preferred_element_type=jnp.float32
        ).astype(jnp.bfloat16)
        spec[p * 64 : p * 64 + 64, 0:128] = x[:64]
        spec[p * 64 : p * 64 + 64, 128:256] = x[64:]


def pick(spec, gidx, meta, out):
    width = 256

    def step(i, carry):
        at = pl.ds(pl.multiple_of(i * width, width), width)
        g = gidx[:, at]
        k1 = lax.bitwise_and(g, 127)
        kk = lax.shift_right_logical(k1, 6) * 128 + lax.shift_right_logical(g, 7)
        hot = jnp.where(
            lax.broadcasted_iota(jnp.int32, (256, width), 0) == kk, 1.0, 0.0
        ).astype(jnp.bfloat16)
        o = jnp.dot(spec[...], hot, preferred_element_type=jnp.float32)
        m = lax.broadcasted_iota(jnp.int32, (64, width), 0) == lax.bitwise_and(k1, 63)
        picked = jnp.sum(jnp.where(m[None], o.reshape(PAIRS, 64, width), 0.0), axis=1)
        out[:, at] = picked.astype(jnp.bfloat16)
        return carry

    lax.fori_loop(0, HALF // width, step, 0)
    out[:, HALF:WIDE] = meta[...]


def transform_kernel(psi, gidx, meta, first, tcos, tsin, second, spec, out):
    transform(psi, first, tcos, tsin, second, spec)
    pick(spec, gidx, meta, out)


def rho_spectrum(psi, gidx, meta):
    return pl.pallas_call(
        transform_kernel,
        out_shape=[
            jax.ShapeDtypeStruct((PAIRS * 64, 256), jnp.bfloat16),
            jax.ShapeDtypeStruct((PAIRS, WIDE), jnp.bfloat16),
        ],
        in_specs=[VM] * 7,
        out_specs=[VM] * 2,
        compiler_params=PARAMS,
        name="rho_spectrum",
    )(psi, gidx, meta, *(jnp.asarray(c) for c in dft_constants()))


def rho_pick(spec, gidx, meta):
    return pl.pallas_call(
        pick,
        out_shape=jax.ShapeDtypeStruct((PAIRS, WIDE), jnp.bfloat16),
        in_specs=[VM] * 3,
        out_specs=VM,
        compiler_params=PARAMS,
        name="rho_pick",
    )(spec, gidx, meta)


def device_index(x, y, z, c):
    return (z * 4 + (y >> 1) * 2 + c) * 8 + (y & 1) * 4 + x


CHIPS = tuple(itertools.product(range(4), repeat=3))


@functools.cache
def offset_pairs(offset):
    return tuple(
        (device_index(*chip, c), device_index(*((a + (1 - 2 * c) * b) % 4 for a, b in zip(chip, offset)), c))
        for chip in CHIPS for c in range(2)
    )


@functools.cache
def core_pairs():
    return tuple((device_index(*chip, c), device_index(*chip, 1 - c)) for chip in CHIPS for c in range(2))


def send(a, pairs):
    return lax.ppermute(a, ("ga", "ba"), pairs)


def level(a, offsets):
    return [a] + [send(a, offset_pairs(offset)) for offset in offsets[1:]]


def join_kernel(n, *refs):
    out = refs[n]
    row = 0
    for ref in refs[:n]:
        out[row : row + ref.shape[0], :] = ref[...]
        row += ref.shape[0]


def join(blocks):
    rows = sum(b.shape[0] for b in blocks)
    return pl.pallas_call(
        functools.partial(join_kernel, len(blocks)),
        out_shape=jax.ShapeDtypeStruct((rows, WIDE), jnp.bfloat16),
        in_specs=[VM] * len(blocks),
        out_specs=VM,
        compiler_params=PARAMS,
        name="join",
    )(*blocks)


def deal_kernel(b0, b1, b2, b3, out0, out1):
    for i, ref in enumerate((b0, b1, b2, b3)):
        out0[i * 64 : i * 64 + 64, :] = ref[0:64, :]
        out1[i * 64 : i * 64 + 64, :] = ref[64:128, :]


def deal(blocks):
    return pl.pallas_call(
        deal_kernel,
        out_shape=[jax.ShapeDtypeStruct((256, WIDE), jnp.bfloat16)] * 2,
        in_specs=[VM] * 4,
        out_specs=[VM] * 2,
        compiler_params=PARAMS,
        name="deal",
    )(*blocks)


def place_of(half, step):
    return [
        tuple(sum(v) % 4 for v in zip(NEAR[2 * half + i], EVEN[j], STEP[step]))
        for j in range(4) for i in range(2)
    ]


def mirrored(half, step):
    places = place_of(half, step)
    return [places.index(tuple(-v % 4 for v in p)) for p in places]


def weighted_kernel(place, omega, *refs):
    pieces, left = refs[:-2], refs[-1]
    w2 = omega[0] * omega[0]
    row = lax.broadcasted_iota(jnp.int32, (LANES, 2 * LANES), 0)
    lane = lax.broadcasted_iota(jnp.int32, (LANES, 2 * LANES), 1)
    spread = jnp.where((row < 3) & (lane < LANES) | (row == 3) & (lane >= LANES), 1.0, 0.0)
    spread = spread.astype(jnp.bfloat16)
    for i, piece in enumerate(pieces):
        m = jnp.dot(piece[:, HALF:WIDE], spread, preferred_element_type=jnp.float32)
        delta, taken = m[:, :LANES], m[:, LANES:]
        weight = (-4.0 / math.sqrt(NV * NC)) * taken * delta / (delta * delta + w2)
        for e in range(3):
            cols = pl.ds(pl.multiple_of(place[0] * ROWS + e * LANES, LANES), LANES)
            left[i * 256 : i * 256 + 256, e * LANES : (e + 1) * LANES] = (
                piece[:, cols].astype(jnp.float32) * weight
            ).astype(jnp.bfloat16)


def weighted(place, omega, pieces, tie):
    return pl.pallas_call(
        weighted_kernel,
        out_shape=jax.ShapeDtypeStruct((256 * len(pieces), ROWS), jnp.bfloat16),
        in_specs=[SM, SM] + [VM] * (len(pieces) + 1),
        out_specs=VM,
        compiler_params=PARAMS,
        name="weighted",
    )(place, omega, *pieces, tie)


def product(names, other, left, pieces, cols):
    total = None
    for i, (half, step) in enumerate(names):
        if other:
            rows = []
            for j in mirrored(half, step):
                at = i * 256 + j * BLOCK
                rows += [left[at + PAIRS : at + BLOCK, :], left[at : at + PAIRS, :]]
            mine = jnp.concatenate(rows, 0)
        else:
            mine = left[i * 256 : i * 256 + 256, :]
        term = lax.dot_general(
            mine, pieces[i][:, cols], (((0,), (0,)), ((), ())), preferred_element_type=jnp.float32
        )
        total = term if total is None else total + term
    return total


def chunk(i, width=CHUNK, start=0):
    return pl.ds(pl.multiple_of(start + i * width, LANES), width)


def cost(names, columns):
    return pl.CostEstimate(
        flops=2 * ROWS * columns * 256 * len(names),
        bytes_accessed=(2 * 256 * len(names) + 8 * ROWS) * columns,
        transcendentals=0,
    )


def partial_kernel(names, other, left, *refs):
    pieces, before = refs[: len(names)], refs[len(names) : -3]
    out, after = refs[-2:]
    after[...] = jnp.zeros_like(after)

    def step(i, carry):
        total = product(names, other, left, pieces, chunk(i))
        out[:, chunk(i)] = total + before[0][:, chunk(i)] if before else total
        return carry

    lax.fori_loop(0, HALF // CHUNK, step, 0)


TIE = jax.ShapeDtypeStruct((8, LANES), jnp.float32)


def partial_rows(names, other, left, pieces, before, tie):
    before = [] if before is None else [before]
    return pl.pallas_call(
        functools.partial(partial_kernel, names, other),
        out_shape=[jax.ShapeDtypeStruct((ROWS, HALF), jnp.float32), TIE],
        in_specs=[VM] * (2 + len(names) + len(before)),
        out_specs=[VM] * 2,
        input_output_aliases={1 + len(names): 0} if before else {},
        compiler_params=PARAMS,
        cost_estimate=cost(names, HALF),
        name="partial_other" if other else "partial_own",
    )(left, *pieces, *before, tie)


def own_kernel(names, core, left, *refs):
    pieces = refs[: len(names)]
    before, out, tie, wide, sem = refs[len(names) :]
    tie[...] = jnp.zeros_like(tie)

    def copies(i):
        slot = lax.rem(i, 2)
        return [
            pltpu.make_async_copy(
                wide.at[slot, :, pl.ds(j * ROWS, ROWS)],
                out.at[:, pl.ds(pl.multiple_of(((i * 2 + j) * 2 + core[0]) * ROWS, LANES), ROWS)],
                sem.at[slot, j],
            )
            for j in range(2)
        ]

    def step(i, carry):
        @pl.when(i >= 2)
        def _():
            for copy in copies(i - 2):
                copy.wait()

        wide[lax.rem(i, 2)] = product(names, False, left, pieces, chunk(i)) + before[:, chunk(i)]
        for copy in copies(i):
            copy.start()
        return carry

    lax.fori_loop(0, 4, step, 0)
    for i in (2, 3):
        for copy in copies(i):
            copy.wait()


def own_rows(names, core, left, pieces, before):
    return pl.pallas_call(
        functools.partial(own_kernel, names),
        out_shape=[jax.ShapeDtypeStruct((ROWS, NG), jnp.float32), TIE],
        in_specs=[SM, VM] + [VM] * (len(names) + 1),
        out_specs=[HBM, VM],
        scratch_shapes=[pltpu.VMEM((2, ROWS, CHUNK), jnp.float32), pltpu.SemaphoreType.DMA((2, 2))],
        compiler_params=PARAMS,
        cost_estimate=cost(names, HALF),
        name="own_rows",
    )(core, left, *pieces, before)


def other_kernel(names, start, left, *refs):
    pieces = refs[: len(names)]
    before, _, out = refs[len(names) :]

    def step(i, carry):
        total = product(names, True, left, pieces, chunk(i, start=start)) + before[:, chunk(i, start=start)]
        out[:, chunk(i)] = total.astype(jnp.bfloat16)
        return carry

    lax.fori_loop(0, 2, step, 0)


def other_rows(names, start, left, pieces, before, tie):
    return pl.pallas_call(
        functools.partial(other_kernel, names, start),
        out_shape=jax.ShapeDtypeStruct((ROWS, HALF // 2), jnp.bfloat16),
        in_specs=[VM] * (len(names) + 3),
        out_specs=VM,
        compiler_params=PARAMS,
        cost_estimate=cost(names, HALF // 2),
        name="other_rows",
    )(left, *pieces, before, tie)


def finish_kernel(core, r0, r1, _, out, wide, sem):
    def copy(i):
        return pltpu.make_async_copy(
            wide.at[:, pl.ds(i * ROWS, ROWS)],
            out.at[:, pl.ds(pl.multiple_of((i * 2 + 1 - core[0]) * ROWS, LANES), ROWS)],
            sem.at[i],
        )

    for i in range(8):
        src = (r0, r1)[i // 4]
        wide[:, i * ROWS : (i + 1) * ROWS] = src[:, (i % 4) * ROWS : (i % 4 + 1) * ROWS].astype(jnp.float32)
        copy(i).start()
    for i in range(8):
        copy(i).wait()


def finish(core, rows, out):
    return pl.pallas_call(
        finish_kernel,
        out_shape=jax.ShapeDtypeStruct((ROWS, NG), jnp.float32),
        in_specs=[SM, VM, VM, HBM],
        out_specs=HBM,
        scratch_shapes=[pltpu.VMEM((ROWS, HALF), jnp.float32), pltpu.SemaphoreType.DMA((8,))],
        input_output_aliases={3: 0},
        compiler_params=PARAMS,
        name="finish",
    )(core, *rows, out)


def in_vmem(a):
    return pltpu.with_memory_space_constraint(a, pltpu.VMEM)


def on_device(psi_val, psi_con, e_val, e_con, occ, omega, g_index):
    ga = lax.axis_index("ga")
    ba = lax.axis_index("ba")
    core = lax.rem(ga, 2).astype(jnp.int32)
    con = psi_con.reshape(16, 4, 8, NB)
    val = jnp.broadcast_to(psi_val.reshape(1, 4, 8, NB), (16, 4, 8, NB))
    psi = lax.all_to_all(jnp.concatenate([val, con], 1), "ga", 0, 0, tiled=True)

    delta = (lax.dynamic_slice(e_con, (ga * 4,), (4,))[None, :] - e_val[:, None]).reshape(PAIRS)
    taken = jnp.broadcast_to(occ.astype(jnp.float32)[:, None], (4, 4)).reshape(PAIRS)
    d1 = lax.reduce_precision(delta, 8, 7)
    d2 = lax.reduce_precision(delta - d1, 8, 7)
    d3 = delta - d1 - d2
    meta = jnp.stack([d1, d2, d3, taken], 1).astype(jnp.bfloat16)
    meta = jnp.pad(meta, ((0, 0), (0, LANES - 4)))

    halves = g_index.reshape(8, 2, ROWS).transpose(1, 0, 2).reshape(2, HALF)
    kept = lax.dynamic_slice(halves, (core, 0), (1, HALF))
    given = lax.dynamic_slice(halves, (1 - core, 0), (1, HALF))
    spec, give = rho_spectrum(psi, given, meta)
    got = send(give, core_pairs())
    keep = rho_pick(spec, kept, meta)

    a = join(level(join([keep, got]), NEAR))
    halved = [[in_vmem(b) for b in level(m, STEP)] for m in deal(level(a, EVEN))]

    place = lax.div(ga, 2).astype(jnp.int32).reshape(1)
    mine_omega = lax.dynamic_slice(omega, (ba,), (1,))
    core = core.reshape(1)
    own = other = None
    tie = jnp.zeros(TIE.shape, TIE.dtype)
    groups = (((0, 0), (1, 0)), ((0, 1), (0, 2), (0, 3)), ((1, 1), (1, 2), (1, 3)))
    for names in groups:
        pieces = [halved[h][s] for h, s in names]
        left = weighted(place, mine_omega, pieces, tie)
        mirror = send(left, core_pairs())
        if names is not groups[-1]:
            own, tie = partial_rows(names, False, left, pieces, own, tie)
            other, tie = partial_rows(names, True, mirror, pieces, other, tie)
    out, tie = own_rows(names, core, left, pieces, own)
    rows = [send(other_rows(names, s, mirror, pieces, other, tie), core_pairs()) for s in (0, HALF // 2)]
    return finish(core, rows, out)[None]


def solution(mesh):
    placed = (P("ba", "ga"), P(None, "ga"), P("ba"), P(), P("ba"), P(), P())
    return jax.shard_map(
        on_device, mesh=mesh, in_specs=placed, out_specs=P("ba", "ga", None), check_vma=False
    )
```

```python
import functools
import itertools
import math

import jax
import jax.numpy as jnp
import numpy as np
from jax import lax
from jax.experimental import pallas as pl
from jax.experimental.pallas import tpu as pltpu
from jax.sharding import PartitionSpec as P

NV = 32
NC = 64
N = 32768
NA = 128
NB = 256
NG = 6144
HALF = NG // 2
ROWS = 384
LANES = 128
PAIRS = 16
WIDE = HALF + LANES
BLOCK = 2 * PAIRS
CHUNK = 768
MIB = 1024 * 1024
VM = pl.BlockSpec(memory_space=pltpu.VMEM)
SM = pl.BlockSpec(memory_space=pltpu.SMEM)
HBM = pl.BlockSpec(memory_space=pltpu.HBM)
PARAMS = pltpu.CompilerParams(vmem_limit_bytes=14 * MIB)

NEAR = ((0, 0, 0), (2, 2, 2), (1, 1, 1), (3, 3, 3))
EVEN = ((0, 0, 0), (2, 0, 0), (0, 2, 0), (0, 0, 2))
STEP = ((0, 0, 0), (1, 0, 0), (0, 1, 0), (0, 0, 1))


def split_bf16(a):
    hi = a.astype(np.float32).astype(jnp.bfloat16)
    lo = (a - hi.astype(np.float64)).astype(np.float32).astype(jnp.bfloat16)
    return hi, lo


def dft_constants():
    k1 = np.arange(NA)[:, None]
    ang = 2.0 * math.pi * ((k1 * np.arange(NA)[None, :]) % NA) / NA
    fh, fl = split_bf16(np.concatenate([np.cos(ang), np.sin(ang)], 0))
    first = np.concatenate([fh, fl], 1)
    tw = 2.0 * math.pi * ((k1 * np.arange(NB)[None, :]) % N) / N
    norm = math.sqrt(2.0 / N)
    tcos = (np.cos(tw) * norm).astype(np.float32)
    tsin = (np.sin(tw) * norm).astype(np.float32)
    b2 = 2.0 * math.pi * ((np.arange(NB)[:, None] * np.arange(NA)[None, :]) % NB) / NB
    sh, sl = split_bf16(np.concatenate([np.cos(b2), -np.sin(b2)], 0))
    second = np.concatenate([sh, sl, sh], 0)
    return first, tcos, tsin, second


def transform(psi, first, tcos, tsin, second, spec):
    bands = [psi[:, i].astype(jnp.float32).reshape(NA, NB) for i in range(8)]
    ca = tcos[...]
    sa = tsin[...]
    for p in range(PAIRS):
        d = (bands[p // 4] * bands[4 + p % 4]).astype(jnp.bfloat16)
        y = jnp.dot(first[...], jnp.concatenate([d, d], 0), preferred_element_type=jnp.float32)
        a, b = y[:NA], y[NA:]
        uv = jnp.concatenate([a * ca - b * sa, a * sa + b * ca], 1)
        hi = uv.astype(jnp.bfloat16)
        lo = (uv - hi.astype(jnp.float32)).astype(jnp.bfloat16)
        x = jnp.dot(
            jnp.concatenate([hi, hi, lo], 1), second[...], preferred_element_type=jnp.float32
        ).astype(jnp.bfloat16)
        spec[p * 64 : p * 64 + 64, 0:128] = x[:64]
        spec[p * 64 : p * 64 + 64, 128:256] = x[64:]


def pick(spec, gidx, meta, out):
    width = 256

    def step(i, carry):
        at = pl.ds(pl.multiple_of(i * width, width), width)
        g = gidx[:, at]
        k1 = lax.bitwise_and(g, 127)
        kk = lax.shift_right_logical(k1, 6) * 128 + lax.shift_right_logical(g, 7)
        hot = jnp.where(
            lax.broadcasted_iota(jnp.int32, (256, width), 0) == kk, 1.0, 0.0
        ).astype(jnp.bfloat16)
        o = jnp.dot(spec[...], hot, preferred_element_type=jnp.float32)
        m = lax.broadcasted_iota(jnp.int32, (64, width), 0) == lax.bitwise_and(k1, 63)
        picked = jnp.sum(jnp.where(m[None], o.reshape(PAIRS, 64, width), 0.0), axis=1)
        out[:, at] = picked.astype(jnp.bfloat16)
        return carry

    lax.fori_loop(0, HALF // width, step, 0)
    out[:, HALF:WIDE] = meta[...]


def transform_kernel(psi, gidx, meta, first, tcos, tsin, second, spec, out):
    transform(psi, first, tcos, tsin, second, spec)
    pick(spec, gidx, meta, out)


def rho_spectrum(psi, gidx, meta):
    return pl.pallas_call(
        transform_kernel,
        out_shape=[
            jax.ShapeDtypeStruct((PAIRS * 64, 256), jnp.bfloat16),
            jax.ShapeDtypeStruct((PAIRS, WIDE), jnp.bfloat16),
        ],
        in_specs=[VM] * 7,
        out_specs=[VM] * 2,
        compiler_params=PARAMS,
        name="rho_spectrum",
    )(psi, gidx, meta, *(jnp.asarray(c) for c in dft_constants()))


def rho_pick(spec, gidx, meta):
    return pl.pallas_call(
        pick,
        out_shape=jax.ShapeDtypeStruct((PAIRS, WIDE), jnp.bfloat16),
        in_specs=[VM] * 3,
        out_specs=VM,
        compiler_params=PARAMS,
        name="rho_pick",
    )(spec, gidx, meta)


def device_index(x, y, z, c):
    return (z * 4 + (y >> 1) * 2 + c) * 8 + (y & 1) * 4 + x


CHIPS = tuple(itertools.product(range(4), repeat=3))


@functools.cache
def offset_pairs(offset):
    return tuple(
        (device_index(*chip, c), device_index(*((a + (1 - 2 * c) * b) % 4 for a, b in zip(chip, offset)), c))
        for chip in CHIPS for c in range(2)
    )


@functools.cache
def core_pairs():
    return tuple((device_index(*chip, c), device_index(*chip, 1 - c)) for chip in CHIPS for c in range(2))


def send(a, pairs):
    return lax.ppermute(a, ("ga", "ba"), pairs)


def level(a, offsets):
    return [a] + [send(a, offset_pairs(offset)) for offset in offsets[1:]]


def join_kernel(n, *refs):
    out = refs[-1]
    row = 0
    for ref in refs[:n]:
        out[row : row + ref.shape[0], :] = ref[...]
        row += ref.shape[0]


def join(blocks, after=()):
    rows = sum(b.shape[0] for b in blocks)
    return pl.pallas_call(
        functools.partial(join_kernel, len(blocks)),
        out_shape=jax.ShapeDtypeStruct((rows, WIDE), jnp.bfloat16),
        in_specs=[VM] * (len(blocks) + len(after)),
        out_specs=VM,
        compiler_params=PARAMS,
        name="join",
    )(*blocks, *after)


def place_of(half, step):
    return [
        tuple(sum(v) % 4 for v in zip(NEAR[2 * half + i], EVEN[j], STEP[step]))
        for j in range(4) for i in range(2)
    ]


def mirrored(half, step):
    places = place_of(half, step)
    return [places.index(tuple(-v % 4 for v in p)) for p in places]


def weighted_kernel(place, omega, *refs):
    pieces, left = refs[:-2], refs[-1]
    w2 = omega[0] * omega[0]
    row = lax.broadcasted_iota(jnp.int32, (LANES, 2 * LANES), 0)
    lane = lax.broadcasted_iota(jnp.int32, (LANES, 2 * LANES), 1)
    spread = jnp.where((row < 3) & (lane < LANES) | (row == 3) & (lane >= LANES), 1.0, 0.0)
    spread = spread.astype(jnp.bfloat16)
    for i, piece in enumerate(pieces):
        m = jnp.dot(piece[:, HALF:WIDE], spread, preferred_element_type=jnp.float32)
        delta, taken = m[:, :LANES], m[:, LANES:]
        weight = (-4.0 / math.sqrt(NV * NC)) * taken * delta / (delta * delta + w2)
        for e in range(3):
            cols = pl.ds(pl.multiple_of(place[0] * ROWS + e * LANES, LANES), LANES)
            left[i * 256 : i * 256 + 256, e * LANES : (e + 1) * LANES] = (
                piece[:, cols].astype(jnp.float32) * weight
            ).astype(jnp.bfloat16)


def weighted(place, omega, pieces, tie):
    return pl.pallas_call(
        weighted_kernel,
        out_shape=jax.ShapeDtypeStruct((256 * len(pieces), ROWS), jnp.bfloat16),
        in_specs=[SM, SM] + [VM] * (len(pieces) + 1),
        out_specs=VM,
        compiler_params=PARAMS,
        name="weighted",
    )(place, omega, *pieces, tie)


def product(names, other, left, pieces, cols):
    total = None
    for i, (half, step) in enumerate(names):
        if other:
            rows = []
            for j in mirrored(half, step):
                at = i * 256 + j * BLOCK
                rows += [left[at + PAIRS : at + BLOCK, :], left[at : at + PAIRS, :]]
            mine = jnp.concatenate(rows, 0)
        else:
            mine = left[i * 256 : i * 256 + 256, :]
        term = lax.dot_general(
            mine, pieces[i][:, cols], (((0,), (0,)), ((), ())), preferred_element_type=jnp.float32
        )
        total = term if total is None else total + term
    return total


def chunk(i, width=CHUNK, start=0):
    return pl.ds(pl.multiple_of(start + i * width, LANES), width)


def cost(names, columns):
    return pl.CostEstimate(
        flops=2 * ROWS * columns * 256 * len(names),
        bytes_accessed=(2 * 256 * len(names) + 8 * ROWS) * columns,
        transcendentals=0,
    )


def partial_kernel(names, other, left, *refs):
    pieces, before = refs[: len(names)], refs[len(names) : -3]
    out, after = refs[-2:]
    after[...] = jnp.zeros_like(after)

    def step(i, carry):
        total = product(names, other, left, pieces, chunk(i))
        out[:, chunk(i)] = total + before[0][:, chunk(i)] if before else total
        return carry

    lax.fori_loop(0, HALF // CHUNK, step, 0)


TIE = jax.ShapeDtypeStruct((8, LANES), jnp.float32)


def partial_rows(names, other, left, pieces, before, tie):
    before = [] if before is None else [before]
    return pl.pallas_call(
        functools.partial(partial_kernel, names, other),
        out_shape=[jax.ShapeDtypeStruct((ROWS, HALF), jnp.float32), TIE],
        in_specs=[VM] * (2 + len(names) + len(before)),
        out_specs=[VM] * 2,
        input_output_aliases={1 + len(names): 0} if before else {},
        compiler_params=PARAMS,
        cost_estimate=cost(names, HALF),
        name="partial_other" if other else "partial_own",
    )(left, *pieces, *before, tie)


def own_kernel(names, start, n_swapped, core, left, *refs):
    pieces = refs[: len(names)]
    before = refs[len(names)]
    swapped = refs[len(names) + 1 : len(names) + 1 + n_swapped]
    out, wide, sem, wide_swapped, sem_swapped = refs[-5:]

    def copy(src, block, half, s):
        return pltpu.make_async_copy(
            src, out.at[:, pl.ds(pl.multiple_of((block * 2 + half) * ROWS, LANES), ROWS)], s
        )

    copies = []
    for i in range(4 * n_swapped):
        at = slice(i * ROWS, (i + 1) * ROWS)
        src = slice((i % 4) * ROWS, (i % 4 + 1) * ROWS)
        wide_swapped[:, at] = swapped[i // 4][:, src].astype(jnp.float32)
        copies.append(copy(wide_swapped.at[:, pl.ds(i * ROWS, ROWS)], i, 1 - core[0], sem_swapped.at[i]))
        copies[-1].start()
    for i in range(2):
        cols = slice(start + i * CHUNK, start + (i + 1) * CHUNK)
        wide[:, i * CHUNK : (i + 1) * CHUNK] = product(names, False, left, pieces, cols) + before[:, cols]
        for j in (2 * i, 2 * i + 1):
            block = start // ROWS + j
            copies.append(copy(wide.at[:, pl.ds(j * ROWS, ROWS)], block, core[0], sem.at[j]))
            copies[-1].start()
    for c in copies:
        c.wait()


def own_rows(names, start, core, left, pieces, before, swapped, after):
    grows = after.shape == (ROWS, NG)
    n = len(swapped)
    return pl.pallas_call(
        functools.partial(own_kernel, names, start, n),
        out_shape=jax.ShapeDtypeStruct((ROWS, NG), jnp.float32),
        in_specs=[SM, VM] + [VM] * (len(names) + 1 + n) + [HBM if grows else VM],
        out_specs=HBM,
        scratch_shapes=[
            pltpu.VMEM((ROWS, HALF // 2), jnp.float32),
            pltpu.SemaphoreType.DMA((4,)),
            pltpu.VMEM((ROWS, HALF) if n else (8, LANES), jnp.float32),
            pltpu.SemaphoreType.DMA((8,)),
        ],
        input_output_aliases={3 + len(names) + n: 0} if grows else {},
        compiler_params=PARAMS,
        cost_estimate=cost(names, HALF // 2),
        name="own_rows",
    )(core, left, *pieces, before, *swapped, after)


def other_kernel(names, start, left, *refs):
    pieces = refs[: len(names)]
    before, _, out, after = refs[len(names) :]
    after[...] = jnp.zeros_like(after)

    def step(i, carry):
        total = product(names, True, left, pieces, chunk(i, start=start)) + before[:, chunk(i, start=start)]
        out[:, chunk(i)] = total.astype(jnp.bfloat16)
        return carry

    lax.fori_loop(0, 2, step, 0)


def other_rows(names, start, left, pieces, before, tie):
    return pl.pallas_call(
        functools.partial(other_kernel, names, start),
        out_shape=[jax.ShapeDtypeStruct((ROWS, HALF // 2), jnp.bfloat16), TIE],
        in_specs=[VM] * (len(names) + 3),
        out_specs=[VM] * 2,
        compiler_params=PARAMS,
        cost_estimate=cost(names, HALF // 2),
        name="other_rows",
    )(left, *pieces, before, tie)


def in_vmem(a):
    return pltpu.with_memory_space_constraint(a, pltpu.VMEM)


def on_device(psi_val, psi_con, e_val, e_con, occ, omega, g_index):
    ga = lax.axis_index("ga")
    ba = lax.axis_index("ba")
    core = lax.rem(ga, 2).astype(jnp.int32)
    con = psi_con.reshape(16, 4, 8, NB)
    val = jnp.broadcast_to(psi_val.reshape(1, 4, 8, NB), (16, 4, 8, NB))
    psi = lax.all_to_all(jnp.concatenate([val, con], 1), "ga", 0, 0, tiled=True)

    delta = (lax.dynamic_slice(e_con, (ga * 4,), (4,))[None, :] - e_val[:, None]).reshape(PAIRS)
    taken = jnp.broadcast_to(occ.astype(jnp.float32)[:, None], (4, 4)).reshape(PAIRS)
    d1 = lax.reduce_precision(delta, 8, 7)
    d2 = lax.reduce_precision(delta - d1, 8, 7)
    d3 = delta - d1 - d2
    meta = jnp.stack([d1, d2, d3, taken], 1).astype(jnp.bfloat16)
    meta = jnp.pad(meta, ((0, 0), (0, LANES - 4)))

    halves = g_index.reshape(8, 2, ROWS).transpose(1, 0, 2).reshape(2, HALF)
    kept = lax.dynamic_slice(halves, (core, 0), (1, HALF))
    given = lax.dynamic_slice(halves, (1 - core, 0), (1, HALF))
    spec, give = rho_spectrum(psi, given, meta)
    got = send(give, core_pairs())
    keep = rho_pick(spec, kept, meta)

    mine = join([keep, got])
    near = {o: send(mine, offset_pairs(o)) for o in (NEAR[2], NEAR[3], NEAR[1])}
    halved = [None, None]
    for half, blocks in ((1, [near[NEAR[2]], near[NEAR[3]]]), (0, [mine, near[NEAR[1]]])):
        a = join(level(join(blocks), EVEN), [near[NEAR[1]]] if half else [])
        halved[half] = [in_vmem(b) for b in level(a, STEP)]

    place = lax.div(ga, 2).astype(jnp.int32).reshape(1)
    mine_omega = lax.dynamic_slice(omega, (ba,), (1,))
    core = core.reshape(1)
    own = other = None
    tie = jnp.zeros(TIE.shape, TIE.dtype)
    groups = (((1, 0), (0, 0)), ((1, 1), (1, 2), (1, 3)), ((0, 1), (0, 2), (0, 3)))
    for names in groups:
        pieces = [halved[h][s] for h, s in names]
        left = weighted(place, mine_omega, pieces, tie)
        mirror = send(left, core_pairs())
        if names is not groups[-1]:
            own, tie = partial_rows(names, False, left, pieces, own, tie)
            other, tie = partial_rows(names, True, mirror, pieces, other, tie)
    rows = []
    for start in (0, HALF // 2):
        row, tie = other_rows(names, start, mirror, pieces, other, tie)
        rows.append(send(row, core_pairs()))
    out = own_rows(names, 0, core, left, pieces, own, [], tie)
    return own_rows(names, HALF // 2, core, left, pieces, own, rows, out)[None]


def solution(mesh):
    placed = (P("ba", "ga"), P(None, "ga"), P("ba"), P(), P("ba"), P(), P())
    return jax.shard_map(
        on_device, mesh=mesh, in_specs=placed, out_specs=P("ba", "ga", None), check_vma=False
    )
```

```python
import functools
import itertools
import math

import jax
import jax.numpy as jnp
import numpy as np
from jax import lax
from jax.experimental import pallas as pl
from jax.experimental.pallas import tpu as pltpu
from jax.sharding import PartitionSpec as P

NV = 32
NC = 64
N = 32768
NA = 128
NB = 256
NG = 6144
HALF = NG // 2
ROWS = 384
LANES = 128
PAIRS = 16
WIDE = HALF + LANES
BLOCK = 2 * PAIRS
CHUNK = 768
MIB = 1024 * 1024
VM = pl.BlockSpec(memory_space=pltpu.VMEM)
SM = pl.BlockSpec(memory_space=pltpu.SMEM)
HBM = pl.BlockSpec(memory_space=pltpu.HBM)
PARAMS = pltpu.CompilerParams(vmem_limit_bytes=14 * MIB)

NEAR = ((0, 0, 0), (2, 2, 2), (1, 1, 1), (3, 3, 3))
EVEN = ((0, 0, 0), (2, 0, 0), (0, 2, 0), (0, 0, 2))
STEP = ((0, 0, 0), (1, 0, 0), (0, 1, 0), (0, 0, 1))


def split_bf16(a):
    hi = a.astype(np.float32).astype(jnp.bfloat16)
    lo = (a - hi.astype(np.float64)).astype(np.float32).astype(jnp.bfloat16)
    return hi, lo


def dft_constants():
    k1 = np.arange(NA)[:, None]
    chip, a = np.arange(8)[:, None], np.arange(8)[None, :]
    kinds = [((chip * 2 + kind) * 8 + a).reshape(64) for kind in range(2)]
    first = []
    for core in range(2):
        order = np.concatenate([kinds[core], kinds[1 - core]])
        ang = 2.0 * math.pi * ((k1 * order[None, :]) % NA) / NA
        fh, fl = split_bf16(np.concatenate([np.cos(ang), np.sin(ang)], 0))
        first.append(np.concatenate([fh, fl], 1))
    tw = 2.0 * math.pi * ((k1 * np.arange(NB)[None, :]) % N) / N
    norm = math.sqrt(2.0 / N)
    tcos = (np.cos(tw) * norm).astype(np.float32)
    tsin = (np.sin(tw) * norm).astype(np.float32)
    b2 = 2.0 * math.pi * ((np.arange(NB)[:, None] * np.arange(NA)[None, :]) % NB) / NB
    sh, sl = split_bf16(np.concatenate([np.cos(b2), -np.sin(b2)], 0))
    return np.stack(first), tcos, tsin, np.concatenate([sh, sl], 1)


def transform(core, mine, others, first, tcos, tsin, second, spec, high, low):
    def band(row):
        both = jnp.concatenate([mine[:, row], others[:, row]], 0)
        return both.astype(jnp.float32).reshape(NA, NB)

    con = [band(core[0] * 4 + i) for i in range(4)]
    ca = tcos[...]
    sa = tsin[...]
    f = first[core[0]]
    for v in range(4):
        val = band(8 + v)
        for c in range(4):
            d = (val * con[c]).astype(jnp.bfloat16)
            y = jnp.dot(f, jnp.concatenate([d, d], 0), preferred_element_type=jnp.float32)
            a, b = y[:NA], y[NA:]
            uv = jnp.concatenate([a * ca - b * sa, a * sa + b * ca], 1)
            hi = uv.astype(jnp.bfloat16)
            at = slice((v * 4 + c) * NA, (v * 4 + c + 1) * NA)
            high[at, :] = hi
            low[at, :] = (uv - hi.astype(jnp.float32)).astype(jnp.bfloat16)
    for n in range(4):
        at = slice(n * 512, n * 512 + 512)
        y = jnp.dot(high[at, :], second[...], preferred_element_type=jnp.float32)
        z = jnp.dot(low[at, :], second[:, :NA], preferred_element_type=jnp.float32)
        x = (y[:, :NA] + (y[:, NA:] + z)).astype(jnp.bfloat16)
        for i in range(4):
            p = n * 4 + i
            spec[p * 64 : p * 64 + 64, 0:128] = x[i * NA : i * NA + 64]
            spec[p * 64 : p * 64 + 64, 128:256] = x[i * NA + 64 : i * NA + NA]


def pick(spec, gidx, meta, out):
    width = 1024

    def step(i, carry):
        at = pl.ds(pl.multiple_of(i * width, width), width)
        g = gidx[:, at]
        k1 = lax.bitwise_and(g, 127)
        kk = lax.shift_right_logical(k1, 6) * 128 + lax.shift_right_logical(g, 7)
        hot = jnp.where(
            lax.broadcasted_iota(jnp.int32, (256, width), 0) == kk, 1.0, 0.0
        ).astype(jnp.bfloat16)
        o = jnp.dot(spec[...], hot, preferred_element_type=jnp.float32)
        m = lax.broadcasted_iota(jnp.int32, (64, width), 0) == lax.bitwise_and(k1, 63)
        picked = jnp.sum(jnp.where(m[None], o.reshape(PAIRS, 64, width), 0.0), axis=1)
        out[:, at] = picked.astype(jnp.bfloat16)
        return carry

    lax.fori_loop(0, HALF // width, step, 0)
    out[:, HALF:WIDE] = meta[...]


def transform_kernel(core, mine, others, gidx, meta, first, tcos, tsin, second, spec, out, high, low):
    transform(core, mine, others, first, tcos, tsin, second, spec, high, low)
    pick(spec, gidx, meta, out)


def rho_spectrum(core, mine, others, gidx, meta):
    return pl.pallas_call(
        transform_kernel,
        out_shape=[
            jax.ShapeDtypeStruct((PAIRS * 64, 256), jnp.bfloat16),
            jax.ShapeDtypeStruct((PAIRS, WIDE), jnp.bfloat16),
        ],
        in_specs=[SM] + [VM] * 8,
        out_specs=[VM] * 2,
        scratch_shapes=[pltpu.VMEM((PAIRS * NA, 2 * NB), jnp.bfloat16)] * 2,
        compiler_params=PARAMS,
        name="rho_spectrum",
    )(core, mine, others, gidx, meta, *(jnp.asarray(c) for c in dft_constants()))


def rho_pick(spec, gidx, meta):
    return pl.pallas_call(
        pick,
        out_shape=jax.ShapeDtypeStruct((PAIRS, WIDE), jnp.bfloat16),
        in_specs=[VM] * 3,
        out_specs=VM,
        compiler_params=PARAMS,
        name="rho_pick",
    )(spec, gidx, meta)


def device_index(x, y, z, c):
    return (z * 4 + (y >> 1) * 2 + c) * 8 + (y & 1) * 4 + x


CHIPS = tuple(itertools.product(range(4), repeat=3))


@functools.cache
def offset_pairs(offset):
    return tuple(
        (device_index(*chip, c), device_index(*((a + (1 - 2 * c) * b) % 4 for a, b in zip(chip, offset)), c))
        for chip in CHIPS for c in range(2)
    )


@functools.cache
def core_pairs():
    return tuple((device_index(*chip, c), device_index(*chip, 1 - c)) for chip in CHIPS for c in range(2))


def send(a, pairs):
    return lax.ppermute(a, ("ga", "ba"), pairs)


def level(a, offsets):
    return [a] + [send(a, offset_pairs(offset)) for offset in offsets[1:]]


def join_kernel(n, *refs):
    out = refs[n]
    row = 0
    for ref in refs[:n]:
        out[row : row + ref.shape[0], :] = ref[...]
        row += ref.shape[0]


def join(blocks):
    rows = sum(b.shape[0] for b in blocks)
    return pl.pallas_call(
        functools.partial(join_kernel, len(blocks)),
        out_shape=jax.ShapeDtypeStruct((rows, WIDE), jnp.bfloat16),
        in_specs=[VM] * len(blocks),
        out_specs=VM,
        compiler_params=PARAMS,
        name="join",
    )(*blocks)


def deal_kernel(b0, b1, b2, b3, out0, out1):
    for i, ref in enumerate((b0, b1, b2, b3)):
        out0[i * 64 : i * 64 + 64, :] = ref[0:64, :]
        out1[i * 64 : i * 64 + 64, :] = ref[64:128, :]


def deal(blocks):
    return pl.pallas_call(
        deal_kernel,
        out_shape=[jax.ShapeDtypeStruct((256, WIDE), jnp.bfloat16)] * 2,
        in_specs=[VM] * 4,
        out_specs=[VM] * 2,
        compiler_params=PARAMS,
        name="deal",
    )(*blocks)


def place_of(half, step):
    return [
        tuple(sum(v) % 4 for v in zip(NEAR[2 * half + i], EVEN[j], STEP[step]))
        for j in range(4) for i in range(2)
    ]


def mirrored(half, step):
    places = place_of(half, step)
    return [places.index(tuple(-v % 4 for v in p)) for p in places]


def weighted_kernel(place, omega, *refs):
    pieces, left = refs[:-2], refs[-1]
    w2 = omega[0] * omega[0]
    row = lax.broadcasted_iota(jnp.int32, (LANES, 2 * LANES), 0)
    lane = lax.broadcasted_iota(jnp.int32, (LANES, 2 * LANES), 1)
    spread = jnp.where((row < 3) & (lane < LANES) | (row == 3) & (lane >= LANES), 1.0, 0.0)
    spread = spread.astype(jnp.bfloat16)
    for i, piece in enumerate(pieces):
        m = jnp.dot(piece[:, HALF:WIDE], spread, preferred_element_type=jnp.float32)
        delta, taken = m[:, :LANES], m[:, LANES:]
        weight = (-4.0 / math.sqrt(NV * NC)) * taken * delta / (delta * delta + w2)
        for e in range(3):
            cols = pl.ds(pl.multiple_of(place[0] * ROWS + e * LANES, LANES), LANES)
            left[i * 256 : i * 256 + 256, e * LANES : (e + 1) * LANES] = (
                piece[:, cols].astype(jnp.float32) * weight
            ).astype(jnp.bfloat16)


def weighted(place, omega, pieces, tie):
    return pl.pallas_call(
        weighted_kernel,
        out_shape=jax.ShapeDtypeStruct((256 * len(pieces), ROWS), jnp.bfloat16),
        in_specs=[SM, SM] + [VM] * (len(pieces) + 1),
        out_specs=VM,
        compiler_params=PARAMS,
        name="weighted",
    )(place, omega, *pieces, tie)


def product(names, other, left, pieces, cols):
    total = None
    for i, (half, step) in enumerate(names):
        if other:
            rows = []
            for j in mirrored(half, step):
                at = i * 256 + j * BLOCK
                rows += [left[at + PAIRS : at + BLOCK, :], left[at : at + PAIRS, :]]
            mine = jnp.concatenate(rows, 0)
        else:
            mine = left[i * 256 : i * 256 + 256, :]
        term = lax.dot_general(
            mine, pieces[i][:, cols], (((0,), (0,)), ((), ())), preferred_element_type=jnp.float32
        )
        total = term if total is None else total + term
    return total


def chunk(i, width=CHUNK, start=0):
    return pl.ds(pl.multiple_of(start + i * width, LANES), width)


def cost(names, columns):
    return pl.CostEstimate(
        flops=2 * ROWS * columns * 256 * len(names),
        bytes_accessed=(2 * 256 * len(names) + 8 * ROWS) * columns,
        transcendentals=0,
    )


def partial_kernel(names, other, left, *refs):
    pieces, before = refs[: len(names)], refs[len(names) : -3]
    out, after = refs[-2:]
    after[...] = jnp.zeros_like(after)

    def step(i, carry):
        total = product(names, other, left, pieces, chunk(i))
        out[:, chunk(i)] = total + before[0][:, chunk(i)] if before else total
        return carry

    lax.fori_loop(0, HALF // CHUNK, step, 0)


TIE = jax.ShapeDtypeStruct((8, LANES), jnp.float32)


def partial_rows(names, other, left, pieces, before, tie):
    before = [] if before is None else [before]
    return pl.pallas_call(
        functools.partial(partial_kernel, names, other),
        out_shape=[jax.ShapeDtypeStruct((ROWS, HALF), jnp.float32), TIE],
        in_specs=[VM] * (2 + len(names) + len(before)),
        out_specs=[VM] * 2,
        input_output_aliases={1 + len(names): 0} if before else {},
        compiler_params=PARAMS,
        cost_estimate=cost(names, HALF),
        name="partial_other" if other else "partial_own",
    )(left, *pieces, *before, tie)


def own_kernel(names, start, core, left, *refs):
    pieces = refs[: len(names)]
    before, _, out, tie, wide, sem = refs[len(names) :]
    tie[...] = jnp.zeros_like(tie)
    copies = []
    for i in range(2):
        cols = slice(start + i * CHUNK, start + (i + 1) * CHUNK)
        wide[:, i * CHUNK : (i + 1) * CHUNK] = product(names, False, left, pieces, cols) + before[:, cols]
        for j in (2 * i, 2 * i + 1):
            block = (start // ROWS + j) * 2 + core[0]
            copies.append(
                pltpu.make_async_copy(
                    wide.at[:, pl.ds(j * ROWS, ROWS)],
                    out.at[:, pl.ds(pl.multiple_of(block * ROWS, LANES), ROWS)],
                    sem.at[j],
                )
            )
            copies[-1].start()
    for copy in copies:
        copy.wait()


def own_rows(names, start, core, left, pieces, before, after):
    grows = after.shape == (ROWS, NG)
    return pl.pallas_call(
        functools.partial(own_kernel, names, start),
        out_shape=[jax.ShapeDtypeStruct((ROWS, NG), jnp.float32), TIE],
        in_specs=[SM, VM] + [VM] * (len(names) + 1) + [HBM if grows else VM],
        out_specs=[HBM, VM],
        scratch_shapes=[pltpu.VMEM((ROWS, HALF // 2), jnp.float32), pltpu.SemaphoreType.DMA((4,))],
        input_output_aliases={3 + len(names): 0} if grows else {},
        compiler_params=PARAMS,
        cost_estimate=cost(names, HALF // 2),
        name="own_rows",
    )(core, left, *pieces, before, after)


def other_kernel(names, start, left, *refs):
    pieces = refs[: len(names)]
    before, _, out = refs[len(names) :]

    def step(i, carry):
        total = product(names, True, left, pieces, chunk(i, start=start)) + before[:, chunk(i, start=start)]
        out[:, chunk(i)] = total.astype(jnp.bfloat16)
        return carry

    lax.fori_loop(0, 2, step, 0)


def other_rows(names, start, left, pieces, before, tie):
    return pl.pallas_call(
        functools.partial(other_kernel, names, start),
        out_shape=jax.ShapeDtypeStruct((ROWS, HALF // 2), jnp.bfloat16),
        in_specs=[VM] * (len(names) + 3),
        out_specs=VM,
        compiler_params=PARAMS,
        cost_estimate=cost(names, HALF // 2),
        name="other_rows",
    )(left, *pieces, before, tie)


def finish_kernel(core, r0, r1, _, out, wide, sem):
    def copy(i):
        return pltpu.make_async_copy(
            wide.at[:, pl.ds(i * ROWS, ROWS)],
            out.at[:, pl.ds(pl.multiple_of((i * 2 + 1 - core[0]) * ROWS, LANES), ROWS)],
            sem.at[i],
        )

    for i in range(8):
        src = (r0, r1)[i // 4]
        wide[:, i * ROWS : (i + 1) * ROWS] = src[:, (i % 4) * ROWS : (i % 4 + 1) * ROWS].astype(jnp.float32)
        copy(i).start()
    for i in range(8):
        copy(i).wait()


def finish(core, rows, out):
    return pl.pallas_call(
        finish_kernel,
        out_shape=jax.ShapeDtypeStruct((ROWS, NG), jnp.float32),
        in_specs=[SM, VM, VM, HBM],
        out_specs=HBM,
        scratch_shapes=[pltpu.VMEM((ROWS, HALF), jnp.float32), pltpu.SemaphoreType.DMA((8,))],
        input_output_aliases={3: 0},
        compiler_params=PARAMS,
        name="finish",
    )(core, *rows, out)


def in_vmem(a):
    return pltpu.with_memory_space_constraint(a, pltpu.VMEM)


def on_device(psi_val, psi_con, e_val, e_con, occ, omega, g_index):
    ga = lax.axis_index("ga")
    ba = lax.axis_index("ba")
    core = lax.rem(ga, 2).astype(jnp.int32)
    con = psi_con.reshape(8, 8, 8, NB)
    val = jnp.broadcast_to(psi_val.reshape(1, 4, 8, NB), (8, 4, 8, NB))
    kinds = [[2 * i + c for i in range(8)] for c in range(2)]
    psi = lax.all_to_all(
        jnp.concatenate([con, val], 1), "ga", 0, 0, tiled=True, axis_index_groups=kinds
    )
    psi_other = send(psi, core_pairs())

    delta = (lax.dynamic_slice(e_con, (ga * 4,), (4,))[None, :] - e_val[:, None]).reshape(PAIRS)
    taken = jnp.broadcast_to(occ.astype(jnp.float32)[:, None], (4, 4)).reshape(PAIRS)
    d1 = lax.reduce_precision(delta, 8, 7)
    d2 = lax.reduce_precision(delta - d1, 8, 7)
    d3 = delta - d1 - d2
    meta = jnp.stack([d1, d2, d3, taken], 1).astype(jnp.bfloat16)
    meta = jnp.pad(meta, ((0, 0), (0, LANES - 4)))

    halves = g_index.reshape(8, 2, ROWS).transpose(1, 0, 2).reshape(2, HALF)
    kept = lax.dynamic_slice(halves, (core, 0), (1, HALF))
    given = lax.dynamic_slice(halves, (1 - core, 0), (1, HALF))
    spec, give = rho_spectrum(core.reshape(1), psi, psi_other, given, meta)
    got = send(give, core_pairs())
    keep = rho_pick(spec, kept, meta)

    a = join(level(join([keep, got]), NEAR))
    halved = [[in_vmem(b) for b in level(m, STEP)] for m in deal(level(a, EVEN))]

    place = lax.div(ga, 2).astype(jnp.int32).reshape(1)
    mine_omega = lax.dynamic_slice(omega, (ba,), (1,))
    core = core.reshape(1)
    own = other = None
    tie = jnp.zeros(TIE.shape, TIE.dtype)
    groups = (((0, 0), (1, 0)), ((0, 1), (0, 2), (0, 3)), ((1, 1), (1, 2), (1, 3)))
    for names in groups:
        pieces = [halved[h][s] for h, s in names]
        left = weighted(place, mine_omega, pieces, tie)
        mirror = send(left, core_pairs())
        if names is not groups[-1]:
            own, tie = partial_rows(names, False, left, pieces, own, tie)
            other, tie = partial_rows(names, True, mirror, pieces, other, tie)
    out, tie = own_rows(names, 0, core, left, pieces, own, tie)
    rows = [send(other_rows(names, s, mirror, pieces, other, tie), core_pairs()) for s in (0, HALF // 2)]
    out, _ = own_rows(names, HALF // 2, core, left, pieces, own, out)
    return finish(core, rows, out)[None]


def solution(mesh):
    placed = (P("ba", "ga"), P(None, "ga"), P("ba"), P(), P("ba"), P(), P())
    return jax.shard_map(
        on_device, mesh=mesh, in_specs=placed, out_specs=P("ba", "ga", None), check_vma=False
    )
```

```python
import functools
import itertools
import math

import jax
import jax.numpy as jnp
import numpy as np
from jax import lax
from jax.experimental import pallas as pl
from jax.experimental.pallas import tpu as pltpu
from jax.sharding import PartitionSpec as P

NV = 32
NC = 64
N = 32768
NA = 128
NB = 256
NG = 6144
HALF = NG // 2
ROWS = 384
LANES = 128
PAIRS = 16
WIDE = HALF + LANES
BLOCK = 2 * PAIRS
CHUNK = 768
MIB = 1024 * 1024
VM = pl.BlockSpec(memory_space=pltpu.VMEM)
SM = pl.BlockSpec(memory_space=pltpu.SMEM)
HBM = pl.BlockSpec(memory_space=pltpu.HBM)
PARAMS = pltpu.CompilerParams(vmem_limit_bytes=14 * MIB)

NEAR = ((0, 0, 0), (2, 2, 2), (1, 1, 1), (3, 3, 3))
EVEN = ((0, 0, 0), (2, 0, 0), (0, 2, 0), (0, 0, 2))
STEP = ((0, 0, 0), (1, 0, 0), (0, 1, 0), (0, 0, 1))


def split_bf16(a):
    hi = a.astype(np.float32).astype(jnp.bfloat16)
    lo = (a - hi.astype(np.float64)).astype(np.float32).astype(jnp.bfloat16)
    return hi, lo


def dft_constants():
    k1 = np.arange(NA)[:, None]
    a, kind, chip = np.arange(8)[:, None, None], np.arange(2)[:, None], np.arange(8)
    first = []
    for core in range(2):
        order = ((chip * 2 + (kind + core) % 2) * 8 + a).reshape(NA)
        ang = 2.0 * math.pi * ((k1 * order[None, :]) % NA) / NA
        fh, fl = split_bf16(np.concatenate([np.cos(ang), np.sin(ang)], 0))
        first.append(np.concatenate([fh, fl], 1))
    tw = 2.0 * math.pi * ((k1 * np.arange(NB)[None, :]) % N) / N
    norm = math.sqrt(2.0 / N)
    tcos = (np.cos(tw) * norm).astype(np.float32)
    tsin = (np.sin(tw) * norm).astype(np.float32)
    b2 = 2.0 * math.pi * ((np.arange(NB)[:, None] * np.arange(NA)[None, :]) % NB) / NB
    sh, sl = split_bf16(np.concatenate([np.cos(b2), -np.sin(b2)], 0))
    return np.stack(first), tcos, tsin, np.concatenate([sh, sl], 1)


def payload_kernel(val, con, out):
    v = val[...].astype(jnp.float32)
    values = jnp.concatenate([v[:, :1024], v[:, 1024:]], 0)
    for chip in range(8):
        c = con[chip * 8 : chip * 8 + 8, :].astype(jnp.float32)
        rows = jnp.concatenate([c[:, :1024], c[:, 1024:], values], 0)
        out[chip] = rows.astype(jnp.bfloat16)


def payload(val, con):
    return pl.pallas_call(
        payload_kernel,
        out_shape=jax.ShapeDtypeStruct((8, 24, 1024), jnp.bfloat16),
        in_specs=[VM] * 2,
        out_specs=VM,
        compiler_params=PARAMS,
        name="payload",
    )(val, con)


def transform(core, mine, others, first, tcos, tsin, second, spec, high, low, grid):
    for kind, ref in enumerate((mine, others)):
        for chip in range(8):
            for j in range(8):
                grid[kind, j, chip * 24 : chip * 24 + 24, :] = ref[
                    chip, :, j * LANES : (j + 1) * LANES
                ].astype(jnp.float32)

    def band(row, apart):
        parts = []
        for half in range(2):
            at = pl.ds(row + half * apart, 8, stride=24)
            for a in range(4):
                for kind in range(2):
                    parts.append(jnp.concatenate([grid[kind, 2 * a + j, at, :] for j in range(2)], 1))
        return jnp.concatenate(parts, 0)

    con = [band(core[0] * 4 + i, 8) for i in range(4)]
    ca = tcos[...]
    sa = tsin[...]
    f = first[core[0]]
    for v in range(4):
        val = band(16 + v, 4)
        for c in range(4):
            d = (val * con[c]).astype(jnp.bfloat16)
            y = jnp.dot(f, jnp.concatenate([d, d], 0), preferred_element_type=jnp.float32)
            a, b = y[:NA], y[NA:]
            uv = jnp.concatenate([a * ca - b * sa, a * sa + b * ca], 1)
            hi = uv.astype(jnp.bfloat16)
            at = slice((v * 4 + c) * NA, (v * 4 + c + 1) * NA)
            high[at, :] = hi
            low[at, :] = (uv - hi.astype(jnp.float32)).astype(jnp.bfloat16)
    for n in range(4):
        at = slice(n * 512, n * 512 + 512)
        y = jnp.dot(high[at, :], second[...], preferred_element_type=jnp.float32)
        z = jnp.dot(low[at, :], second[:, :NA], preferred_element_type=jnp.float32)
        x = (y[:, :NA] + (y[:, NA:] + z)).astype(jnp.bfloat16)
        for i in range(4):
            p = n * 4 + i
            spec[p * 64 : p * 64 + 64, 0:128] = x[i * NA : i * NA + 64]
            spec[p * 64 : p * 64 + 64, 128:256] = x[i * NA + 64 : i * NA + NA]


def pick(spec, gidx, meta, out):
    width = 1024

    def step(i, carry):
        at = pl.ds(pl.multiple_of(i * width, width), width)
        g = gidx[:, at]
        k1 = lax.bitwise_and(g, 127)
        kk = lax.shift_right_logical(k1, 6) * 128 + lax.shift_right_logical(g, 7)
        hot = jnp.where(
            lax.broadcasted_iota(jnp.int32, (256, width), 0) == kk, 1.0, 0.0
        ).astype(jnp.bfloat16)
        o = jnp.dot(spec[...], hot, preferred_element_type=jnp.float32)
        m = lax.broadcasted_iota(jnp.int32, (64, width), 0) == lax.bitwise_and(k1, 63)
        picked = jnp.sum(jnp.where(m[None], o.reshape(PAIRS, 64, width), 0.0), axis=1)
        out[:, at] = picked.astype(jnp.bfloat16)
        return carry

    lax.fori_loop(0, HALF // width, step, 0)
    out[:, HALF:WIDE] = meta[...]


def transform_kernel(core, mine, others, gidx, meta, first, tcos, tsin, second, spec, out, high, low, grid):
    transform(core, mine, others, first, tcos, tsin, second, spec, high, low, grid)
    pick(spec, gidx, meta, out)


def rho_spectrum(core, mine, others, gidx, meta):
    return pl.pallas_call(
        transform_kernel,
        out_shape=[
            jax.ShapeDtypeStruct((PAIRS * 64, 256), jnp.bfloat16),
            jax.ShapeDtypeStruct((PAIRS, WIDE), jnp.bfloat16),
        ],
        in_specs=[SM] + [VM] * 8,
        out_specs=[VM] * 2,
        scratch_shapes=[pltpu.VMEM((PAIRS * NA, 2 * NB), jnp.bfloat16)] * 2
        + [pltpu.VMEM((2, 8, 8 * 24, LANES), jnp.float32)],
        compiler_params=PARAMS,
        name="rho_spectrum",
    )(core, mine, others, gidx, meta, *(jnp.asarray(c) for c in dft_constants()))


def rho_pick(spec, gidx, meta):
    return pl.pallas_call(
        pick,
        out_shape=jax.ShapeDtypeStruct((PAIRS, WIDE), jnp.bfloat16),
        in_specs=[VM] * 3,
        out_specs=VM,
        compiler_params=PARAMS,
        name="rho_pick",
    )(spec, gidx, meta)


def device_index(x, y, z, c):
    return (z * 4 + (y >> 1) * 2 + c) * 8 + (y & 1) * 4 + x


CHIPS = tuple(itertools.product(range(4), repeat=3))


@functools.cache
def offset_pairs(offset):
    return tuple(
        (device_index(*chip, c), device_index(*((a + (1 - 2 * c) * b) % 4 for a, b in zip(chip, offset)), c))
        for chip in CHIPS for c in range(2)
    )


@functools.cache
def core_pairs():
    return tuple((device_index(*chip, c), device_index(*chip, 1 - c)) for chip in CHIPS for c in range(2))


def send(a, pairs):
    return lax.ppermute(a, ("ga", "ba"), pairs)


def level(a, offsets):
    return [a] + [send(a, offset_pairs(offset)) for offset in offsets[1:]]


def join_kernel(n, *refs):
    out = refs[n]
    row = 0
    for ref in refs[:n]:
        out[row : row + ref.shape[0], :] = ref[...]
        row += ref.shape[0]


def join(blocks):
    rows = sum(b.shape[0] for b in blocks)
    return pl.pallas_call(
        functools.partial(join_kernel, len(blocks)),
        out_shape=jax.ShapeDtypeStruct((rows, WIDE), jnp.bfloat16),
        in_specs=[VM] * len(blocks),
        out_specs=VM,
        compiler_params=PARAMS,
        name="join",
    )(*blocks)


def deal_kernel(b0, b1, b2, b3, out0, out1):
    for i, ref in enumerate((b0, b1, b2, b3)):
        out0[i * 64 : i * 64 + 64, :] = ref[0:64, :]
        out1[i * 64 : i * 64 + 64, :] = ref[64:128, :]


def deal(blocks):
    return pl.pallas_call(
        deal_kernel,
        out_shape=[jax.ShapeDtypeStruct((256, WIDE), jnp.bfloat16)] * 2,
        in_specs=[VM] * 4,
        out_specs=[VM] * 2,
        compiler_params=PARAMS,
        name="deal",
    )(*blocks)


def place_of(half, step):
    return [
        tuple(sum(v) % 4 for v in zip(NEAR[2 * half + i], EVEN[j], STEP[step]))
        for j in range(4) for i in range(2)
    ]


def mirrored(half, step):
    places = place_of(half, step)
    return [places.index(tuple(-v % 4 for v in p)) for p in places]


def weighted_kernel(place, omega, *refs):
    pieces, left = refs[:-2], refs[-1]
    w2 = omega[0] * omega[0]
    row = lax.broadcasted_iota(jnp.int32, (LANES, 2 * LANES), 0)
    lane = lax.broadcasted_iota(jnp.int32, (LANES, 2 * LANES), 1)
    spread = jnp.where((row < 3) & (lane < LANES) | (row == 3) & (lane >= LANES), 1.0, 0.0)
    spread = spread.astype(jnp.bfloat16)
    for i, piece in enumerate(pieces):
        m = jnp.dot(piece[:, HALF:WIDE], spread, preferred_element_type=jnp.float32)
        delta, taken = m[:, :LANES], m[:, LANES:]
        weight = (-4.0 / math.sqrt(NV * NC)) * taken * delta / (delta * delta + w2)
        for e in range(3):
            cols = pl.ds(pl.multiple_of(place[0] * ROWS + e * LANES, LANES), LANES)
            left[i * 256 : i * 256 + 256, e * LANES : (e + 1) * LANES] = (
                piece[:, cols].astype(jnp.float32) * weight
            ).astype(jnp.bfloat16)


def weighted(place, omega, pieces, tie):
    return pl.pallas_call(
        weighted_kernel,
        out_shape=jax.ShapeDtypeStruct((256 * len(pieces), ROWS), jnp.bfloat16),
        in_specs=[SM, SM] + [VM] * (len(pieces) + 1),
        out_specs=VM,
        compiler_params=PARAMS,
        name="weighted",
    )(place, omega, *pieces, tie)


def product(names, other, left, pieces, cols):
    total = None
    for i, (half, step) in enumerate(names):
        if other:
            rows = []
            for j in mirrored(half, step):
                at = i * 256 + j * BLOCK
                rows += [left[at + PAIRS : at + BLOCK, :], left[at : at + PAIRS, :]]
            mine = jnp.concatenate(rows, 0)
        else:
            mine = left[i * 256 : i * 256 + 256, :]
        term = lax.dot_general(
            mine, pieces[i][:, cols], (((0,), (0,)), ((), ())), preferred_element_type=jnp.float32
        )
        total = term if total is None else total + term
    return total


def chunk(i, width=CHUNK, start=0):
    return pl.ds(pl.multiple_of(start + i * width, LANES), width)


def cost(names, columns):
    return pl.CostEstimate(
        flops=2 * ROWS * columns * 256 * len(names),
        bytes_accessed=(2 * 256 * len(names) + 8 * ROWS) * columns,
        transcendentals=0,
    )


def partial_kernel(names, other, left, *refs):
    pieces, before = refs[: len(names)], refs[len(names) : -3]
    out, after = refs[-2:]
    after[...] = jnp.zeros_like(after)

    def step(i, carry):
        total = product(names, other, left, pieces, chunk(i))
        out[:, chunk(i)] = total + before[0][:, chunk(i)] if before else total
        return carry

    lax.fori_loop(0, HALF // CHUNK, step, 0)


TIE = jax.ShapeDtypeStruct((8, LANES), jnp.float32)


def partial_rows(names, other, left, pieces, before, tie):
    before = [] if before is None else [before]
    return pl.pallas_call(
        functools.partial(partial_kernel, names, other),
        out_shape=[jax.ShapeDtypeStruct((ROWS, HALF), jnp.float32), TIE],
        in_specs=[VM] * (2 + len(names) + len(before)),
        out_specs=[VM] * 2,
        input_output_aliases={1 + len(names): 0} if before else {},
        compiler_params=PARAMS,
        cost_estimate=cost(names, HALF),
        name="partial_other" if other else "partial_own",
    )(left, *pieces, *before, tie)


def own_kernel(names, start, core, left, *refs):
    pieces = refs[: len(names)]
    before, _, out, tie, wide, sem = refs[len(names) :]
    tie[...] = jnp.zeros_like(tie)
    copies = []
    for i in range(2):
        cols = slice(start + i * CHUNK, start + (i + 1) * CHUNK)
        wide[:, i * CHUNK : (i + 1) * CHUNK] = product(names, False, left, pieces, cols) + before[:, cols]
        for j in (2 * i, 2 * i + 1):
            block = (start // ROWS + j) * 2 + core[0]
            copies.append(
                pltpu.make_async_copy(
                    wide.at[:, pl.ds(j * ROWS, ROWS)],
                    out.at[:, pl.ds(pl.multiple_of(block * ROWS, LANES), ROWS)],
                    sem.at[j],
                )
            )
            copies[-1].start()
    for copy in copies:
        copy.wait()


def own_rows(names, start, core, left, pieces, before, after):
    grows = after.shape == (ROWS, NG)
    return pl.pallas_call(
        functools.partial(own_kernel, names, start),
        out_shape=[jax.ShapeDtypeStruct((ROWS, NG), jnp.float32), TIE],
        in_specs=[SM, VM] + [VM] * (len(names) + 1) + [HBM if grows else VM],
        out_specs=[HBM, VM],
        scratch_shapes=[pltpu.VMEM((ROWS, HALF // 2), jnp.float32), pltpu.SemaphoreType.DMA((4,))],
        input_output_aliases={3 + len(names): 0} if grows else {},
        compiler_params=PARAMS,
        cost_estimate=cost(names, HALF // 2),
        name="own_rows",
    )(core, left, *pieces, before, after)


def other_kernel(names, start, left, *refs):
    pieces = refs[: len(names)]
    before, _, out = refs[len(names) :]

    def step(i, carry):
        total = product(names, True, left, pieces, chunk(i, start=start)) + before[:, chunk(i, start=start)]
        out[:, chunk(i)] = total.astype(jnp.bfloat16)
        return carry

    lax.fori_loop(0, 2, step, 0)


def other_rows(names, start, left, pieces, before, tie):
    return pl.pallas_call(
        functools.partial(other_kernel, names, start),
        out_shape=jax.ShapeDtypeStruct((ROWS, HALF // 2), jnp.bfloat16),
        in_specs=[VM] * (len(names) + 3),
        out_specs=VM,
        compiler_params=PARAMS,
        cost_estimate=cost(names, HALF // 2),
        name="other_rows",
    )(left, *pieces, before, tie)


def finish_kernel(core, r0, r1, _, out, wide, sem):
    def copy(i):
        return pltpu.make_async_copy(
            wide.at[:, pl.ds(i * ROWS, ROWS)],
            out.at[:, pl.ds(pl.multiple_of((i * 2 + 1 - core[0]) * ROWS, LANES), ROWS)],
            sem.at[i],
        )

    for i in range(8):
        src = (r0, r1)[i // 4]
        wide[:, i * ROWS : (i + 1) * ROWS] = src[:, (i % 4) * ROWS : (i % 4 + 1) * ROWS].astype(jnp.float32)
        copy(i).start()
    for i in range(8):
        copy(i).wait()


def finish(core, rows, out):
    return pl.pallas_call(
        finish_kernel,
        out_shape=jax.ShapeDtypeStruct((ROWS, NG), jnp.float32),
        in_specs=[SM, VM, VM, HBM],
        out_specs=HBM,
        scratch_shapes=[pltpu.VMEM((ROWS, HALF), jnp.float32), pltpu.SemaphoreType.DMA((8,))],
        input_output_aliases={3: 0},
        compiler_params=PARAMS,
        name="finish",
    )(core, *rows, out)


def held_kernel(a, _, out):
    pass


def held(a, tie):
    return pl.pallas_call(
        held_kernel,
        out_shape=jax.ShapeDtypeStruct(a.shape, a.dtype),
        in_specs=[VM] * 2,
        out_specs=VM,
        input_output_aliases={0: 0},
        compiler_params=PARAMS,
        name="held",
    )(a, tie)


def in_vmem(a):
    return pltpu.with_memory_space_constraint(a, pltpu.VMEM)


def on_device(psi_val, psi_con, e_val, e_con, occ, omega, g_index):
    ga = lax.axis_index("ga")
    ba = lax.axis_index("ba")
    core = lax.rem(ga, 2).astype(jnp.int32)
    kinds = [[2 * i + c for i in range(8)] for c in range(2)]
    psi = lax.all_to_all(payload(psi_val, psi_con), "ga", 0, 0, tiled=True, axis_index_groups=kinds)
    psi_other = send(psi, core_pairs())

    delta = (lax.dynamic_slice(e_con, (ga * 4,), (4,))[None, :] - e_val[:, None]).reshape(PAIRS)
    taken = jnp.broadcast_to(occ.astype(jnp.float32)[:, None], (4, 4)).reshape(PAIRS)
    d1 = lax.reduce_precision(delta, 8, 7)
    d2 = lax.reduce_precision(delta - d1, 8, 7)
    d3 = delta - d1 - d2
    meta = jnp.stack([d1, d2, d3, taken], 1).astype(jnp.bfloat16)
    meta = jnp.pad(meta, ((0, 0), (0, LANES - 4)))

    halves = g_index.reshape(8, 2, ROWS).transpose(1, 0, 2).reshape(2, HALF)
    kept = lax.dynamic_slice(halves, (core, 0), (1, HALF))
    given = lax.dynamic_slice(halves, (1 - core, 0), (1, HALF))
    spec, give = rho_spectrum(core.reshape(1), psi, psi_other, given, meta)
    swapped = send(give, core_pairs())
    keep = rho_pick(spec, kept, meta)

    a = join(level(join([keep, swapped]), NEAR))
    sources = deal(level(a, EVEN))
    got = {(h, 0): m for h, m in enumerate(sources)}
    for h in range(2):
        for s in range(1, 3 + (h == 0)):
            got[h, s] = send(sources[h], offset_pairs(STEP[s]))

    place = lax.div(ga, 2).astype(jnp.int32).reshape(1)
    mine_omega = lax.dynamic_slice(omega, (ba,), (1,))
    core = core.reshape(1)
    own = other = None
    tie = jnp.zeros(TIE.shape, TIE.dtype)
    groups = (((0, 0), (1, 0)), ((1, 1), (1, 2)), ((0, 1), (0, 2), (0, 3)), ((1, 3),))
    for names in groups:
        pieces = [in_vmem(got[name]) for name in names]
        left = weighted(place, mine_omega, pieces, tie)
        mirror = send(left, core_pairs())
        if names is not groups[-1]:
            own, tie = partial_rows(names, False, left, pieces, own, tie)
            other, tie = partial_rows(names, True, mirror, pieces, other, tie)
        if names is groups[0]:
            got[1, 3] = send(held(sources[1], tie), offset_pairs(STEP[3]))
    out, tie = own_rows(names, 0, core, left, pieces, own, tie)
    rows = [send(other_rows(names, s, mirror, pieces, other, tie), core_pairs()) for s in (0, HALF // 2)]
    out, _ = own_rows(names, HALF // 2, core, left, pieces, own, out)
    return finish(core, rows, out)[None]


def solution(mesh):
    placed = (P("ba", "ga"), P(None, "ga"), P("ba"), P(), P("ba"), P(), P())
    return jax.shard_map(
        on_device, mesh=mesh, in_specs=placed, out_specs=P("ba", "ga", None), check_vma=False
    )
```

```python
import functools
import itertools
import math

import jax
import jax.numpy as jnp
import numpy as np
from jax import lax
from jax.experimental import pallas as pl
from jax.experimental.pallas import tpu as pltpu
from jax.sharding import PartitionSpec as P

NV = 32
NC = 64
N = 32768
NA = 128
NB = 256
NG = 6144
HALF = NG // 2
ROWS = 384
LANES = 128
PAIRS = 16
WIDE = HALF + LANES
BLOCK = 2 * PAIRS
CHUNK = 768
MIB = 1024 * 1024
VM = pl.BlockSpec(memory_space=pltpu.VMEM)
SM = pl.BlockSpec(memory_space=pltpu.SMEM)
HBM = pl.BlockSpec(memory_space=pltpu.HBM)
PARAMS = pltpu.CompilerParams(vmem_limit_bytes=14 * MIB)

NEAR = ((0, 0, 0), (2, 2, 2), (1, 1, 1), (3, 3, 3))
EVEN = ((0, 0, 0), (2, 0, 0), (0, 2, 0), (0, 0, 2))
STEP = ((0, 0, 0), (1, 0, 0), (0, 1, 0), (0, 0, 1))


def split_bf16(a):
    hi = a.astype(np.float32).astype(jnp.bfloat16)
    lo = (a - hi.astype(np.float64)).astype(np.float32).astype(jnp.bfloat16)
    return hi, lo


def dft_constants():
    k1 = np.arange(NA)[:, None]
    a, kind, chip = np.arange(8)[:, None, None], np.arange(2)[:, None], np.arange(8)
    first = []
    for core in range(2):
        order = ((chip * 2 + (kind + core) % 2) * 8 + a).reshape(NA)
        ang = 2.0 * math.pi * ((k1 * order[None, :]) % NA) / NA
        fh, fl = split_bf16(np.concatenate([np.cos(ang), np.sin(ang)], 0))
        first.append(np.concatenate([fh, fl], 1))
    tw = 2.0 * math.pi * ((k1 * np.arange(NB)[None, :]) % N) / N
    norm = math.sqrt(2.0 / N)
    tcos = (np.cos(tw) * norm).astype(np.float32)
    tsin = (np.sin(tw) * norm).astype(np.float32)
    b2 = 2.0 * math.pi * ((np.arange(NB)[:, None] * np.arange(NA)[None, :]) % NB) / NB
    sh, sl = split_bf16(np.concatenate([np.cos(b2), -np.sin(b2)], 0))
    return np.stack(first), tcos, tsin, np.concatenate([sh, sl], 1)


def payload_kernel(val, con, out, val_here, con_here, sem):
    copies = [
        pltpu.make_async_copy(val, val_here, sem.at[0]),
        pltpu.make_async_copy(con, con_here, sem.at[1]),
    ]
    for copy in copies:
        copy.start()
    for copy in copies:
        copy.wait()
    v = val_here[...].astype(jnp.float32)
    values = jnp.concatenate([v[:, :1024], v[:, 1024:]], 0)
    for chip in range(8):
        c = con_here[chip * 8 : chip * 8 + 8, :].astype(jnp.float32)
        rows = jnp.concatenate([c[:, :1024], c[:, 1024:], values], 0)
        out[chip] = rows.astype(jnp.bfloat16)


def payload(val, con):
    return pl.pallas_call(
        payload_kernel,
        out_shape=jax.ShapeDtypeStruct((8, 24, 1024), jnp.bfloat16),
        in_specs=[HBM] * 2,
        out_specs=VM,
        scratch_shapes=[
            pltpu.VMEM(val.shape, val.dtype),
            pltpu.VMEM(con.shape, con.dtype),
            pltpu.SemaphoreType.DMA((2,)),
        ],
        compiler_params=PARAMS,
        name="payload",
    )(val, con)


def transform(core, mine, others, first, tcos, tsin, second, spec, high, low, grid):
    for kind, ref in enumerate((mine, others)):
        for chip in range(8):
            for j in range(8):
                grid[kind, j, chip * 24 : chip * 24 + 24, :] = ref[
                    chip, :, j * LANES : (j + 1) * LANES
                ].astype(jnp.float32)

    def band(row, apart):
        parts = []
        for half in range(2):
            at = pl.ds(row + half * apart, 8, stride=24)
            for a in range(4):
                for kind in range(2):
                    parts.append(jnp.concatenate([grid[kind, 2 * a + j, at, :] for j in range(2)], 1))
        return jnp.concatenate(parts, 0)

    con = [band(core[0] * 4 + i, 8) for i in range(4)]
    ca = tcos[...]
    sa = tsin[...]
    f = first[core[0]]
    for v in range(4):
        val = band(16 + v, 4)
        for c in range(4):
            d = (val * con[c]).astype(jnp.bfloat16)
            y = jnp.dot(f, jnp.concatenate([d, d], 0), preferred_element_type=jnp.float32)
            a, b = y[:NA], y[NA:]
            uv = jnp.concatenate([a * ca - b * sa, a * sa + b * ca], 1)
            hi = uv.astype(jnp.bfloat16)
            at = slice((v * 4 + c) * NA, (v * 4 + c + 1) * NA)
            high[at, :] = hi
            low[at, :] = (uv - hi.astype(jnp.float32)).astype(jnp.bfloat16)
    for n in range(4):
        at = slice(n * 512, n * 512 + 512)
        y = jnp.dot(high[at, :], second[...], preferred_element_type=jnp.float32)
        z = jnp.dot(low[at, :], second[:, :NA], preferred_element_type=jnp.float32)
        x = (y[:, :NA] + (y[:, NA:] + z)).astype(jnp.bfloat16)
        for i in range(4):
            p = n * 4 + i
            spec[p * 64 : p * 64 + 64, 0:128] = x[i * NA : i * NA + 64]
            spec[p * 64 : p * 64 + 64, 128:256] = x[i * NA + 64 : i * NA + NA]


def pick(spec, gidx, meta, out):
    width = 1024

    def step(i, carry):
        at = pl.ds(pl.multiple_of(i * width, width), width)
        g = gidx[:, at]
        k1 = lax.bitwise_and(g, 127)
        kk = lax.shift_right_logical(k1, 6) * 128 + lax.shift_right_logical(g, 7)
        hot = jnp.where(
            lax.broadcasted_iota(jnp.int32, (256, width), 0) == kk, 1.0, 0.0
        ).astype(jnp.bfloat16)
        o = jnp.dot(spec[...], hot, preferred_element_type=jnp.float32)
        m = lax.broadcasted_iota(jnp.int32, (64, width), 0) == lax.bitwise_and(k1, 63)
        picked = jnp.sum(jnp.where(m[None], o.reshape(PAIRS, 64, width), 0.0), axis=1)
        out[:, at] = picked.astype(jnp.bfloat16)
        return carry

    lax.fori_loop(0, HALF // width, step, 0)
    out[:, HALF:WIDE] = meta[...]


def transform_kernel(core, mine, others, gidx, meta, first, tcos, tsin, second, spec, out, high, low, grid):
    transform(core, mine, others, first, tcos, tsin, second, spec, high, low, grid)
    pick(spec, gidx, meta, out)


def rho_spectrum(core, mine, others, gidx, meta):
    return pl.pallas_call(
        transform_kernel,
        out_shape=[
            jax.ShapeDtypeStruct((PAIRS * 64, 256), jnp.bfloat16),
            jax.ShapeDtypeStruct((PAIRS, WIDE), jnp.bfloat16),
        ],
        in_specs=[SM] + [VM] * 8,
        out_specs=[VM] * 2,
        scratch_shapes=[pltpu.VMEM((PAIRS * NA, 2 * NB), jnp.bfloat16)] * 2
        + [pltpu.VMEM((2, 8, 8 * 24, LANES), jnp.float32)],
        compiler_params=PARAMS,
        name="rho_spectrum",
    )(core, mine, others, gidx, meta, *(jnp.asarray(c) for c in dft_constants()))


def rho_pick(spec, gidx, meta):
    return pl.pallas_call(
        pick,
        out_shape=jax.ShapeDtypeStruct((PAIRS, WIDE), jnp.bfloat16),
        in_specs=[VM] * 3,
        out_specs=VM,
        compiler_params=PARAMS,
        name="rho_pick",
    )(spec, gidx, meta)


def device_index(x, y, z, c):
    return (z * 4 + (y >> 1) * 2 + c) * 8 + (y & 1) * 4 + x


CHIPS = tuple(itertools.product(range(4), repeat=3))


@functools.cache
def offset_pairs(offset):
    return tuple(
        (device_index(*chip, c), device_index(*((a + (1 - 2 * c) * b) % 4 for a, b in zip(chip, offset)), c))
        for chip in CHIPS for c in range(2)
    )


@functools.cache
def core_pairs():
    return tuple((device_index(*chip, c), device_index(*chip, 1 - c)) for chip in CHIPS for c in range(2))


def send(a, pairs):
    return lax.ppermute(a, ("ga", "ba"), pairs)


def level(a, offsets):
    return [a] + [send(a, offset_pairs(offset)) for offset in offsets[1:]]


def join_kernel(n, *refs):
    out = refs[n]
    row = 0
    for ref in refs[:n]:
        out[row : row + ref.shape[0], :] = ref[...]
        row += ref.shape[0]


def join(blocks):
    rows = sum(b.shape[0] for b in blocks)
    return pl.pallas_call(
        functools.partial(join_kernel, len(blocks)),
        out_shape=jax.ShapeDtypeStruct((rows, WIDE), jnp.bfloat16),
        in_specs=[VM] * len(blocks),
        out_specs=VM,
        compiler_params=PARAMS,
        name="join",
    )(*blocks)


def deal_kernel(b0, b1, b2, b3, out0, out1, both):
    for i, ref in enumerate((b0, b1, b2, b3)):
        for half, out in enumerate((out0, out1)):
            rows = ref[half * 64 : half * 64 + 64, :]
            out[i * 64 : i * 64 + 64, :] = rows
            both[half * 256 + i * 64 : half * 256 + i * 64 + 64, :] = rows


def deal(blocks):
    return pl.pallas_call(
        deal_kernel,
        out_shape=[jax.ShapeDtypeStruct((rows, WIDE), jnp.bfloat16) for rows in (256, 256, 512)],
        in_specs=[VM] * 4,
        out_specs=[VM] * 3,
        compiler_params=PARAMS,
        name="deal",
    )(*blocks)


def halves(refs):
    return [ref.at[pl.ds(at, 256)] for ref in refs for at in range(0, ref.shape[0], 256)]


def place_of(half, step):
    return [
        tuple(sum(v) % 4 for v in zip(NEAR[2 * half + i], EVEN[j], STEP[step]))
        for j in range(4) for i in range(2)
    ]


def mirrored(half, step):
    places = place_of(half, step)
    return [places.index(tuple(-v % 4 for v in p)) for p in places]


def weighted_kernel(place, omega, *refs):
    pieces, left = halves(refs[:-2]), refs[-1]
    w2 = omega[0] * omega[0]
    row = lax.broadcasted_iota(jnp.int32, (LANES, 2 * LANES), 0)
    lane = lax.broadcasted_iota(jnp.int32, (LANES, 2 * LANES), 1)
    spread = jnp.where((row < 3) & (lane < LANES) | (row == 3) & (lane >= LANES), 1.0, 0.0)
    spread = spread.astype(jnp.bfloat16)
    for i, piece in enumerate(pieces):
        m = jnp.dot(piece[:, HALF:WIDE], spread, preferred_element_type=jnp.float32)
        delta, taken = m[:, :LANES], m[:, LANES:]
        weight = (-4.0 / math.sqrt(NV * NC)) * taken * delta / (delta * delta + w2)
        for e in range(3):
            cols = pl.ds(pl.multiple_of(place[0] * ROWS + e * LANES, LANES), LANES)
            left[i * 256 : i * 256 + 256, e * LANES : (e + 1) * LANES] = (
                piece[:, cols].astype(jnp.float32) * weight
            ).astype(jnp.bfloat16)


def weighted(place, omega, pieces, tie):
    return pl.pallas_call(
        weighted_kernel,
        out_shape=jax.ShapeDtypeStruct((sum(p.shape[0] for p in pieces), ROWS), jnp.bfloat16),
        in_specs=[SM, SM] + [VM] * (len(pieces) + 1),
        out_specs=VM,
        compiler_params=PARAMS,
        name="weighted",
    )(place, omega, *pieces, tie)


def product(names, other, left, pieces, cols):
    total = None
    for i, (half, step) in enumerate(names):
        if other:
            rows = []
            for j in mirrored(half, step):
                at = i * 256 + j * BLOCK
                rows += [left[at + PAIRS : at + BLOCK, :], left[at : at + PAIRS, :]]
            mine = jnp.concatenate(rows, 0)
        else:
            mine = left[i * 256 : i * 256 + 256, :]
        term = lax.dot_general(
            mine, pieces[i][:, cols], (((0,), (0,)), ((), ())), preferred_element_type=jnp.float32
        )
        total = term if total is None else total + term
    return total


def chunk(i, width=CHUNK, start=0):
    return pl.ds(pl.multiple_of(start + i * width, LANES), width)


def cost(names, columns):
    return pl.CostEstimate(
        flops=2 * ROWS * columns * 256 * len(names),
        bytes_accessed=(2 * 256 * len(names) + 8 * ROWS) * columns,
        transcendentals=0,
    )


def partial_kernel(names, n, other, left, *refs):
    pieces, before = halves(refs[:n]), refs[n:-3]
    out, after = refs[-2:]
    after[...] = jnp.zeros_like(after)

    def step(i, carry):
        total = product(names, other, left, pieces, chunk(i))
        out[:, chunk(i)] = total + before[0][:, chunk(i)] if before else total
        return carry

    lax.fori_loop(0, HALF // CHUNK, step, 0)


TIE = jax.ShapeDtypeStruct((8, LANES), jnp.float32)


def partial_rows(names, other, left, pieces, before, tie):
    before = [] if before is None else [before]
    return pl.pallas_call(
        functools.partial(partial_kernel, names, len(pieces), other),
        out_shape=[jax.ShapeDtypeStruct((ROWS, HALF), jnp.float32), TIE],
        in_specs=[VM] * (2 + len(pieces) + len(before)),
        out_specs=[VM] * 2,
        input_output_aliases={1 + len(pieces): 0} if before else {},
        compiler_params=PARAMS,
        cost_estimate=cost(names, HALF),
        name="partial_other" if other else "partial_own",
    )(left, *pieces, *before, tie)


def own_kernel(names, n, start, core, left, *refs):
    pieces = halves(refs[:n])
    before, _, out, tie, wide, sem = refs[n:]
    tie[...] = jnp.zeros_like(tie)
    copies = []
    for i in range(2):
        cols = slice(start + i * CHUNK, start + (i + 1) * CHUNK)
        wide[:, i * CHUNK : (i + 1) * CHUNK] = product(names, False, left, pieces, cols) + before[:, cols]
        for j in (2 * i, 2 * i + 1):
            block = (start // ROWS + j) * 2 + core[0]
            copies.append(
                pltpu.make_async_copy(
                    wide.at[:, pl.ds(j * ROWS, ROWS)],
                    out.at[:, pl.ds(pl.multiple_of(block * ROWS, LANES), ROWS)],
                    sem.at[j],
                )
            )
            copies[-1].start()
    for copy in copies:
        copy.wait()


def own_rows(names, start, core, left, pieces, before, after):
    grows = after.shape == (ROWS, NG)
    return pl.pallas_call(
        functools.partial(own_kernel, names, len(pieces), start),
        out_shape=[jax.ShapeDtypeStruct((ROWS, NG), jnp.float32), TIE],
        in_specs=[SM, VM] + [VM] * (len(pieces) + 1) + [HBM if grows else VM],
        out_specs=[HBM, VM],
        scratch_shapes=[pltpu.VMEM((ROWS, HALF // 2), jnp.float32), pltpu.SemaphoreType.DMA((4,))],
        input_output_aliases={3 + len(pieces): 0} if grows else {},
        compiler_params=PARAMS,
        cost_estimate=cost(names, HALF // 2),
        name="own_rows",
    )(core, left, *pieces, before, after)


def other_kernel(names, n, start, left, *refs):
    pieces = halves(refs[:n])
    before, _, out = refs[n:]

    def step(i, carry):
        total = product(names, True, left, pieces, chunk(i, start=start)) + before[:, chunk(i, start=start)]
        out[:, chunk(i)] = total.astype(jnp.bfloat16)
        return carry

    lax.fori_loop(0, 2, step, 0)


def other_rows(names, start, left, pieces, before, tie):
    return pl.pallas_call(
        functools.partial(other_kernel, names, len(pieces), start),
        out_shape=jax.ShapeDtypeStruct((ROWS, HALF // 2), jnp.bfloat16),
        in_specs=[VM] * (len(pieces) + 3),
        out_specs=VM,
        compiler_params=PARAMS,
        cost_estimate=cost(names, HALF // 2),
        name="other_rows",
    )(left, *pieces, before, tie)


def finish_kernel(core, r0, r1, _, out, wide, sem):
    def copy(i):
        return pltpu.make_async_copy(
            wide.at[:, pl.ds(i * ROWS, ROWS)],
            out.at[:, pl.ds(pl.multiple_of((i * 2 + 1 - core[0]) * ROWS, LANES), ROWS)],
            sem.at[i],
        )

    for i in range(8):
        src = (r0, r1)[i // 4]
        wide[:, i * ROWS : (i + 1) * ROWS] = src[:, (i % 4) * ROWS : (i % 4 + 1) * ROWS].astype(jnp.float32)
        copy(i).start()
    for i in range(8):
        copy(i).wait()


def finish(core, rows, out):
    return pl.pallas_call(
        finish_kernel,
        out_shape=jax.ShapeDtypeStruct((ROWS, NG), jnp.float32),
        in_specs=[SM, VM, VM, HBM],
        out_specs=HBM,
        scratch_shapes=[pltpu.VMEM((ROWS, HALF), jnp.float32), pltpu.SemaphoreType.DMA((8,))],
        input_output_aliases={3: 0},
        compiler_params=PARAMS,
        name="finish",
    )(core, *rows, out)


def in_vmem(a):
    return pltpu.with_memory_space_constraint(a, pltpu.VMEM)


def on_device(psi_val, psi_con, e_val, e_con, occ, omega, g_index):
    ga = lax.axis_index("ga")
    ba = lax.axis_index("ba")
    core = lax.rem(ga, 2).astype(jnp.int32)
    kinds = [[2 * i + c for i in range(8)] for c in range(2)]
    psi = lax.all_to_all(payload(psi_val, psi_con), "ga", 0, 0, tiled=True, axis_index_groups=kinds)
    psi_other = send(psi, core_pairs())

    delta = (lax.dynamic_slice(e_con, (ga * 4,), (4,))[None, :] - e_val[:, None]).reshape(PAIRS)
    taken = jnp.broadcast_to(occ.astype(jnp.float32)[:, None], (4, 4)).reshape(PAIRS)
    d1 = lax.reduce_precision(delta, 8, 7)
    d2 = lax.reduce_precision(delta - d1, 8, 7)
    d3 = delta - d1 - d2
    meta = jnp.stack([d1, d2, d3, taken], 1).astype(jnp.bfloat16)
    meta = jnp.pad(meta, ((0, 0), (0, LANES - 4)))

    kinds_of_rows = g_index.reshape(8, 2, ROWS).transpose(1, 0, 2).reshape(2, HALF)
    kept = lax.dynamic_slice(kinds_of_rows, (core, 0), (1, HALF))
    given = lax.dynamic_slice(kinds_of_rows, (1 - core, 0), (1, HALF))
    spec, give = rho_spectrum(core.reshape(1), psi, psi_other, given, meta)
    swapped = send(give, core_pairs())
    keep = rho_pick(spec, kept, meta)

    a = join(level(join([keep, swapped]), NEAR))
    *sources, both = deal(level(a, EVEN))
    got = {(h, 0): m for h, m in enumerate(sources)}
    for h in range(2):
        for s in (1, 2):
            got[h, s] = send(sources[h], offset_pairs(STEP[s]))
    got["z"] = send(both, offset_pairs(STEP[3]))

    place = lax.div(ga, 2).astype(jnp.int32).reshape(1)
    mine_omega = lax.dynamic_slice(omega, (ba,), (1,))
    core = core.reshape(1)
    own = other = None
    tie = jnp.zeros(TIE.shape, TIE.dtype)
    groups = (((0, 0), (1, 0)), ((0, 1), (0, 2)), ((1, 1), (1, 2)), ((0, 3), (1, 3)))
    for names in groups:
        pieces = [in_vmem(got[name]) for name in (("z",) if names is groups[-1] else names)]
        left = weighted(place, mine_omega, pieces, tie)
        mirror = send(left, core_pairs())
        if names is not groups[-1]:
            own, tie = partial_rows(names, False, left, pieces, own, tie)
            other, tie = partial_rows(names, True, mirror, pieces, other, tie)
    out, tie = own_rows(names, 0, core, left, pieces, own, tie)
    rows = [send(other_rows(names, s, mirror, pieces, other, tie), core_pairs()) for s in (0, HALF // 2)]
    out, _ = own_rows(names, HALF // 2, core, left, pieces, own, out)
    return finish(core, rows, out)[None]


def solution(mesh):
    placed = (P("ba", "ga"), P(None, "ga"), P("ba"), P(), P("ba"), P(), P())
    return jax.shard_map(
        on_device, mesh=mesh, in_specs=placed, out_specs=P("ba", "ga", None), check_vma=False
    )
```

```python
import functools
import itertools
import math

import jax
import jax.numpy as jnp
import numpy as np
from jax import lax
from jax.experimental import pallas as pl
from jax.experimental.pallas import tpu as pltpu
from jax.sharding import PartitionSpec as P

NV = 32
NC = 64
N = 32768
NA = 128
NB = 256
NG = 6144
HALF = NG // 2
ROWS = 384
LANES = 128
PAIRS = 16
WIDE = HALF + LANES
BLOCK = 2 * PAIRS
CHUNK = 768
MIB = 1024 * 1024
VM = pl.BlockSpec(memory_space=pltpu.VMEM)
SM = pl.BlockSpec(memory_space=pltpu.SMEM)
HBM = pl.BlockSpec(memory_space=pltpu.HBM)
PARAMS = pltpu.CompilerParams(vmem_limit_bytes=14 * MIB)

NEAR = ((0, 0, 0), (2, 2, 2), (1, 1, 1), (3, 3, 3))
EVEN = ((0, 0, 0), (2, 0, 0), (0, 2, 0), (0, 0, 2))
STEP = ((0, 0, 0), (1, 0, 0), (0, 1, 0), (0, 0, 1))


def split_bf16(a):
    hi = a.astype(np.float32).astype(jnp.bfloat16)
    lo = (a - hi.astype(np.float64)).astype(np.float32).astype(jnp.bfloat16)
    return hi, lo


def dft_constants():
    k1 = np.arange(NA)[:, None]
    a, kind, chip = np.arange(8)[:, None, None], np.arange(2)[:, None], np.arange(8)
    first = []
    for core in range(2):
        order = ((chip * 2 + (kind + core) % 2) * 8 + a).reshape(NA)
        ang = 2.0 * math.pi * ((k1 * order[None, :]) % NA) / NA
        fh, fl = split_bf16(np.concatenate([np.cos(ang), np.sin(ang)], 0))
        first.append(np.concatenate([fh, fl], 1))
    tw = 2.0 * math.pi * ((k1 * np.arange(NB)[None, :]) % N) / N
    norm = math.sqrt(2.0 / N)
    tcos = (np.cos(tw) * norm).astype(np.float32)
    tsin = (np.sin(tw) * norm).astype(np.float32)
    b2 = 2.0 * math.pi * ((np.arange(NB)[:, None] * np.arange(NA)[None, :]) % NB) / NB
    sh, sl = split_bf16(np.concatenate([np.cos(b2), -np.sin(b2)], 0))
    return np.stack(first), tcos, tsin, np.concatenate([sh, sl], 1)


def payload_kernel(val, con, first, tcos, tsin, second, out, *refs):
    here, (val_here, con_here, sem) = refs[:4], refs[4:]
    pairs = [(val, val_here), (con, con_here), *zip((first, tcos, tsin, second), here)]
    copies = [pltpu.make_async_copy(src, dst, sem.at[i]) for i, (src, dst) in enumerate(pairs)]
    for copy in copies:
        copy.start()
    for copy in copies[:2]:
        copy.wait()
    v = val_here[...].astype(jnp.float32)
    values = jnp.concatenate([v[:, :1024], v[:, 1024:]], 0)
    for chip in range(8):
        c = con_here[chip * 8 : chip * 8 + 8, :].astype(jnp.float32)
        rows = jnp.concatenate([c[:, :1024], c[:, 1024:], values], 0)
        out[chip] = rows.astype(jnp.bfloat16)
    for copy in copies[2:]:
        copy.wait()


def payload(val, con):
    constants = [jnp.asarray(c) for c in dft_constants()]
    operands = [pltpu.with_memory_space_constraint(a, pltpu.HBM) for a in (val, con, *constants)]
    return pl.pallas_call(
        payload_kernel,
        out_shape=[pltpu.VMEM((8, 24, 1024), jnp.bfloat16)]
        + [pltpu.VMEM(c.shape, c.dtype) for c in constants],
        in_specs=[HBM] * 6,
        out_specs=[VM] * 5,
        scratch_shapes=[
            pltpu.VMEM(val.shape, val.dtype),
            pltpu.VMEM(con.shape, con.dtype),
            pltpu.SemaphoreType.DMA((6,)),
        ],
        compiler_params=PARAMS,
        name="payload",
    )(*operands)


def transform(core, mine, others, first, tcos, tsin, second, spec, high, low, grid):
    for kind, ref in enumerate((mine, others)):
        for chip in range(8):
            for j in range(8):
                grid[kind, j, chip * 24 : chip * 24 + 24, :] = ref[
                    chip, :, j * LANES : (j + 1) * LANES
                ].astype(jnp.float32)

    def band(row, apart):
        parts = []
        for half in range(2):
            at = pl.ds(row + half * apart, 8, stride=24)
            for a in range(4):
                for kind in range(2):
                    parts.append(jnp.concatenate([grid[kind, 2 * a + j, at, :] for j in range(2)], 1))
        return jnp.concatenate(parts, 0)

    con = [band(core[0] * 4 + i, 8) for i in range(4)]
    ca = tcos[...]
    sa = tsin[...]
    f = first[core[0]]
    for v in range(4):
        val = band(16 + v, 4)
        for c in range(4):
            d = (val * con[c]).astype(jnp.bfloat16)
            y = jnp.dot(f, jnp.concatenate([d, d], 0), preferred_element_type=jnp.float32)
            a, b = y[:NA], y[NA:]
            uv = jnp.concatenate([a * ca - b * sa, a * sa + b * ca], 1)
            hi = uv.astype(jnp.bfloat16)
            at = slice((v * 4 + c) * NA, (v * 4 + c + 1) * NA)
            high[at, :] = hi
            low[at, :] = (uv - hi.astype(jnp.float32)).astype(jnp.bfloat16)
    for n in range(4):
        at = slice(n * 512, n * 512 + 512)
        y = jnp.dot(high[at, :], second[...], preferred_element_type=jnp.float32)
        z = jnp.dot(low[at, :], second[:, :NA], preferred_element_type=jnp.float32)
        x = (y[:, :NA] + (y[:, NA:] + z)).astype(jnp.bfloat16)
        for i in range(4):
            p = n * 4 + i
            spec[p * 64 : p * 64 + 64, 0:128] = x[i * NA : i * NA + 64]
            spec[p * 64 : p * 64 + 64, 128:256] = x[i * NA + 64 : i * NA + NA]


def pick(spec, gidx, meta, out):
    width = 1024

    def step(i, carry):
        at = pl.ds(pl.multiple_of(i * width, width), width)
        g = gidx[:, at]
        k1 = lax.bitwise_and(g, 127)
        kk = lax.shift_right_logical(k1, 6) * 128 + lax.shift_right_logical(g, 7)
        hot = jnp.where(
            lax.broadcasted_iota(jnp.int32, (256, width), 0) == kk, 1.0, 0.0
        ).astype(jnp.bfloat16)
        o = jnp.dot(spec[...], hot, preferred_element_type=jnp.float32)
        m = lax.broadcasted_iota(jnp.int32, (64, width), 0) == lax.bitwise_and(k1, 63)
        picked = jnp.sum(jnp.where(m[None], o.reshape(PAIRS, 64, width), 0.0), axis=1)
        out[:, at] = picked.astype(jnp.bfloat16)
        return carry

    lax.fori_loop(0, HALF // width, step, 0)
    out[:, HALF:WIDE] = meta[...]


def transform_kernel(core, mine, others, gidx, meta, first, tcos, tsin, second, spec, out, high, low, grid):
    transform(core, mine, others, first, tcos, tsin, second, spec, high, low, grid)
    pick(spec, gidx, meta, out)


def rho_spectrum(core, mine, others, gidx, meta, constants):
    return pl.pallas_call(
        transform_kernel,
        out_shape=[
            pltpu.VMEM((PAIRS * 64, 256), jnp.bfloat16),
            pltpu.VMEM((PAIRS, WIDE), jnp.bfloat16),
        ],
        in_specs=[SM] + [VM] * 8,
        out_specs=[VM] * 2,
        scratch_shapes=[pltpu.VMEM((PAIRS * NA, 2 * NB), jnp.bfloat16)] * 2
        + [pltpu.VMEM((2, 8, 8 * 24, LANES), jnp.float32)],
        compiler_params=PARAMS,
        name="rho_spectrum",
    )(core, mine, others, gidx, meta, *constants)


def rho_pick(spec, gidx, meta):
    return pl.pallas_call(
        pick,
        out_shape=pltpu.VMEM((PAIRS, WIDE), jnp.bfloat16),
        in_specs=[VM] * 3,
        out_specs=VM,
        compiler_params=PARAMS,
        name="rho_pick",
    )(spec, gidx, meta)


def device_index(x, y, z, c):
    return (z * 4 + (y >> 1) * 2 + c) * 8 + (y & 1) * 4 + x


CHIPS = tuple(itertools.product(range(4), repeat=3))


@functools.cache
def offset_pairs(offset):
    return tuple(
        (device_index(*chip, c), device_index(*((a + (1 - 2 * c) * b) % 4 for a, b in zip(chip, offset)), c))
        for chip in CHIPS for c in range(2)
    )


@functools.cache
def core_pairs():
    return tuple((device_index(*chip, c), device_index(*chip, 1 - c)) for chip in CHIPS for c in range(2))


def send(a, pairs):
    return lax.ppermute(a, ("ga", "ba"), pairs)


def level(a, offsets):
    return [a] + [send(a, offset_pairs(offset)) for offset in offsets[1:]]


def join_kernel(n, *refs):
    out = refs[n]
    row = 0
    for ref in refs[:n]:
        out[row : row + ref.shape[0], :] = ref[...]
        row += ref.shape[0]


def join(blocks):
    rows = sum(b.shape[0] for b in blocks)
    return pl.pallas_call(
        functools.partial(join_kernel, len(blocks)),
        out_shape=pltpu.VMEM((rows, WIDE), jnp.bfloat16),
        in_specs=[VM] * len(blocks),
        out_specs=VM,
        compiler_params=PARAMS,
        name="join",
    )(*blocks)


def deal_kernel(b0, b1, b2, b3, out0, out1, both):
    for i, ref in enumerate((b0, b1, b2, b3)):
        for half, out in enumerate((out0, out1)):
            rows = ref[half * 64 : half * 64 + 64, :]
            out[i * 64 : i * 64 + 64, :] = rows
            both[half * 256 + i * 64 : half * 256 + i * 64 + 64, :] = rows


def deal(blocks):
    return pl.pallas_call(
        deal_kernel,
        out_shape=[pltpu.VMEM((rows, WIDE), jnp.bfloat16) for rows in (256, 256, 512)],
        in_specs=[VM] * 4,
        out_specs=[VM] * 3,
        compiler_params=PARAMS,
        name="deal",
    )(*blocks)


def halves(refs):
    return [ref.at[pl.ds(at, 256)] for ref in refs for at in range(0, ref.shape[0], 256)]


def place_of(half, step):
    return [
        tuple(sum(v) % 4 for v in zip(NEAR[2 * half + i], EVEN[j], STEP[step]))
        for j in range(4) for i in range(2)
    ]


def mirrored(half, step):
    places = place_of(half, step)
    return [places.index(tuple(-v % 4 for v in p)) for p in places]


def weighted_kernel(place, omega, *refs):
    pieces, left = halves(refs[:-2]), refs[-1]
    w2 = omega[0] * omega[0]
    row = lax.broadcasted_iota(jnp.int32, (LANES, 2 * LANES), 0)
    lane = lax.broadcasted_iota(jnp.int32, (LANES, 2 * LANES), 1)
    spread = jnp.where((row < 3) & (lane < LANES) | (row == 3) & (lane >= LANES), 1.0, 0.0)
    spread = spread.astype(jnp.bfloat16)
    for i, piece in enumerate(pieces):
        m = jnp.dot(piece[:, HALF:WIDE], spread, preferred_element_type=jnp.float32)
        delta, taken = m[:, :LANES], m[:, LANES:]
        weight = (-4.0 / math.sqrt(NV * NC)) * taken * delta / (delta * delta + w2)
        for e in range(3):
            cols = pl.ds(pl.multiple_of(place[0] * ROWS + e * LANES, LANES), LANES)
            left[i * 256 : i * 256 + 256, e * LANES : (e + 1) * LANES] = (
                piece[:, cols].astype(jnp.float32) * weight
            ).astype(jnp.bfloat16)


def weighted(place, omega, pieces, tie):
    return pl.pallas_call(
        weighted_kernel,
        out_shape=pltpu.VMEM((sum(p.shape[0] for p in pieces), ROWS), jnp.bfloat16),
        in_specs=[SM, SM] + [VM] * (len(pieces) + 1),
        out_specs=VM,
        compiler_params=PARAMS,
        name="weighted",
    )(place, omega, *pieces, tie)


def product(names, other, left, pieces, cols):
    total = None
    for i, (half, step) in enumerate(names):
        if other:
            rows = []
            for j in mirrored(half, step):
                at = i * 256 + j * BLOCK
                rows += [left[at + PAIRS : at + BLOCK, :], left[at : at + PAIRS, :]]
            mine = jnp.concatenate(rows, 0)
        else:
            mine = left[i * 256 : i * 256 + 256, :]
        term = lax.dot_general(
            mine, pieces[i][:, cols], (((0,), (0,)), ((), ())), preferred_element_type=jnp.float32
        )
        total = term if total is None else total + term
    return total


def chunk(i, width=CHUNK, start=0):
    return pl.ds(pl.multiple_of(start + i * width, LANES), width)


def cost(names, columns):
    return pl.CostEstimate(
        flops=2 * ROWS * columns * 256 * len(names),
        bytes_accessed=(2 * 256 * len(names) + 8 * ROWS) * columns,
        transcendentals=0,
    )


def partial_kernel(names, n, other, left, *refs):
    pieces, before = halves(refs[:n]), refs[n:-3]
    out, after = refs[-2:]
    after[...] = jnp.zeros_like(after)

    def step(i, carry):
        total = product(names, other, left, pieces, chunk(i))
        out[:, chunk(i)] = total + before[0][:, chunk(i)] if before else total
        return carry

    lax.fori_loop(0, HALF // CHUNK, step, 0)


TIE = jax.ShapeDtypeStruct((8, LANES), jnp.float32)


def partial_rows(names, other, left, pieces, before, tie):
    before = [] if before is None else [before]
    return pl.pallas_call(
        functools.partial(partial_kernel, names, len(pieces), other),
        out_shape=[pltpu.VMEM((ROWS, HALF), jnp.float32), TIE],
        in_specs=[VM] * (2 + len(pieces) + len(before)),
        out_specs=[VM] * 2,
        input_output_aliases={1 + len(pieces): 0} if before else {},
        compiler_params=PARAMS,
        cost_estimate=cost(names, HALF),
        name="partial_other" if other else "partial_own",
    )(left, *pieces, *before, tie)


def own_kernel(names, n, start, core, left, *refs):
    pieces = halves(refs[:n])
    before, _, out, tie, wide, sem = refs[n:]
    tie[...] = jnp.zeros_like(tie)
    copies = []
    for i in range(2):
        cols = slice(start + i * CHUNK, start + (i + 1) * CHUNK)
        wide[:, i * CHUNK : (i + 1) * CHUNK] = product(names, False, left, pieces, cols) + before[:, cols]
        for j in (2 * i, 2 * i + 1):
            block = (start // ROWS + j) * 2 + core[0]
            copies.append(
                pltpu.make_async_copy(
                    wide.at[:, pl.ds(j * ROWS, ROWS)],
                    out.at[:, pl.ds(pl.multiple_of(block * ROWS, LANES), ROWS)],
                    sem.at[j],
                )
            )
            copies[-1].start()
    for copy in copies:
        copy.wait()


def own_rows(names, start, core, left, pieces, before, after):
    grows = after.shape == (ROWS, NG)
    return pl.pallas_call(
        functools.partial(own_kernel, names, len(pieces), start),
        out_shape=[jax.ShapeDtypeStruct((ROWS, NG), jnp.float32), TIE],
        in_specs=[SM, VM] + [VM] * (len(pieces) + 1) + [HBM if grows else VM],
        out_specs=[HBM, VM],
        scratch_shapes=[pltpu.VMEM((ROWS, HALF // 2), jnp.float32), pltpu.SemaphoreType.DMA((4,))],
        input_output_aliases={3 + len(pieces): 0} if grows else {},
        compiler_params=PARAMS,
        cost_estimate=cost(names, HALF // 2),
        name="own_rows",
    )(core, left, *pieces, before, after)


def other_kernel(names, n, start, left, *refs):
    pieces = halves(refs[:n])
    before, _, out = refs[n:]

    def step(i, carry):
        total = product(names, True, left, pieces, chunk(i, start=start)) + before[:, chunk(i, start=start)]
        out[:, chunk(i)] = total.astype(jnp.bfloat16)
        return carry

    lax.fori_loop(0, 2, step, 0)


def other_rows(names, start, left, pieces, before, tie):
    return pl.pallas_call(
        functools.partial(other_kernel, names, len(pieces), start),
        out_shape=pltpu.VMEM((ROWS, HALF // 2), jnp.bfloat16),
        in_specs=[VM] * (len(pieces) + 3),
        out_specs=VM,
        compiler_params=PARAMS,
        cost_estimate=cost(names, HALF // 2),
        name="other_rows",
    )(left, *pieces, before, tie)


def finish_kernel(core, r0, r1, _, out, wide, sem):
    def copy(i):
        return pltpu.make_async_copy(
            wide.at[:, pl.ds(i * ROWS, ROWS)],
            out.at[:, pl.ds(pl.multiple_of((i * 2 + 1 - core[0]) * ROWS, LANES), ROWS)],
            sem.at[i],
        )

    for i in range(8):
        src = (r0, r1)[i // 4]
        wide[:, i * ROWS : (i + 1) * ROWS] = src[:, (i % 4) * ROWS : (i % 4 + 1) * ROWS].astype(jnp.float32)
        copy(i).start()
    for i in range(8):
        copy(i).wait()


def finish(core, rows, out):
    return pl.pallas_call(
        finish_kernel,
        out_shape=jax.ShapeDtypeStruct((ROWS, NG), jnp.float32),
        in_specs=[SM, VM, VM, HBM],
        out_specs=HBM,
        scratch_shapes=[pltpu.VMEM((ROWS, HALF), jnp.float32), pltpu.SemaphoreType.DMA((8,))],
        input_output_aliases={3: 0},
        compiler_params=PARAMS,
        name="finish",
    )(core, *rows, out)


def in_vmem(a):
    return pltpu.with_memory_space_constraint(a, pltpu.VMEM)


def on_device(psi_val, psi_con, e_val, e_con, occ, omega, g_index):
    ga = lax.axis_index("ga")
    ba = lax.axis_index("ba")
    core = lax.rem(ga, 2).astype(jnp.int32)
    kinds = [[2 * i + c for i in range(8)] for c in range(2)]
    rows, *constants = payload(psi_val, psi_con)
    psi = lax.all_to_all(rows, "ga", 0, 0, tiled=True, axis_index_groups=kinds)
    psi_other = send(psi, core_pairs())

    delta = (lax.dynamic_slice(e_con, (ga * 4,), (4,))[None, :] - e_val[:, None]).reshape(PAIRS)
    taken = jnp.broadcast_to(occ.astype(jnp.float32)[:, None], (4, 4)).reshape(PAIRS)
    d1 = lax.reduce_precision(delta, 8, 7)
    d2 = lax.reduce_precision(delta - d1, 8, 7)
    d3 = delta - d1 - d2
    meta = jnp.stack([d1, d2, d3, taken], 1).astype(jnp.bfloat16)
    meta = jnp.pad(meta, ((0, 0), (0, LANES - 4)))

    kinds_of_rows = g_index.reshape(8, 2, ROWS).transpose(1, 0, 2).reshape(2, HALF)
    kept = lax.dynamic_slice(kinds_of_rows, (core, 0), (1, HALF))
    given = lax.dynamic_slice(kinds_of_rows, (1 - core, 0), (1, HALF))
    spec, give = rho_spectrum(core.reshape(1), psi, psi_other, given, meta, constants)
    swapped = send(give, core_pairs())
    keep = rho_pick(spec, kept, meta)

    a = join(level(join([keep, swapped]), NEAR))
    *sources, both = deal(level(a, EVEN))
    got = {(h, 0): m for h, m in enumerate(sources)}
    for h in range(2):
        for s in (1, 2):
            got[h, s] = send(sources[h], offset_pairs(STEP[s]))
    got["z"] = send(both, offset_pairs(STEP[3]))

    place = lax.div(ga, 2).astype(jnp.int32).reshape(1)
    mine_omega = lax.dynamic_slice(omega, (ba,), (1,))
    core = core.reshape(1)
    own = other = None
    tie = jnp.zeros(TIE.shape, TIE.dtype)
    groups = (((0, 0), (1, 0)), ((0, 1), (0, 2)), ((1, 1), (1, 2)), ((0, 3), (1, 3)))
    for names in groups:
        pieces = [in_vmem(got[name]) for name in (("z",) if names is groups[-1] else names)]
        left = weighted(place, mine_omega, pieces, tie)
        mirror = send(left, core_pairs())
        if names is not groups[-1]:
            own, tie = partial_rows(names, False, left, pieces, own, tie)
            other, tie = partial_rows(names, True, mirror, pieces, other, tie)
    out, tie = own_rows(names, 0, core, left, pieces, own, tie)
    rows = [send(other_rows(names, s, mirror, pieces, other, tie), core_pairs()) for s in (0, HALF // 2)]
    out, _ = own_rows(names, HALF // 2, core, left, pieces, own, out)
    return finish(core, rows, out)[None]


def solution(mesh):
    placed = (P("ba", "ga"), P(None, "ga"), P("ba"), P(), P("ba"), P(), P())
    return jax.shard_map(
        on_device, mesh=mesh, in_specs=placed, out_specs=P("ba", "ga", None), check_vma=False
    )
```

```python
import functools
import itertools
import math

import jax
import jax.numpy as jnp
import numpy as np
from jax import lax
from jax.experimental import pallas as pl
from jax.experimental.pallas import tpu as pltpu
from jax.sharding import PartitionSpec as P

NV = 32
NC = 64
N = 32768
NA = 128
NB = 256
NG = 6144
HALF = NG // 2
ROWS = 384
LANES = 128
PAIRS = 16
WIDE = HALF + LANES
BLOCK = 2 * PAIRS
CHUNK = 768
MIB = 1024 * 1024
VM = pl.BlockSpec(memory_space=pltpu.VMEM)
SM = pl.BlockSpec(memory_space=pltpu.SMEM)
HBM = pl.BlockSpec(memory_space=pltpu.HBM)
PARAMS = pltpu.CompilerParams(vmem_limit_bytes=14 * MIB)

NEAR = ((0, 0, 0), (2, 2, 2), (1, 1, 1), (3, 3, 3))
EVEN = ((0, 0, 0), (2, 0, 0), (0, 2, 0), (0, 0, 2))
STEP = ((0, 0, 0), (1, 0, 0), (0, 1, 0), (0, 0, 1))


def split_bf16(a):
    hi = a.astype(np.float32).astype(jnp.bfloat16)
    lo = (a - hi.astype(np.float64)).astype(np.float32).astype(jnp.bfloat16)
    return hi, lo


def dft_constants():
    k1 = np.arange(NA)[:, None]
    a, kind, chip = np.arange(8)[:, None, None], np.arange(2)[:, None], np.arange(8)
    first = []
    for core in range(2):
        order = ((chip * 2 + (kind + core) % 2) * 8 + a).reshape(NA)
        ang = 2.0 * math.pi * ((k1 * order[None, :]) % NA) / NA
        fh, fl = split_bf16(np.concatenate([np.cos(ang), np.sin(ang)], 0))
        first.append(np.concatenate([fh, fl], 1))
    tw = 2.0 * math.pi * ((k1 * np.arange(NB)[None, :]) % N) / N
    norm = math.sqrt(2.0 / N)
    tcos = (np.cos(tw) * norm).astype(np.float32)
    tsin = (np.sin(tw) * norm).astype(np.float32)
    b2 = 2.0 * math.pi * ((np.arange(NB)[:, None] * np.arange(NA)[None, :]) % NB) / NB
    sh, sl = split_bf16(np.concatenate([np.cos(b2), -np.sin(b2)], 0))
    return np.stack(first), tcos, tsin, np.concatenate([sh, sl], 1)


def payload_kernel(val, con, first, tcos, tsin, second, out, *refs):
    here, (val_here, con_here, sem) = refs[:4], refs[4:]
    pairs = [(val, val_here), (con, con_here), *zip((first, tcos, tsin, second), here)]
    copies = [pltpu.make_async_copy(src, dst, sem.at[i]) for i, (src, dst) in enumerate(pairs)]
    for copy in copies:
        copy.start()
    for copy in copies[:2]:
        copy.wait()
    v = val_here[...].astype(jnp.float32)
    values = jnp.concatenate([v[:, :1024], v[:, 1024:]], 0)
    for chip in range(8):
        c = con_here[chip * 8 : chip * 8 + 8, :].astype(jnp.float32)
        rows = jnp.concatenate([c[:, :1024], c[:, 1024:], values], 0)
        out[chip] = rows.astype(jnp.bfloat16)
    for copy in copies[2:]:
        copy.wait()


def payload(val, con):
    constants = [jnp.asarray(c) for c in dft_constants()]
    operands = [pltpu.with_memory_space_constraint(a, pltpu.HBM) for a in (val, con, *constants)]
    return pl.pallas_call(
        payload_kernel,
        out_shape=[pltpu.VMEM((8, 24, 1024), jnp.bfloat16)]
        + [pltpu.VMEM(c.shape, c.dtype) for c in constants],
        in_specs=[HBM] * 6,
        out_specs=[VM] * 5,
        scratch_shapes=[
            pltpu.VMEM(val.shape, val.dtype),
            pltpu.VMEM(con.shape, con.dtype),
            pltpu.SemaphoreType.DMA((6,)),
        ],
        compiler_params=PARAMS,
        name="payload",
    )(*operands)


def transform(core, mine, others, first, tcos, tsin, second, spec, high, low, grid):
    for kind, ref in enumerate((mine, others)):
        for chip in range(8):
            for j in range(8):
                grid[kind, j, chip * 24 : chip * 24 + 24, :] = ref[
                    chip, :, j * LANES : (j + 1) * LANES
                ].astype(jnp.float32)

    def band(row, apart):
        parts = []
        for half in range(2):
            at = pl.ds(row + half * apart, 8, stride=24)
            for a in range(4):
                for kind in range(2):
                    parts.append(jnp.concatenate([grid[kind, 2 * a + j, at, :] for j in range(2)], 1))
        return jnp.concatenate(parts, 0)

    con = [band(core[0] * 4 + i, 8) for i in range(4)]
    ca = tcos[...]
    sa = tsin[...]
    f = first[core[0]]
    for v in range(4):
        val = band(16 + v, 4)
        for c in range(4):
            d = (val * con[c]).astype(jnp.bfloat16)
            y = jnp.dot(f, jnp.concatenate([d, d], 0), preferred_element_type=jnp.float32)
            a, b = y[:NA], y[NA:]
            uv = jnp.concatenate([a * ca - b * sa, a * sa + b * ca], 1)
            hi = uv.astype(jnp.bfloat16)
            at = slice((v * 4 + c) * NA, (v * 4 + c + 1) * NA)
            high[at, :] = hi
            low[at, :] = (uv - hi.astype(jnp.float32)).astype(jnp.bfloat16)
    for n in range(4):
        at = slice(n * 512, n * 512 + 512)
        y = jnp.dot(high[at, :], second[...], preferred_element_type=jnp.float32)
        z = jnp.dot(low[at, :], second[:, :NA], preferred_element_type=jnp.float32)
        x = (y[:, :NA] + (y[:, NA:] + z)).astype(jnp.bfloat16)
        for i in range(4):
            p = n * 4 + i
            spec[p * 64 : p * 64 + 64, 0:128] = x[i * NA : i * NA + 64]
            spec[p * 64 : p * 64 + 64, 128:256] = x[i * NA + 64 : i * NA + NA]


def pick(spec, gidx, meta, out):
    width = 1024

    def step(i, carry):
        at = pl.ds(pl.multiple_of(i * width, width), width)
        g = gidx[:, at]
        k1 = lax.bitwise_and(g, 127)
        kk = lax.shift_right_logical(k1, 6) * 128 + lax.shift_right_logical(g, 7)
        hot = jnp.where(
            lax.broadcasted_iota(jnp.int32, (256, width), 0) == kk, 1.0, 0.0
        ).astype(jnp.bfloat16)
        o = jnp.dot(spec[...], hot, preferred_element_type=jnp.float32)
        m = lax.broadcasted_iota(jnp.int32, (64, width), 0) == lax.bitwise_and(k1, 63)
        picked = jnp.sum(jnp.where(m[None], o.reshape(PAIRS, 64, width), 0.0), axis=1)
        out[:, at] = picked.astype(jnp.bfloat16)
        return carry

    lax.fori_loop(0, HALF // width, step, 0)
    out[:, HALF:WIDE] = meta[...]


def transform_kernel(core, mine, others, gidx, meta, first, tcos, tsin, second, spec, out, high, low, grid):
    transform(core, mine, others, first, tcos, tsin, second, spec, high, low, grid)
    pick(spec, gidx, meta, out)


def rho_spectrum(core, mine, others, gidx, meta, constants):
    return pl.pallas_call(
        transform_kernel,
        out_shape=[
            pltpu.VMEM((PAIRS * 64, 256), jnp.bfloat16),
            pltpu.VMEM((PAIRS, WIDE), jnp.bfloat16),
        ],
        in_specs=[SM] + [VM] * 8,
        out_specs=[VM] * 2,
        scratch_shapes=[pltpu.VMEM((PAIRS * NA, 2 * NB), jnp.bfloat16)] * 2
        + [pltpu.VMEM((2, 8, 8 * 24, LANES), jnp.float32)],
        compiler_params=PARAMS,
        name="rho_spectrum",
    )(core, mine, others, gidx, meta, *constants)


def rho_pick(spec, gidx, meta):
    return pl.pallas_call(
        pick,
        out_shape=pltpu.VMEM((PAIRS, WIDE), jnp.bfloat16),
        in_specs=[VM] * 3,
        out_specs=VM,
        compiler_params=PARAMS,
        name="rho_pick",
    )(spec, gidx, meta)


def device_index(x, y, z, c):
    return (z * 4 + (y >> 1) * 2 + c) * 8 + (y & 1) * 4 + x


CHIPS = tuple(itertools.product(range(4), repeat=3))


@functools.cache
def offset_pairs(offset):
    return tuple(
        (device_index(*chip, c), device_index(*((a + (1 - 2 * c) * b) % 4 for a, b in zip(chip, offset)), c))
        for chip in CHIPS for c in range(2)
    )


@functools.cache
def core_pairs():
    return tuple((device_index(*chip, c), device_index(*chip, 1 - c)) for chip in CHIPS for c in range(2))


def send(a, pairs):
    return lax.ppermute(a, ("ga", "ba"), pairs)


def level(a, offsets):
    return [a] + [send(a, offset_pairs(offset)) for offset in offsets[1:]]


def join_kernel(n, *refs):
    out = refs[-1]
    row = 0
    for ref in refs[:n]:
        out[row : row + ref.shape[0], :] = ref[...]
        row += ref.shape[0]


def join(blocks):
    rows = sum(b.shape[0] for b in blocks)
    return pl.pallas_call(
        functools.partial(join_kernel, len(blocks)),
        out_shape=pltpu.VMEM((rows, WIDE), jnp.bfloat16),
        in_specs=[VM] * len(blocks),
        out_specs=VM,
        compiler_params=PARAMS,
        name="join",
    )(*blocks)


def deal_kernel(b0, b1, b2, b3, out0, out1):
    for i, ref in enumerate((b0, b1, b2, b3)):
        out0[i * 64 : i * 64 + 64, :] = ref[0:64, :]
        out1[i * 64 : i * 64 + 64, :] = ref[64:128, :]


def deal(blocks):
    return pl.pallas_call(
        deal_kernel,
        out_shape=[pltpu.VMEM((256, WIDE), jnp.bfloat16)] * 2,
        in_specs=[VM] * 4,
        out_specs=[VM] * 2,
        compiler_params=PARAMS,
        name="deal",
    )(*blocks)


def halves(refs):
    return [ref.at[pl.ds(at, 256)] for ref in refs for at in range(0, ref.shape[0], 256)]


def place_of(half, step):
    return [
        tuple(sum(v) % 4 for v in zip(NEAR[2 * half + i], EVEN[j], STEP[step]))
        for j in range(4) for i in range(2)
    ]


def mirrored(half, step):
    places = place_of(half, step)
    return [places.index(tuple(-v % 4 for v in p)) for p in places]


def weighted_kernel(place, omega, *refs):
    pieces, left = halves(refs[:-2]), refs[-1]
    w2 = omega[0] * omega[0]
    row = lax.broadcasted_iota(jnp.int32, (LANES, 2 * LANES), 0)
    lane = lax.broadcasted_iota(jnp.int32, (LANES, 2 * LANES), 1)
    spread = jnp.where((row < 3) & (lane < LANES) | (row == 3) & (lane >= LANES), 1.0, 0.0)
    spread = spread.astype(jnp.bfloat16)
    for i, piece in enumerate(pieces):
        m = jnp.dot(piece[:, HALF:WIDE], spread, preferred_element_type=jnp.float32)
        delta, taken = m[:, :LANES], m[:, LANES:]
        weight = (-4.0 / math.sqrt(NV * NC)) * taken * delta / (delta * delta + w2)
        for e in range(3):
            cols = pl.ds(pl.multiple_of(place[0] * ROWS + e * LANES, LANES), LANES)
            left[i * 256 : i * 256 + 256, e * LANES : (e + 1) * LANES] = (
                piece[:, cols].astype(jnp.float32) * weight
            ).astype(jnp.bfloat16)


def weighted(place, omega, pieces, tie):
    return pl.pallas_call(
        weighted_kernel,
        out_shape=pltpu.VMEM((sum(p.shape[0] for p in pieces), ROWS), jnp.bfloat16),
        in_specs=[SM, SM] + [VM] * (len(pieces) + 1),
        out_specs=VM,
        compiler_params=PARAMS,
        name="weighted",
    )(place, omega, *pieces, tie)


def product(names, other, left, pieces, cols):
    total = None
    for i, (half, step) in enumerate(names):
        if other:
            rows = []
            for j in mirrored(half, step):
                at = i * 256 + j * BLOCK
                rows += [left[at + PAIRS : at + BLOCK, :], left[at : at + PAIRS, :]]
            mine = jnp.concatenate(rows, 0)
        else:
            mine = left[i * 256 : i * 256 + 256, :]
        term = lax.dot_general(
            mine, pieces[i][:, cols], (((0,), (0,)), ((), ())), preferred_element_type=jnp.float32
        )
        total = term if total is None else total + term
    return total


def chunk(i, width=CHUNK, start=0):
    return pl.ds(pl.multiple_of(start + i * width, LANES), width)


def cost(names, columns):
    return pl.CostEstimate(
        flops=2 * ROWS * columns * 256 * len(names),
        bytes_accessed=(2 * 256 * len(names) + 8 * ROWS) * columns,
        transcendentals=0,
    )


def partial_kernel(names, n, other, left, *refs):
    pieces, before = halves(refs[:n]), refs[n:-3]
    out, after = refs[-2:]
    after[...] = jnp.zeros_like(after)

    def step(i, carry):
        total = product(names, other, left, pieces, chunk(i))
        out[:, chunk(i)] = total + before[0][:, chunk(i)] if before else total
        return carry

    lax.fori_loop(0, HALF // CHUNK, step, 0)


TIE = jax.ShapeDtypeStruct((8, LANES), jnp.float32)


def partial_rows(names, other, left, pieces, before, tie):
    before = [] if before is None else [before]
    return pl.pallas_call(
        functools.partial(partial_kernel, names, len(pieces), other),
        out_shape=[pltpu.VMEM((ROWS, HALF), jnp.float32), TIE],
        in_specs=[VM] * (2 + len(pieces) + len(before)),
        out_specs=[VM] * 2,
        input_output_aliases={1 + len(pieces): 0} if before else {},
        compiler_params=PARAMS,
        cost_estimate=cost(names, HALF),
        name="partial_other" if other else "partial_own",
    )(left, *pieces, *before, tie)


def own_kernel(names, n, start, core, left, *refs):
    pieces = halves(refs[:n])
    before, _, out, tie, wide, sem = refs[n:]
    tie[...] = jnp.zeros_like(tie)
    copies = []
    for i in range(2):
        cols = slice(start + i * CHUNK, start + (i + 1) * CHUNK)
        wide[:, i * CHUNK : (i + 1) * CHUNK] = product(names, False, left, pieces, cols) + before[:, cols]
        for j in (2 * i, 2 * i + 1):
            block = (start // ROWS + j) * 2 + core[0]
            copies.append(
                pltpu.make_async_copy(
                    wide.at[:, pl.ds(j * ROWS, ROWS)],
                    out.at[:, pl.ds(pl.multiple_of(block * ROWS, LANES), ROWS)],
                    sem.at[j],
                )
            )
            copies[-1].start()
    for copy in copies:
        copy.wait()


def own_rows(names, start, core, left, pieces, before, after):
    grows = after.shape == (ROWS, NG)
    return pl.pallas_call(
        functools.partial(own_kernel, names, len(pieces), start),
        out_shape=[jax.ShapeDtypeStruct((ROWS, NG), jnp.float32), TIE],
        in_specs=[SM, VM] + [VM] * (len(pieces) + 1) + [HBM if grows else VM],
        out_specs=[HBM, VM],
        scratch_shapes=[pltpu.VMEM((ROWS, HALF // 2), jnp.float32), pltpu.SemaphoreType.DMA((4,))],
        input_output_aliases={3 + len(pieces): 0} if grows else {},
        compiler_params=PARAMS,
        cost_estimate=cost(names, HALF // 2),
        name="own_rows",
    )(core, left, *pieces, before, after)


def other_kernel(names, n, start, left, *refs):
    pieces = halves(refs[:n])
    before, _, out = refs[n:]

    def step(i, carry):
        total = product(names, True, left, pieces, chunk(i, start=start)) + before[:, chunk(i, start=start)]
        out[:, chunk(i)] = total.astype(jnp.bfloat16)
        return carry

    lax.fori_loop(0, 2, step, 0)


def other_rows(names, start, left, pieces, before, tie):
    return pl.pallas_call(
        functools.partial(other_kernel, names, len(pieces), start),
        out_shape=pltpu.VMEM((ROWS, HALF // 2), jnp.bfloat16),
        in_specs=[VM] * (len(pieces) + 3),
        out_specs=VM,
        compiler_params=PARAMS,
        cost_estimate=cost(names, HALF // 2),
        name="other_rows",
    )(left, *pieces, before, tie)


def finish_kernel(core, r0, r1, _, out, wide, sem):
    def copy(i):
        return pltpu.make_async_copy(
            wide.at[:, pl.ds(i * ROWS, ROWS)],
            out.at[:, pl.ds(pl.multiple_of((i * 2 + 1 - core[0]) * ROWS, LANES), ROWS)],
            sem.at[i],
        )

    for i in range(8):
        src = (r0, r1)[i // 4]
        wide[:, i * ROWS : (i + 1) * ROWS] = src[:, (i % 4) * ROWS : (i % 4 + 1) * ROWS].astype(jnp.float32)
        copy(i).start()
    for i in range(8):
        copy(i).wait()


def finish(core, rows, out):
    return pl.pallas_call(
        finish_kernel,
        out_shape=jax.ShapeDtypeStruct((ROWS, NG), jnp.float32),
        in_specs=[SM, VM, VM, HBM],
        out_specs=HBM,
        scratch_shapes=[pltpu.VMEM((ROWS, HALF), jnp.float32), pltpu.SemaphoreType.DMA((8,))],
        input_output_aliases={3: 0},
        compiler_params=PARAMS,
        name="finish",
    )(core, *rows, out)


def in_vmem(a):
    return pltpu.with_memory_space_constraint(a, pltpu.VMEM)


def on_device(psi_val, psi_con, e_val, e_con, occ, omega, g_index):
    ga = lax.axis_index("ga")
    ba = lax.axis_index("ba")
    core = lax.rem(ga, 2).astype(jnp.int32)
    kinds = [[2 * i + c for i in range(8)] for c in range(2)]
    rows, *constants = payload(psi_val, psi_con)
    psi = lax.all_to_all(rows, "ga", 0, 0, tiled=True, axis_index_groups=kinds)
    psi_other = send(psi, core_pairs())

    delta = (lax.dynamic_slice(e_con, (ga * 4,), (4,))[None, :] - e_val[:, None]).reshape(PAIRS)
    taken = jnp.broadcast_to(occ.astype(jnp.float32)[:, None], (4, 4)).reshape(PAIRS)
    d1 = lax.reduce_precision(delta, 8, 7)
    d2 = lax.reduce_precision(delta - d1, 8, 7)
    d3 = delta - d1 - d2
    meta = jnp.stack([d1, d2, d3, taken], 1).astype(jnp.bfloat16)
    meta = jnp.pad(meta, ((0, 0), (0, LANES - 4)))

    kinds_of_rows = g_index.reshape(8, 2, ROWS).transpose(1, 0, 2).reshape(2, HALF)
    kept = lax.dynamic_slice(kinds_of_rows, (core, 0), (1, HALF))
    given = lax.dynamic_slice(kinds_of_rows, (1 - core, 0), (1, HALF))
    spec, give = rho_spectrum(core.reshape(1), psi, psi_other, given, meta, constants)
    swapped = send(give, core_pairs())
    keep = rho_pick(spec, kept, meta)

    a = join(level(join([keep, swapped]), NEAR))
    sources = deal(level(a, EVEN))
    got = {(h, 0): m for h, m in enumerate(sources)}
    for h in range(2):
        for s in (1, 2):
            got[h, s] = send(sources[h], offset_pairs(STEP[s]))
    got["z"] = send(join(sources), offset_pairs(STEP[3]))

    place = lax.div(ga, 2).astype(jnp.int32).reshape(1)
    mine_omega = lax.dynamic_slice(omega, (ba,), (1,))
    core = core.reshape(1)
    own = other = None
    tie = jnp.zeros(TIE.shape, TIE.dtype)
    groups = (((0, 0), (1, 0)), ((0, 1), (0, 2)), ((0, 3), (1, 3)), ((1, 1), (1, 2)))
    for names in groups:
        pieces = [in_vmem(got[name]) for name in (("z",) if (0, 3) in names else names)]
        left = weighted(place, mine_omega, pieces, tie)
        mirror = send(left, core_pairs())
        if names is not groups[-1]:
            own, tie = partial_rows(names, False, left, pieces, own, tie)
            other, tie = partial_rows(names, True, mirror, pieces, other, tie)
    out, tie = own_rows(names, 0, core, left, pieces, own, tie)
    rows = [send(other_rows(names, s, mirror, pieces, other, tie), core_pairs()) for s in (0, HALF // 2)]
    out, _ = own_rows(names, HALF // 2, core, left, pieces, own, out)
    return finish(core, rows, out)[None]


def solution(mesh):
    placed = (P("ba", "ga"), P(None, "ga"), P("ba"), P(), P("ba"), P(), P())
    return jax.shard_map(
        on_device, mesh=mesh, in_specs=placed, out_specs=P("ba", "ga", None), check_vma=False
    )
```

```python
import functools
import itertools
import math

import jax
import jax.numpy as jnp
import numpy as np
from jax import lax
from jax.experimental import pallas as pl
from jax.experimental.pallas import tpu as pltpu
from jax.sharding import PartitionSpec as P

NV = 32
NC = 64
N = 32768
NA = 128
NB = 256
NG = 6144
HALF = NG // 2
ROWS = 384
LANES = 128
PAIRS = 16
WIDE = HALF + LANES
BLOCK = 2 * PAIRS
CHUNK = 768
MIB = 1024 * 1024
VM = pl.BlockSpec(memory_space=pltpu.VMEM)
SM = pl.BlockSpec(memory_space=pltpu.SMEM)
HBM = pl.BlockSpec(memory_space=pltpu.HBM)
PARAMS = pltpu.CompilerParams(vmem_limit_bytes=14 * MIB)

NEAR = ((0, 0, 0), (2, 2, 2), (1, 1, 1), (3, 3, 3))
EVEN = ((0, 0, 0), (2, 0, 0), (0, 2, 0), (0, 0, 2))
STEP = ((0, 0, 0), (1, 0, 0), (0, 1, 0), (0, 0, 1))


def split_bf16(a):
    hi = a.astype(np.float32).astype(jnp.bfloat16)
    lo = (a - hi.astype(np.float64)).astype(np.float32).astype(jnp.bfloat16)
    return hi, lo


def dft_constants():
    k1 = np.arange(NA)[:, None]
    a, kind, chip = np.arange(8)[:, None, None], np.arange(2)[:, None], np.arange(8)
    first = []
    for core in range(2):
        order = ((chip * 2 + (kind + core) % 2) * 8 + a).reshape(NA)
        ang = 2.0 * math.pi * ((k1 * order[None, :]) % NA) / NA
        fh, fl = split_bf16(np.concatenate([np.cos(ang), np.sin(ang)], 0))
        first.append(np.concatenate([fh, fl], 1))
    tw = 2.0 * math.pi * ((k1 * np.arange(NB)[None, :]) % N) / N
    norm = math.sqrt(2.0 / N)
    tcos = (np.cos(tw) * norm).astype(np.float32)
    tsin = (np.sin(tw) * norm).astype(np.float32)
    b2 = 2.0 * math.pi * ((np.arange(NB)[:, None] * np.arange(NA)[None, :]) % NB) / NB
    sh, sl = split_bf16(np.concatenate([np.cos(b2), -np.sin(b2)], 0))
    return np.stack(first), tcos, tsin, np.concatenate([sh, sl], 1)


def payload_kernel(val, con, first, tcos, tsin, second, out, *refs):
    here, (val_here, con_here, sem) = refs[:4], refs[4:]
    pairs = [(val, val_here), (con, con_here), *zip((first, tcos, tsin, second), here)]
    copies = [pltpu.make_async_copy(src, dst, sem.at[i]) for i, (src, dst) in enumerate(pairs)]
    for copy in copies:
        copy.start()
    for copy in copies[:2]:
        copy.wait()
    v = val_here[...].astype(jnp.float32)
    values = jnp.concatenate([v[:, :1024], v[:, 1024:]], 0)
    for chip in range(8):
        c = con_here[chip * 8 : chip * 8 + 8, :].astype(jnp.float32)
        rows = jnp.concatenate([c[:, :1024], c[:, 1024:], values], 0)
        out[chip] = rows.astype(jnp.bfloat16)
    for copy in copies[2:]:
        copy.wait()


def payload(val, con):
    constants = [jnp.asarray(c) for c in dft_constants()]
    operands = [pltpu.with_memory_space_constraint(a, pltpu.HBM) for a in (val, con, *constants)]
    return pl.pallas_call(
        payload_kernel,
        out_shape=[pltpu.VMEM((8, 24, 1024), jnp.bfloat16)]
        + [pltpu.VMEM(c.shape, c.dtype) for c in constants],
        in_specs=[HBM] * 6,
        out_specs=[VM] * 5,
        scratch_shapes=[
            pltpu.VMEM(val.shape, val.dtype),
            pltpu.VMEM(con.shape, con.dtype),
            pltpu.SemaphoreType.DMA((6,)),
        ],
        compiler_params=PARAMS,
        name="payload",
    )(*operands)


def transform(core, mine, others, first, tcos, tsin, second, spec, high, low, grid):
    for kind, ref in enumerate((mine, others)):
        for chip in range(8):
            for j in range(8):
                grid[kind, j, chip * 24 : chip * 24 + 24, :] = ref[
                    chip, :, j * LANES : (j + 1) * LANES
                ].astype(jnp.float32)

    def band(row, apart):
        parts = []
        for half in range(2):
            at = pl.ds(row + half * apart, 8, stride=24)
            for a in range(4):
                for kind in range(2):
                    parts.append(jnp.concatenate([grid[kind, 2 * a + j, at, :] for j in range(2)], 1))
        return jnp.concatenate(parts, 0)

    con = [band(core[0] * 4 + i, 8) for i in range(4)]
    ca = tcos[...]
    sa = tsin[...]
    f = first[core[0]]
    for v in range(4):
        val = band(16 + v, 4)
        for c in range(4):
            d = (val * con[c]).astype(jnp.bfloat16)
            y = jnp.dot(f, jnp.concatenate([d, d], 0), preferred_element_type=jnp.float32)
            a, b = y[:NA], y[NA:]
            uv = jnp.concatenate([a * ca - b * sa, a * sa + b * ca], 1)
            hi = uv.astype(jnp.bfloat16)
            at = slice((v * 4 + c) * NA, (v * 4 + c + 1) * NA)
            high[at, :] = hi
            low[at, :] = (uv - hi.astype(jnp.float32)).astype(jnp.bfloat16)
    for n in range(4):
        at = slice(n * 512, n * 512 + 512)
        y = jnp.dot(high[at, :], second[...], preferred_element_type=jnp.float32)
        z = jnp.dot(low[at, :], second[:, :NA], preferred_element_type=jnp.float32)
        x = (y[:, :NA] + (y[:, NA:] + z)).astype(jnp.bfloat16)
        for i in range(4):
            p = n * 4 + i
            spec[p * 64 : p * 64 + 64, 0:128] = x[i * NA : i * NA + 64]
            spec[p * 64 : p * 64 + 64, 128:256] = x[i * NA + 64 : i * NA + NA]


def pick(spec, gidx, meta, out):
    width = 1024

    def step(i, carry):
        at = pl.ds(pl.multiple_of(i * width, width), width)
        g = gidx[:, at]
        k1 = lax.bitwise_and(g, 127)
        kk = lax.shift_right_logical(k1, 6) * 128 + lax.shift_right_logical(g, 7)
        hot = jnp.where(
            lax.broadcasted_iota(jnp.int32, (256, width), 0) == kk, 1.0, 0.0
        ).astype(jnp.bfloat16)
        o = jnp.dot(spec[...], hot, preferred_element_type=jnp.float32)
        m = lax.broadcasted_iota(jnp.int32, (64, width), 0) == lax.bitwise_and(k1, 63)
        picked = jnp.sum(jnp.where(m[None], o.reshape(PAIRS, 64, width), 0.0), axis=1)
        out[:, at] = picked.astype(jnp.bfloat16)
        return carry

    lax.fori_loop(0, HALF // width, step, 0)
    out[:, HALF:WIDE] = meta[...]


def transform_kernel(core, mine, others, gidx, meta, first, tcos, tsin, second, spec, out, high, low, grid):
    transform(core, mine, others, first, tcos, tsin, second, spec, high, low, grid)
    pick(spec, gidx, meta, out)


def rho_spectrum(core, mine, others, gidx, meta, constants):
    return pl.pallas_call(
        transform_kernel,
        out_shape=[
            pltpu.VMEM((PAIRS * 64, 256), jnp.bfloat16),
            pltpu.VMEM((PAIRS, WIDE), jnp.bfloat16),
        ],
        in_specs=[SM] + [VM] * 8,
        out_specs=[VM] * 2,
        scratch_shapes=[pltpu.VMEM((PAIRS * NA, 2 * NB), jnp.bfloat16)] * 2
        + [pltpu.VMEM((2, 8, 8 * 24, LANES), jnp.float32)],
        compiler_params=PARAMS,
        name="rho_spectrum",
    )(core, mine, others, gidx, meta, *constants)


def rho_pick(spec, gidx, meta):
    return pl.pallas_call(
        pick,
        out_shape=pltpu.VMEM((PAIRS, WIDE), jnp.bfloat16),
        in_specs=[VM] * 3,
        out_specs=VM,
        compiler_params=PARAMS,
        name="rho_pick",
    )(spec, gidx, meta)


def device_index(x, y, z, c):
    return (z * 4 + (y >> 1) * 2 + c) * 8 + (y & 1) * 4 + x


CHIPS = tuple(itertools.product(range(4), repeat=3))


@functools.cache
def offset_pairs(offset):
    return tuple(
        (device_index(*chip, c), device_index(*((a + (1 - 2 * c) * b) % 4 for a, b in zip(chip, offset)), c))
        for chip in CHIPS for c in range(2)
    )


@functools.cache
def core_pairs():
    return tuple((device_index(*chip, c), device_index(*chip, 1 - c)) for chip in CHIPS for c in range(2))


def send(a, pairs):
    return lax.ppermute(a, ("ga", "ba"), pairs)


def level(a, offsets):
    return [a] + [send(a, offset_pairs(offset)) for offset in offsets[1:]]


def join_kernel(n, *refs):
    out = refs[-1]
    row = 0
    for ref in refs[:n]:
        out[row : row + ref.shape[0], :] = ref[...]
        row += ref.shape[0]


def join(blocks):
    rows = sum(b.shape[0] for b in blocks)
    return pl.pallas_call(
        functools.partial(join_kernel, len(blocks)),
        out_shape=pltpu.VMEM((rows, WIDE), jnp.bfloat16),
        in_specs=[VM] * len(blocks),
        out_specs=VM,
        compiler_params=PARAMS,
        name="join",
    )(*blocks)


def deal_kernel(b0, b1, b2, b3, out0, out1):
    for i, ref in enumerate((b0, b1, b2, b3)):
        out0[i * 64 : i * 64 + 64, :] = ref[0:64, :]
        out1[i * 64 : i * 64 + 64, :] = ref[64:128, :]


def deal(blocks):
    return pl.pallas_call(
        deal_kernel,
        out_shape=[pltpu.VMEM((256, WIDE), jnp.bfloat16)] * 2,
        in_specs=[VM] * 4,
        out_specs=[VM] * 2,
        compiler_params=PARAMS,
        name="deal",
    )(*blocks)


def halves(refs):
    return [ref.at[pl.ds(at, 256)] for ref in refs for at in range(0, ref.shape[0], 256)]


def place_of(half, step):
    return [
        tuple(sum(v) % 4 for v in zip(NEAR[2 * half + i], EVEN[j], STEP[step]))
        for j in range(4) for i in range(2)
    ]


def mirrored(half, step):
    places = place_of(half, step)
    return [places.index(tuple(-v % 4 for v in p)) for p in places]


def weighted_kernel(n, place, omega, *refs):
    pieces, left = halves(refs[:n]), refs[n + 1]
    if len(refs) > n + 2:
        refs[-1][...] = pieces[0][:, :HALF]
    w2 = omega[0] * omega[0]
    row = lax.broadcasted_iota(jnp.int32, (LANES, 2 * LANES), 0)
    lane = lax.broadcasted_iota(jnp.int32, (LANES, 2 * LANES), 1)
    spread = jnp.where((row < 3) & (lane < LANES) | (row == 3) & (lane >= LANES), 1.0, 0.0)
    spread = spread.astype(jnp.bfloat16)
    for i, piece in enumerate(pieces):
        m = jnp.dot(piece[:, HALF:WIDE], spread, preferred_element_type=jnp.float32)
        delta, taken = m[:, :LANES], m[:, LANES:]
        weight = (-4.0 / math.sqrt(NV * NC)) * taken * delta / (delta * delta + w2)
        for e in range(3):
            cols = pl.ds(pl.multiple_of(place[0] * ROWS + e * LANES, LANES), LANES)
            left[i * 256 : i * 256 + 256, e * LANES : (e + 1) * LANES] = (
                piece[:, cols].astype(jnp.float32) * weight
            ).astype(jnp.bfloat16)


def weighted(place, omega, pieces, tie, copied=False):
    shapes = [pltpu.VMEM((sum(p.shape[0] for p in pieces), ROWS), jnp.bfloat16)]
    if copied:
        shapes.append(pltpu.VMEM((pieces[0].shape[0], HALF), jnp.bfloat16))
    return pl.pallas_call(
        functools.partial(weighted_kernel, len(pieces)),
        out_shape=shapes,
        in_specs=[SM, SM] + [VM] * (len(pieces) + 1),
        out_specs=[VM] * len(shapes),
        compiler_params=PARAMS,
        name="weighted",
    )(place, omega, *pieces, tie)


def product(names, other, left, pieces, cols):
    total = None
    for i, (half, step) in enumerate(names):
        if other:
            rows = []
            for j in mirrored(half, step):
                at = i * 256 + j * BLOCK
                rows += [left[at + PAIRS : at + BLOCK, :], left[at : at + PAIRS, :]]
            mine = jnp.concatenate(rows, 0)
        else:
            mine = left[i * 256 : i * 256 + 256, :]
        term = lax.dot_general(
            mine, pieces[i][:, cols], (((0,), (0,)), ((), ())), preferred_element_type=jnp.float32
        )
        total = term if total is None else total + term
    return total


def chunk(i, width=CHUNK, start=0):
    return pl.ds(pl.multiple_of(start + i * width, LANES), width)


def cost(names, columns):
    return pl.CostEstimate(
        flops=2 * ROWS * columns * 256 * len(names),
        bytes_accessed=(2 * 256 * len(names) + 8 * ROWS) * columns,
        transcendentals=0,
    )


def partial_kernel(names, n, other, left, *refs):
    pieces, before = halves(refs[:n]), refs[n:-3]
    out, after = refs[-2:]
    after[...] = jnp.zeros_like(after)

    def step(i, carry):
        total = product(names, other, left, pieces, chunk(i))
        out[:, chunk(i)] = total + before[0][:, chunk(i)] if before else total
        return carry

    lax.fori_loop(0, HALF // CHUNK, step, 0)


TIE = jax.ShapeDtypeStruct((8, LANES), jnp.float32)


def partial_rows(names, other, left, pieces, before, tie):
    before = [] if before is None else [before]
    return pl.pallas_call(
        functools.partial(partial_kernel, names, len(pieces), other),
        out_shape=[pltpu.VMEM((ROWS, HALF), jnp.float32), TIE],
        in_specs=[VM] * (2 + len(pieces) + len(before)),
        out_specs=[VM] * 2,
        input_output_aliases={1 + len(pieces): 0} if before else {},
        compiler_params=PARAMS,
        cost_estimate=cost(names, HALF),
        name="partial_other" if other else "partial_own",
    )(left, *pieces, *before, tie)


def last_kernel(names, other, core, left, piece, *refs):
    n = 2 if other else 1
    before = refs[:n]
    out, wide, sem = refs[-3:]
    half = 1 - core[0] if other else core[0]
    copies = []
    for i in range(4):
        cols = slice(i * CHUNK, (i + 1) * CHUNK)
        if other:
            sofar = before[i // 2][:, (i % 2) * CHUNK : (i % 2 + 1) * CHUNK].astype(jnp.float32)
        else:
            sofar = before[0][:, cols]
        wide[:, cols] = product(names, other, left, [piece], cols) + sofar
        for j in (2 * i, 2 * i + 1):
            copies.append(
                pltpu.make_async_copy(
                    wide.at[:, pl.ds(j * ROWS, ROWS)],
                    out.at[:, pl.ds(pl.multiple_of((j * 2 + half) * ROWS, LANES), ROWS)],
                    sem.at[j],
                )
            )
            copies[-1].start()
    for copy in copies:
        copy.wait()


def last_rows(names, other, core, left, piece, before, out):
    out = [] if out is None else [out]
    return pl.pallas_call(
        functools.partial(last_kernel, names, other),
        out_shape=jax.ShapeDtypeStruct((ROWS, NG), jnp.float32),
        in_specs=[SM, VM, VM] + [VM] * len(before) + [HBM] * len(out),
        out_specs=HBM,
        scratch_shapes=[pltpu.VMEM((ROWS, HALF), jnp.float32), pltpu.SemaphoreType.DMA((8,))],
        input_output_aliases={3 + len(before): 0} if out else {},
        compiler_params=PARAMS,
        cost_estimate=cost(names, HALF),
        name="last_other" if other else "last_own",
    )(core, left, piece, *before, *out)


def other_kernel(names, n, start, left, *refs):
    pieces = halves(refs[:n])
    before, _, out = refs[n:]

    def step(i, carry):
        total = product(names, True, left, pieces, chunk(i, start=start)) + before[:, chunk(i, start=start)]
        out[:, chunk(i)] = total.astype(jnp.bfloat16)
        return carry

    lax.fori_loop(0, 2, step, 0)


def other_rows(names, start, left, pieces, before, tie):
    return pl.pallas_call(
        functools.partial(other_kernel, names, len(pieces), start),
        out_shape=pltpu.VMEM((ROWS, HALF // 2), jnp.bfloat16),
        in_specs=[VM] * (len(pieces) + 3),
        out_specs=VM,
        compiler_params=PARAMS,
        cost_estimate=cost(names, HALF // 2),
        name="other_rows",
    )(left, *pieces, before, tie)


def in_vmem(a):
    return pltpu.with_memory_space_constraint(a, pltpu.VMEM)


def on_device(psi_val, psi_con, e_val, e_con, occ, omega, g_index):
    ga = lax.axis_index("ga")
    ba = lax.axis_index("ba")
    core = lax.rem(ga, 2).astype(jnp.int32)
    kinds = [[2 * i + c for i in range(8)] for c in range(2)]
    rows, *constants = payload(psi_val, psi_con)
    psi = lax.all_to_all(rows, "ga", 0, 0, tiled=True, axis_index_groups=kinds)
    psi_other = send(psi, core_pairs())

    delta = (lax.dynamic_slice(e_con, (ga * 4,), (4,))[None, :] - e_val[:, None]).reshape(PAIRS)
    taken = jnp.broadcast_to(occ.astype(jnp.float32)[:, None], (4, 4)).reshape(PAIRS)
    d1 = lax.reduce_precision(delta, 8, 7)
    d2 = lax.reduce_precision(delta - d1, 8, 7)
    d3 = delta - d1 - d2
    meta = jnp.stack([d1, d2, d3, taken], 1).astype(jnp.bfloat16)
    meta = jnp.pad(meta, ((0, 0), (0, LANES - 4)))

    kinds_of_rows = g_index.reshape(8, 2, ROWS).transpose(1, 0, 2).reshape(2, HALF)
    kept = lax.dynamic_slice(kinds_of_rows, (core, 0), (1, HALF))
    given = lax.dynamic_slice(kinds_of_rows, (1 - core, 0), (1, HALF))
    spec, give = rho_spectrum(core.reshape(1), psi, psi_other, given, meta, constants)
    swapped = send(give, core_pairs())
    keep = rho_pick(spec, kept, meta)

    a = join(level(join([keep, swapped]), NEAR))
    sources = deal(level(a, EVEN))
    got = {(h, 0): m for h, m in enumerate(sources)}
    for h in range(2):
        for s in (1, 2, 3):
            got[h, s] = send(sources[h], offset_pairs(STEP[s]))

    place = lax.div(ga, 2).astype(jnp.int32).reshape(1)
    mine_omega = lax.dynamic_slice(omega, (ba,), (1,))
    core = core.reshape(1)
    own = other = None
    tie = jnp.zeros(TIE.shape, TIE.dtype)
    groups = (((0, 0), (1, 0), (0, 1), (0, 2), (0, 3)), ((1, 1), (1, 2)))
    for names in groups:
        pieces = [in_vmem(got[name]) for name in names]
        (left,) = weighted(place, mine_omega, pieces, tie)
        mirror = send(left, core_pairs())
        own, tie = partial_rows(names, False, left, pieces, own, tie)
        if names is groups[0]:
            other, tie = partial_rows(names, True, mirror, pieces, other, tie)
    rows = []
    for s in (0, HALF // 2):
        rows.append(other_rows(names, s, mirror, pieces, other, rows[0] if rows else tie))
    swapped = [send(row, core_pairs()) for row in rows]

    names = ((1, 3),)
    piece = got[1, 3]
    left, copy = weighted(place, mine_omega, [piece], rows[1], True)
    theirs = send(copy, core_pairs())
    out = last_rows(names, False, core, left, piece, [own], None)
    return last_rows(names, True, core, left, theirs, swapped, out)[None]


def solution(mesh):
    placed = (P("ba", "ga"), P(None, "ga"), P("ba"), P(), P("ba"), P(), P())
    return jax.shard_map(
        on_device, mesh=mesh, in_specs=placed, out_specs=P("ba", "ga", None), check_vma=False
    )
```

```python
import functools
import itertools
import math

import jax
import jax.numpy as jnp
import numpy as np
from jax import lax
from jax.experimental import pallas as pl
from jax.experimental.pallas import tpu as pltpu
from jax.sharding import PartitionSpec as P

NV = 32
NC = 64
N = 32768
NA = 128
NB = 256
NG = 6144
HALF = NG // 2
ROWS = 384
LANES = 128
PAIRS = 16
WIDE = HALF + LANES
BLOCK = 2 * PAIRS
CHUNK = 768
MIB = 1024 * 1024
VM = pl.BlockSpec(memory_space=pltpu.VMEM)
SM = pl.BlockSpec(memory_space=pltpu.SMEM)
HBM = pl.BlockSpec(memory_space=pltpu.HBM)
PARAMS = pltpu.CompilerParams(vmem_limit_bytes=14 * MIB)

NEAR = ((0, 0, 0), (2, 2, 2), (1, 1, 1), (3, 3, 3))
EVEN = ((0, 0, 0), (2, 0, 0), (0, 2, 0), (0, 0, 2))
STEP = ((0, 0, 0), (1, 0, 0), (0, 1, 0), (0, 0, 1))


def split_bf16(a):
    hi = a.astype(np.float32).astype(jnp.bfloat16)
    lo = (a - hi.astype(np.float64)).astype(np.float32).astype(jnp.bfloat16)
    return hi, lo


def dft_constants():
    k1 = np.arange(NA)[:, None]
    a, kind, chip = np.arange(8)[:, None, None], np.arange(2)[:, None], np.arange(8)
    first = []
    for core in range(2):
        order = ((chip * 2 + (kind + core) % 2) * 8 + a).reshape(NA)
        ang = 2.0 * math.pi * ((k1 * order[None, :]) % NA) / NA
        fh, fl = split_bf16(np.concatenate([np.cos(ang), np.sin(ang)], 0))
        first.append(np.concatenate([fh, fl], 1))
    tw = 2.0 * math.pi * ((k1 * np.arange(NB)[None, :]) % N) / N
    norm = math.sqrt(2.0 / N)
    tcos = (np.cos(tw) * norm).astype(np.float32)
    tsin = (np.sin(tw) * norm).astype(np.float32)
    b2 = 2.0 * math.pi * ((np.arange(NB)[:, None] * np.arange(NA)[None, :]) % NB) / NB
    sh, sl = split_bf16(np.concatenate([np.cos(b2), -np.sin(b2)], 0))
    return np.stack(first), tcos, tsin, np.concatenate([sh, sl], 1)


def payload_kernel(val, con, first, tcos, tsin, second, out, *refs):
    here, (val_here, con_here, sem) = refs[:4], refs[4:]
    pairs = [(val, val_here), (con, con_here), *zip((first, tcos, tsin, second), here)]
    copies = [pltpu.make_async_copy(src, dst, sem.at[i]) for i, (src, dst) in enumerate(pairs)]
    for copy in copies:
        copy.start()
    for copy in copies[:2]:
        copy.wait()
    v = val_here[...].astype(jnp.float32)
    values = jnp.concatenate([v[:, :1024], v[:, 1024:]], 0)
    for chip in range(8):
        c = con_here[chip * 8 : chip * 8 + 8, :].astype(jnp.float32)
        rows = jnp.concatenate([c[:, :1024], c[:, 1024:], values], 0)
        out[chip] = rows.astype(jnp.bfloat16)
    for copy in copies[2:]:
        copy.wait()


def payload(val, con):
    constants = [jnp.asarray(c) for c in dft_constants()]
    operands = [pltpu.with_memory_space_constraint(a, pltpu.HBM) for a in (val, con, *constants)]
    return pl.pallas_call(
        payload_kernel,
        out_shape=[pltpu.VMEM((8, 24, 1024), jnp.bfloat16)]
        + [pltpu.VMEM(c.shape, c.dtype) for c in constants],
        in_specs=[HBM] * 6,
        out_specs=[VM] * 5,
        scratch_shapes=[
            pltpu.VMEM(val.shape, val.dtype),
            pltpu.VMEM(con.shape, con.dtype),
            pltpu.SemaphoreType.DMA((6,)),
        ],
        compiler_params=PARAMS,
        name="payload",
    )(*operands)


def transform(core, mine, others, first, tcos, tsin, second, spec, high, low, grid):
    for kind, ref in enumerate((mine, others)):
        for chip in range(8):
            for j in range(8):
                grid[kind, j, chip * 24 : chip * 24 + 24, :] = ref[
                    chip, :, j * LANES : (j + 1) * LANES
                ].astype(jnp.float32)

    def band(row, apart):
        parts = []
        for half in range(2):
            at = pl.ds(row + half * apart, 8, stride=24)
            for a in range(4):
                for kind in range(2):
                    parts.append(jnp.concatenate([grid[kind, 2 * a + j, at, :] for j in range(2)], 1))
        return jnp.concatenate(parts, 0)

    con = [band(core[0] * 4 + i, 8) for i in range(4)]
    ca = tcos[...]
    sa = tsin[...]
    f = first[core[0]]
    for v in range(4):
        val = band(16 + v, 4)
        for c in range(4):
            d = (val * con[c]).astype(jnp.bfloat16)
            y = jnp.dot(f, jnp.concatenate([d, d], 0), preferred_element_type=jnp.float32)
            a, b = y[:NA], y[NA:]
            uv = jnp.concatenate([a * ca - b * sa, a * sa + b * ca], 1)
            hi = uv.astype(jnp.bfloat16)
            at = slice((v * 4 + c) * NA, (v * 4 + c + 1) * NA)
            high[at, :] = hi
            low[at, :] = (uv - hi.astype(jnp.float32)).astype(jnp.bfloat16)
    for n in range(4):
        at = slice(n * 512, n * 512 + 512)
        y = jnp.dot(high[at, :], second[...], preferred_element_type=jnp.float32)
        z = jnp.dot(low[at, :], second[:, :NA], preferred_element_type=jnp.float32)
        x = (y[:, :NA] + (y[:, NA:] + z)).astype(jnp.bfloat16)
        for i in range(4):
            p = n * 4 + i
            spec[p * 64 : p * 64 + 64, 0:128] = x[i * NA : i * NA + 64]
            spec[p * 64 : p * 64 + 64, 128:256] = x[i * NA + 64 : i * NA + NA]


def pick(spec, gidx, meta, out):
    width = 1024

    def step(i, carry):
        at = pl.ds(pl.multiple_of(i * width, width), width)
        g = gidx[:, at]
        k1 = lax.bitwise_and(g, 127)
        kk = lax.shift_right_logical(k1, 6) * 128 + lax.shift_right_logical(g, 7)
        hot = jnp.where(
            lax.broadcasted_iota(jnp.int32, (256, width), 0) == kk, 1.0, 0.0
        ).astype(jnp.bfloat16)
        o = jnp.dot(spec[...], hot, preferred_element_type=jnp.float32)
        m = lax.broadcasted_iota(jnp.int32, (64, width), 0) == lax.bitwise_and(k1, 63)
        picked = jnp.sum(jnp.where(m[None], o.reshape(PAIRS, 64, width), 0.0), axis=1)
        out[:, at] = picked.astype(jnp.bfloat16)
        return carry

    lax.fori_loop(0, HALF // width, step, 0)
    out[:, HALF:WIDE] = meta[...]


def transform_kernel(core, mine, others, gidx, meta, first, tcos, tsin, second, spec, out, high, low, grid):
    transform(core, mine, others, first, tcos, tsin, second, spec, high, low, grid)
    pick(spec, gidx, meta, out)


def rho_spectrum(core, mine, others, gidx, meta, constants):
    return pl.pallas_call(
        transform_kernel,
        out_shape=[
            pltpu.VMEM((PAIRS * 64, 256), jnp.bfloat16),
            pltpu.VMEM((PAIRS, WIDE), jnp.bfloat16),
        ],
        in_specs=[SM] + [VM] * 8,
        out_specs=[VM] * 2,
        scratch_shapes=[pltpu.VMEM((PAIRS * NA, 2 * NB), jnp.bfloat16)] * 2
        + [pltpu.VMEM((2, 8, 8 * 24, LANES), jnp.float32)],
        compiler_params=PARAMS,
        name="rho_spectrum",
    )(core, mine, others, gidx, meta, *constants)


def rho_pick(spec, gidx, meta):
    return pl.pallas_call(
        pick,
        out_shape=pltpu.VMEM((PAIRS, WIDE), jnp.bfloat16),
        in_specs=[VM] * 3,
        out_specs=VM,
        compiler_params=PARAMS,
        name="rho_pick",
    )(spec, gidx, meta)


def device_index(x, y, z, c):
    return (z * 4 + (y >> 1) * 2 + c) * 8 + (y & 1) * 4 + x


CHIPS = tuple(itertools.product(range(4), repeat=3))


@functools.cache
def offset_pairs(offset):
    return tuple(
        (device_index(*chip, c), device_index(*((a + (1 - 2 * c) * b) % 4 for a, b in zip(chip, offset)), c))
        for chip in CHIPS for c in range(2)
    )


@functools.cache
def core_pairs():
    return tuple((device_index(*chip, c), device_index(*chip, 1 - c)) for chip in CHIPS for c in range(2))


def send(a, pairs):
    return lax.ppermute(a, ("ga", "ba"), pairs)


def level(a, offsets):
    return [a] + [send(a, offset_pairs(offset)) for offset in offsets[1:]]


def join_kernel(n, *refs):
    out = refs[n]
    row = 0
    for ref in refs[:n]:
        out[row : row + ref.shape[0], :] = ref[...]
        row += ref.shape[0]


def join(blocks):
    rows = sum(b.shape[0] for b in blocks)
    return pl.pallas_call(
        functools.partial(join_kernel, len(blocks)),
        out_shape=pltpu.VMEM((rows, WIDE), jnp.bfloat16),
        in_specs=[VM] * len(blocks),
        out_specs=VM,
        compiler_params=PARAMS,
        name="join",
    )(*blocks)


def deal_kernel(b0, b1, b2, b3, out0, out1, both):
    for i, ref in enumerate((b0, b1, b2, b3)):
        for half, out in enumerate((out0, out1)):
            rows = ref[half * 64 : half * 64 + 64, :]
            out[i * 64 : i * 64 + 64, :] = rows
            both[half * 256 + i * 64 : half * 256 + i * 64 + 64, :] = rows


def deal(blocks):
    return pl.pallas_call(
        deal_kernel,
        out_shape=[pltpu.VMEM((rows, WIDE), jnp.bfloat16) for rows in (256, 256, 512)],
        in_specs=[VM] * 4,
        out_specs=[VM] * 3,
        compiler_params=PARAMS,
        name="deal",
    )(*blocks)


def halves(refs):
    return [ref.at[pl.ds(at, 256)] for ref in refs for at in range(0, ref.shape[0], 256)]


def place_of(half, step):
    return [
        tuple(sum(v) % 4 for v in zip(NEAR[2 * half + i], EVEN[j], STEP[step]))
        for j in range(4) for i in range(2)
    ]


def mirrored(half, step):
    places = place_of(half, step)
    return [places.index(tuple(-v % 4 for v in p)) for p in places]


def weighted_kernel(place, omega, *refs):
    pieces, left = halves(refs[:-2]), refs[-1]
    w2 = omega[0] * omega[0]
    row = lax.broadcasted_iota(jnp.int32, (LANES, 2 * LANES), 0)
    lane = lax.broadcasted_iota(jnp.int32, (LANES, 2 * LANES), 1)
    spread = jnp.where((row < 3) & (lane < LANES) | (row == 3) & (lane >= LANES), 1.0, 0.0)
    spread = spread.astype(jnp.bfloat16)
    for i, piece in enumerate(pieces):
        m = jnp.dot(piece[:, HALF:WIDE], spread, preferred_element_type=jnp.float32)
        delta, taken = m[:, :LANES], m[:, LANES:]
        weight = (-4.0 / math.sqrt(NV * NC)) * taken * delta / (delta * delta + w2)
        for e in range(3):
            cols = pl.ds(pl.multiple_of(place[0] * ROWS + e * LANES, LANES), LANES)
            left[i * 256 : i * 256 + 256, e * LANES : (e + 1) * LANES] = (
                piece[:, cols].astype(jnp.float32) * weight
            ).astype(jnp.bfloat16)


def weighted(place, omega, pieces, tie):
    return pl.pallas_call(
        weighted_kernel,
        out_shape=pltpu.VMEM((sum(p.shape[0] for p in pieces), ROWS), jnp.bfloat16),
        in_specs=[SM, SM] + [VM] * (len(pieces) + 1),
        out_specs=VM,
        compiler_params=PARAMS,
        name="weighted",
    )(place, omega, *pieces, tie)


def product(names, other, left, pieces, cols):
    total = None
    for i, (half, step) in enumerate(names):
        if other:
            rows = []
            for j in mirrored(half, step):
                at = i * 256 + j * BLOCK
                rows += [left[at + PAIRS : at + BLOCK, :], left[at : at + PAIRS, :]]
            mine = jnp.concatenate(rows, 0)
        else:
            mine = left[i * 256 : i * 256 + 256, :]
        term = lax.dot_general(
            mine, pieces[i][:, cols], (((0,), (0,)), ((), ())), preferred_element_type=jnp.float32
        )
        total = term if total is None else total + term
    return total


def chunk(i, width=CHUNK, start=0):
    return pl.ds(pl.multiple_of(start + i * width, LANES), width)


def cost(names, columns):
    return pl.CostEstimate(
        flops=2 * ROWS * columns * 256 * len(names),
        bytes_accessed=(2 * 256 * len(names) + 8 * ROWS) * columns,
        transcendentals=0,
    )


def partial_kernel(names, n, other, left, *refs):
    pieces, before = halves(refs[:n]), refs[n:-3]
    out, after = refs[-2:]
    after[...] = jnp.zeros_like(after)

    def step(i, carry):
        total = product(names, other, left, pieces, chunk(i))
        out[:, chunk(i)] = total + before[0][:, chunk(i)] if before else total
        return carry

    lax.fori_loop(0, HALF // CHUNK, step, 0)


TIE = jax.ShapeDtypeStruct((8, LANES), jnp.float32)


def partial_rows(names, other, left, pieces, before, tie):
    before = [] if before is None else [before]
    return pl.pallas_call(
        functools.partial(partial_kernel, names, len(pieces), other),
        out_shape=[pltpu.VMEM((ROWS, HALF), jnp.float32), TIE],
        in_specs=[VM] * (2 + len(pieces) + len(before)),
        out_specs=[VM] * 2,
        input_output_aliases={1 + len(pieces): 0} if before else {},
        compiler_params=PARAMS,
        cost_estimate=cost(names, HALF),
        name="partial_other" if other else "partial_own",
    )(left, *pieces, *before, tie)


def own_kernel(names, n, start, core, left, *refs):
    pieces = halves(refs[:n])
    before, _, out, tie, wide, sem = refs[n:]
    tie[...] = jnp.zeros_like(tie)
    copies = []
    for i in range(2):
        cols = slice(start + i * CHUNK, start + (i + 1) * CHUNK)
        wide[:, i * CHUNK : (i + 1) * CHUNK] = product(names, False, left, pieces, cols) + before[:, cols]
        for j in (2 * i, 2 * i + 1):
            block = (start // ROWS + j) * 2 + core[0]
            copies.append(
                pltpu.make_async_copy(
                    wide.at[:, pl.ds(j * ROWS, ROWS)],
                    out.at[:, pl.ds(pl.multiple_of(block * ROWS, LANES), ROWS)],
                    sem.at[j],
                )
            )
            copies[-1].start()
    for copy in copies:
        copy.wait()


def own_rows(names, start, core, left, pieces, before, after):
    grows = after.shape == (ROWS, NG)
    return pl.pallas_call(
        functools.partial(own_kernel, names, len(pieces), start),
        out_shape=[jax.ShapeDtypeStruct((ROWS, NG), jnp.float32), TIE],
        in_specs=[SM, VM] + [VM] * (len(pieces) + 1) + [HBM if grows else VM],
        out_specs=[HBM, VM],
        scratch_shapes=[pltpu.VMEM((ROWS, HALF // 2), jnp.float32), pltpu.SemaphoreType.DMA((4,))],
        input_output_aliases={3 + len(pieces): 0} if grows else {},
        compiler_params=PARAMS,
        cost_estimate=cost(names, HALF // 2),
        name="own_rows",
    )(core, left, *pieces, before, after)


def other_kernel(names, n, start, left, *refs):
    pieces = halves(refs[:n])
    before, _, out = refs[n:]

    def step(i, carry):
        total = product(names, True, left, pieces, chunk(i, start=start)) + before[:, chunk(i, start=start)]
        out[:, chunk(i)] = total.astype(jnp.bfloat16)
        return carry

    lax.fori_loop(0, 2, step, 0)


def other_rows(names, start, left, pieces, before, tie):
    return pl.pallas_call(
        functools.partial(other_kernel, names, len(pieces), start),
        out_shape=pltpu.VMEM((ROWS, HALF // 2), jnp.bfloat16),
        in_specs=[VM] * (len(pieces) + 3),
        out_specs=VM,
        compiler_params=PARAMS,
        cost_estimate=cost(names, HALF // 2),
        name="other_rows",
    )(left, *pieces, before, tie)


def finish_kernel(core, r0, r1, _, out, wide, sem):
    def copy(i):
        return pltpu.make_async_copy(
            wide.at[:, pl.ds(i * ROWS, ROWS)],
            out.at[:, pl.ds(pl.multiple_of((i * 2 + 1 - core[0]) * ROWS, LANES), ROWS)],
            sem.at[i],
        )

    for i in range(8):
        src = (r0, r1)[i // 4]
        wide[:, i * ROWS : (i + 1) * ROWS] = src[:, (i % 4) * ROWS : (i % 4 + 1) * ROWS].astype(jnp.float32)
        copy(i).start()
    for i in range(8):
        copy(i).wait()


def finish(core, rows, out):
    return pl.pallas_call(
        finish_kernel,
        out_shape=jax.ShapeDtypeStruct((ROWS, NG), jnp.float32),
        in_specs=[SM, VM, VM, HBM],
        out_specs=HBM,
        scratch_shapes=[pltpu.VMEM((ROWS, HALF), jnp.float32), pltpu.SemaphoreType.DMA((8,))],
        input_output_aliases={3: 0},
        compiler_params=PARAMS,
        name="finish",
    )(core, *rows, out)


def in_vmem(a):
    return pltpu.with_memory_space_constraint(a, pltpu.VMEM)


def on_device(psi_val, psi_con, e_val, e_con, occ, omega, g_index):
    ga = lax.axis_index("ga")
    ba = lax.axis_index("ba")
    core = lax.rem(ga, 2).astype(jnp.int32)
    kinds = [[2 * i + c for i in range(8)] for c in range(2)]
    rows, *constants = payload(psi_val, psi_con)
    psi = lax.all_to_all(rows, "ga", 0, 0, tiled=True, axis_index_groups=kinds)
    psi_other = send(psi, core_pairs())

    delta = (lax.dynamic_slice(e_con, (ga * 4,), (4,))[None, :] - e_val[:, None]).reshape(PAIRS)
    taken = jnp.broadcast_to(occ.astype(jnp.float32)[:, None], (4, 4)).reshape(PAIRS)
    d1 = lax.reduce_precision(delta, 8, 7)
    d2 = lax.reduce_precision(delta - d1, 8, 7)
    d3 = delta - d1 - d2
    meta = jnp.stack([d1, d2, d3, taken], 1).astype(jnp.bfloat16)
    meta = jnp.pad(meta, ((0, 0), (0, LANES - 4)))

    kinds_of_rows = g_index.reshape(8, 2, ROWS).transpose(1, 0, 2).reshape(2, HALF)
    kept = lax.dynamic_slice(kinds_of_rows, (core, 0), (1, HALF))
    given = lax.dynamic_slice(kinds_of_rows, (1 - core, 0), (1, HALF))
    spec, give = rho_spectrum(core.reshape(1), psi, psi_other, given, meta, constants)
    swapped = send(give, core_pairs())
    keep = rho_pick(spec, kept, meta)

    a = join(level(join([keep, swapped]), NEAR))
    *sources, both = deal(level(a, EVEN))
    got = {(h, 0): m for h, m in enumerate(sources)}
    for h in range(2):
        for s in (1, 2):
            got[h, s] = send(sources[h], offset_pairs(STEP[s]))
    got["z"] = send(both, offset_pairs(STEP[3]))

    place = lax.div(ga, 2).astype(jnp.int32).reshape(1)
    mine_omega = lax.dynamic_slice(omega, (ba,), (1,))
    core = core.reshape(1)
    own = other = None
    tie = jnp.zeros(TIE.shape, TIE.dtype)
    groups = (((0, 0), (1, 0)), ((0, 1), (0, 2)), ((1, 1), (1, 2), (0, 3), (1, 3)))
    for names in groups:
        held = names if names is not groups[-1] else (*names[:2], "z")
        pieces = [in_vmem(got[name]) for name in held]
        left = weighted(place, mine_omega, pieces, tie)
        mirror = send(left, core_pairs())
        if names is not groups[-1]:
            own, tie = partial_rows(names, False, left, pieces, own, tie)
            other, tie = partial_rows(names, True, mirror, pieces, other, tie)
    out, tie = own_rows(names, 0, core, left, pieces, own, tie)
    rows = [send(other_rows(names, s, mirror, pieces, other, tie), core_pairs()) for s in (0, HALF // 2)]
    out, _ = own_rows(names, HALF // 2, core, left, pieces, own, out)
    return finish(core, rows, out)[None]


def solution(mesh):
    placed = (P("ba", "ga"), P(None, "ga"), P("ba"), P(), P("ba"), P(), P())
    return jax.shard_map(
        on_device, mesh=mesh, in_specs=placed, out_specs=P("ba", "ga", None), check_vma=False
    )
```

```python
import functools
import itertools
import math

import jax
import jax.numpy as jnp
import numpy as np
from jax import lax
from jax.experimental import pallas as pl
from jax.experimental.pallas import tpu as pltpu
from jax.sharding import PartitionSpec as P

NV = 32
NC = 64
N = 32768
NA = 128
NB = 256
NG = 6144
HALF = NG // 2
ROWS = 384
LANES = 128
PAIRS = 16
WIDE = HALF + LANES
BLOCK = 2 * PAIRS
CHUNK = 768
MIB = 1024 * 1024
VM = pl.BlockSpec(memory_space=pltpu.VMEM)
SM = pl.BlockSpec(memory_space=pltpu.SMEM)
HBM = pl.BlockSpec(memory_space=pltpu.HBM)
PARAMS = pltpu.CompilerParams(vmem_limit_bytes=14 * MIB)

NEAR = ((0, 0, 0), (2, 2, 2), (1, 1, 1), (3, 3, 3))
EVEN = ((0, 0, 0), (2, 0, 0), (0, 2, 0), (0, 0, 2))
STEP = ((0, 0, 0), (1, 0, 0), (0, 1, 0), (0, 0, 1))


def split_bf16(a):
    hi = a.astype(np.float32).astype(jnp.bfloat16)
    lo = (a - hi.astype(np.float64)).astype(np.float32).astype(jnp.bfloat16)
    return hi, lo


def dft_constants():
    k1 = np.arange(NA)[:, None]
    a, kind, chip = np.arange(8)[:, None, None], np.arange(2)[:, None], np.arange(8)
    first = []
    for core in range(2):
        order = ((chip * 2 + (kind + core) % 2) * 8 + a).reshape(NA)
        ang = 2.0 * math.pi * ((k1 * order[None, :]) % NA) / NA
        fh, fl = split_bf16(np.concatenate([np.cos(ang), np.sin(ang)], 0))
        first.append(np.concatenate([fh, fl], 1))
    tw = 2.0 * math.pi * ((k1 * np.arange(NB)[None, :]) % N) / N
    norm = math.sqrt(2.0 / N)
    tcos = (np.cos(tw) * norm).astype(np.float32)
    tsin = (np.sin(tw) * norm).astype(np.float32)
    b2 = 2.0 * math.pi * ((np.arange(NB)[:, None] * np.arange(NA)[None, :]) % NB) / NB
    sh, sl = split_bf16(np.concatenate([np.cos(b2), -np.sin(b2)], 0))
    return np.stack(first), tcos, tsin, np.concatenate([sh, sl], 1)


def payload_kernel(val, con, first, tcos, tsin, second, out, *refs):
    here, (val_here, con_here, sem) = refs[:4], refs[4:]
    pairs = [(val, val_here), (con, con_here), *zip((first, tcos, tsin, second), here)]
    copies = [pltpu.make_async_copy(src, dst, sem.at[i]) for i, (src, dst) in enumerate(pairs)]
    for copy in copies:
        copy.start()
    for copy in copies[:2]:
        copy.wait()
    v = val_here[...].astype(jnp.float32)
    values = jnp.concatenate([v[:, :1024], v[:, 1024:]], 0)
    for chip in range(8):
        c = con_here[chip * 8 : chip * 8 + 8, :].astype(jnp.float32)
        rows = jnp.concatenate([c[:, :1024], c[:, 1024:], values], 0)
        out[chip] = rows.astype(jnp.bfloat16)
    for copy in copies[2:]:
        copy.wait()


def payload(val, con):
    constants = [jnp.asarray(c) for c in dft_constants()]
    operands = [pltpu.with_memory_space_constraint(a, pltpu.HBM) for a in (val, con, *constants)]
    return pl.pallas_call(
        payload_kernel,
        out_shape=[pltpu.VMEM((8, 24, 1024), jnp.bfloat16)]
        + [pltpu.VMEM(c.shape, c.dtype) for c in constants],
        in_specs=[HBM] * 6,
        out_specs=[VM] * 5,
        scratch_shapes=[
            pltpu.VMEM(val.shape, val.dtype),
            pltpu.VMEM(con.shape, con.dtype),
            pltpu.SemaphoreType.DMA((6,)),
        ],
        compiler_params=PARAMS,
        name="payload",
    )(*operands)


def transform(core, mine, others, first, tcos, tsin, second, spec, high, low, grid):
    for kind, ref in enumerate((mine, others)):
        for chip in range(8):
            for j in range(8):
                grid[kind, j, chip * 24 : chip * 24 + 24, :] = ref[
                    chip, :, j * LANES : (j + 1) * LANES
                ].astype(jnp.float32)

    def band(row, apart):
        parts = []
        for half in range(2):
            at = pl.ds(row + half * apart, 8, stride=24)
            for a in range(4):
                for kind in range(2):
                    parts.append(jnp.concatenate([grid[kind, 2 * a + j, at, :] for j in range(2)], 1))
        return jnp.concatenate(parts, 0)

    con = [band(core[0] * 4 + i, 8) for i in range(4)]
    ca = tcos[...]
    sa = tsin[...]
    f = first[core[0]]
    for v in range(4):
        val = band(16 + v, 4)
        for c in range(4):
            d = (val * con[c]).astype(jnp.bfloat16)
            y = jnp.dot(f, jnp.concatenate([d, d], 0), preferred_element_type=jnp.float32)
            a, b = y[:NA], y[NA:]
            uv = jnp.concatenate([a * ca - b * sa, a * sa + b * ca], 1)
            hi = uv.astype(jnp.bfloat16)
            at = slice((v * 4 + c) * NA, (v * 4 + c + 1) * NA)
            high[at, :] = hi
            low[at, :] = (uv - hi.astype(jnp.float32)).astype(jnp.bfloat16)
    for n in range(4):
        at = slice(n * 512, n * 512 + 512)
        y = jnp.dot(high[at, :], second[...], preferred_element_type=jnp.float32)
        z = jnp.dot(low[at, :], second[:, :NA], preferred_element_type=jnp.float32)
        x = (y[:, :NA] + (y[:, NA:] + z)).astype(jnp.bfloat16)
        for i in range(4):
            p = n * 4 + i
            spec[p * 64 : p * 64 + 64, 0:128] = x[i * NA : i * NA + 64]
            spec[p * 64 : p * 64 + 64, 128:256] = x[i * NA + 64 : i * NA + NA]


def pick(spec, gidx, meta, out):
    width = 1024

    def step(i, carry):
        at = pl.ds(pl.multiple_of(i * width, width), width)
        g = gidx[:, at]
        k1 = lax.bitwise_and(g, 127)
        kk = lax.shift_right_logical(k1, 6) * 128 + lax.shift_right_logical(g, 7)
        hot = jnp.where(
            lax.broadcasted_iota(jnp.int32, (256, width), 0) == kk, 1.0, 0.0
        ).astype(jnp.bfloat16)
        o = jnp.dot(spec[...], hot, preferred_element_type=jnp.float32)
        m = lax.broadcasted_iota(jnp.int32, (64, width), 0) == lax.bitwise_and(k1, 63)
        picked = jnp.sum(jnp.where(m[None], o.reshape(PAIRS, 64, width), 0.0), axis=1)
        out[:, at] = picked.astype(jnp.bfloat16)
        return carry

    lax.fori_loop(0, HALF // width, step, 0)
    out[:, HALF:WIDE] = meta[...]


def transform_kernel(core, mine, others, gidx, meta, first, tcos, tsin, second, spec, out, high, low, grid):
    transform(core, mine, others, first, tcos, tsin, second, spec, high, low, grid)
    pick(spec, gidx, meta, out)


def rho_spectrum(core, mine, others, gidx, meta, constants):
    return pl.pallas_call(
        transform_kernel,
        out_shape=[
            pltpu.VMEM((PAIRS * 64, 256), jnp.bfloat16),
            pltpu.VMEM((PAIRS, WIDE), jnp.bfloat16),
        ],
        in_specs=[SM] + [VM] * 8,
        out_specs=[VM] * 2,
        scratch_shapes=[pltpu.VMEM((PAIRS * NA, 2 * NB), jnp.bfloat16)] * 2
        + [pltpu.VMEM((2, 8, 8 * 24, LANES), jnp.float32)],
        compiler_params=PARAMS,
        name="rho_spectrum",
    )(core, mine, others, gidx, meta, *constants)


def rho_pick(spec, gidx, meta):
    return pl.pallas_call(
        pick,
        out_shape=pltpu.VMEM((PAIRS, WIDE), jnp.bfloat16),
        in_specs=[VM] * 3,
        out_specs=VM,
        compiler_params=PARAMS,
        name="rho_pick",
    )(spec, gidx, meta)


def device_index(x, y, z, c):
    return (z * 4 + (y >> 1) * 2 + c) * 8 + (y & 1) * 4 + x


CHIPS = tuple(itertools.product(range(4), repeat=3))


@functools.cache
def offset_pairs(offset):
    return tuple(
        (device_index(*chip, c), device_index(*((a + (1 - 2 * c) * b) % 4 for a, b in zip(chip, offset)), c))
        for chip in CHIPS for c in range(2)
    )


@functools.cache
def core_pairs():
    return tuple((device_index(*chip, c), device_index(*chip, 1 - c)) for chip in CHIPS for c in range(2))


def send(a, pairs):
    return lax.ppermute(a, ("ga", "ba"), pairs)


def level(a, offsets):
    return [a] + [send(a, offset_pairs(offset)) for offset in offsets[1:]]


def join_kernel(n, *refs):
    out = refs[n]
    row = 0
    for ref in refs[:n]:
        out[row : row + ref.shape[0], :] = ref[...]
        row += ref.shape[0]


def join(blocks):
    rows = sum(b.shape[0] for b in blocks)
    return pl.pallas_call(
        functools.partial(join_kernel, len(blocks)),
        out_shape=pltpu.VMEM((rows, WIDE), jnp.bfloat16),
        in_specs=[VM] * len(blocks),
        out_specs=VM,
        compiler_params=PARAMS,
        name="join",
    )(*blocks)


def deal_kernel(b0, b1, b2, b3, out0, out1, both):
    for i, ref in enumerate((b0, b1, b2, b3)):
        for half, out in enumerate((out0, out1)):
            rows = ref[half * 64 : half * 64 + 64, :]
            out[i * 64 : i * 64 + 64, :] = rows
            both[half * 256 + i * 64 : half * 256 + i * 64 + 64, :] = rows


def deal(blocks):
    return pl.pallas_call(
        deal_kernel,
        out_shape=[pltpu.VMEM((rows, WIDE), jnp.bfloat16) for rows in (256, 256, 512)],
        in_specs=[VM] * 4,
        out_specs=[VM] * 3,
        compiler_params=PARAMS,
        name="deal",
    )(*blocks)


def halves(refs):
    return [ref.at[pl.ds(at, 256)] for ref in refs for at in range(0, ref.shape[0], 256)]


def place_of(half, step):
    return [
        tuple(sum(v) % 4 for v in zip(NEAR[2 * half + i], EVEN[j], STEP[step]))
        for j in range(4) for i in range(2)
    ]


def mirrored(half, step):
    places = place_of(half, step)
    return [places.index(tuple(-v % 4 for v in p)) for p in places]


def weighted_kernel(place, omega, *refs):
    pieces, left = halves(refs[:-2]), refs[-1]
    w2 = omega[0] * omega[0]
    row = lax.broadcasted_iota(jnp.int32, (LANES, 2 * LANES), 0)
    lane = lax.broadcasted_iota(jnp.int32, (LANES, 2 * LANES), 1)
    spread = jnp.where((row < 3) & (lane < LANES) | (row == 3) & (lane >= LANES), 1.0, 0.0)
    spread = spread.astype(jnp.bfloat16)
    for i, piece in enumerate(pieces):
        m = jnp.dot(piece[:, HALF:WIDE], spread, preferred_element_type=jnp.float32)
        delta, taken = m[:, :LANES], m[:, LANES:]
        weight = (-4.0 / math.sqrt(NV * NC)) * taken * delta / (delta * delta + w2)
        for e in range(3):
            cols = pl.ds(pl.multiple_of(place[0] * ROWS + e * LANES, LANES), LANES)
            left[i * 256 : i * 256 + 256, e * LANES : (e + 1) * LANES] = (
                piece[:, cols].astype(jnp.float32) * weight
            ).astype(jnp.bfloat16)


def weighted(place, omega, pieces, tie):
    return pl.pallas_call(
        weighted_kernel,
        out_shape=pltpu.VMEM((sum(p.shape[0] for p in pieces), ROWS), jnp.bfloat16),
        in_specs=[SM, SM] + [VM] * (len(pieces) + 1),
        out_specs=VM,
        compiler_params=PARAMS,
        name="weighted",
    )(place, omega, *pieces, tie)


def product(names, other, left, pieces, cols):
    total = None
    for i, (half, step) in enumerate(names):
        if other:
            rows = []
            for j in mirrored(half, step):
                at = i * 256 + j * BLOCK
                rows += [left[at + PAIRS : at + BLOCK, :], left[at : at + PAIRS, :]]
            mine = jnp.concatenate(rows, 0)
        else:
            mine = left[i * 256 : i * 256 + 256, :]
        term = lax.dot_general(
            mine, pieces[i][:, cols], (((0,), (0,)), ((), ())), preferred_element_type=jnp.float32
        )
        total = term if total is None else total + term
    return total


def chunk(i, width=CHUNK, start=0):
    return pl.ds(pl.multiple_of(start + i * width, LANES), width)


def cost(names, columns):
    return pl.CostEstimate(
        flops=2 * ROWS * columns * 256 * len(names),
        bytes_accessed=(2 * 256 * len(names) + 8 * ROWS) * columns,
        transcendentals=0,
    )


def partial_kernel(names, n, other, left, *refs):
    pieces, before = halves(refs[:n]), refs[n:-3]
    out, after = refs[-2:]
    after[...] = jnp.zeros_like(after)

    def step(i, carry):
        total = product(names, other, left, pieces, chunk(i))
        out[:, chunk(i)] = total + before[0][:, chunk(i)] if before else total
        return carry

    lax.fori_loop(0, HALF // CHUNK, step, 0)


TIE = jax.ShapeDtypeStruct((8, LANES), jnp.float32)


def partial_rows(names, other, left, pieces, before, tie):
    before = [] if before is None else [before]
    return pl.pallas_call(
        functools.partial(partial_kernel, names, len(pieces), other),
        out_shape=[pltpu.VMEM((ROWS, HALF), jnp.float32), TIE],
        in_specs=[VM] * (2 + len(pieces) + len(before)),
        out_specs=[VM] * 2,
        input_output_aliases={1 + len(pieces): 0} if before else {},
        compiler_params=PARAMS,
        cost_estimate=cost(names, HALF),
        name="partial_other" if other else "partial_own",
    )(left, *pieces, *before, tie)


def own_kernel(names, n, start, core, left, *refs):
    pieces = halves(refs[:n])
    before, *swapped = refs[n:-6]
    out, tie, wide, sem, wide_swapped = refs[-5:]
    tie[...] = jnp.zeros_like(tie)
    copies = []

    def write(src, block, half, s):
        at = pl.multiple_of((block * 2 + half) * ROWS, LANES)
        copies.append(pltpu.make_async_copy(src, out.at[:, pl.ds(at, ROWS)], s))
        copies[-1].start()

    for row in swapped:
        for j in range(4):
            at = slice(j * ROWS, (j + 1) * ROWS)
            wide_swapped[:, at] = row[:, at].astype(jnp.float32)
            write(wide_swapped.at[:, pl.ds(j * ROWS, ROWS)], j, 1 - core[0], sem.at[4 + j])
    for i in range(2):
        cols = slice(start + i * CHUNK, start + (i + 1) * CHUNK)
        wide[:, i * CHUNK : (i + 1) * CHUNK] = product(names, False, left, pieces, cols) + before[:, cols]
        for j in (2 * i, 2 * i + 1):
            write(wide.at[:, pl.ds(j * ROWS, ROWS)], start // ROWS + j, core[0], sem.at[j])
    for copy in copies:
        copy.wait()


def own_rows(names, start, core, left, pieces, before, swapped, after):
    grows = after.shape == (ROWS, NG)
    return pl.pallas_call(
        functools.partial(own_kernel, names, len(pieces), start),
        out_shape=[jax.ShapeDtypeStruct((ROWS, NG), jnp.float32), TIE],
        in_specs=[SM, VM] + [VM] * (len(pieces) + 1 + len(swapped)) + [HBM if grows else VM],
        out_specs=[HBM, VM],
        scratch_shapes=[
            pltpu.VMEM((ROWS, HALF // 2), jnp.float32),
            pltpu.SemaphoreType.DMA((8,)),
            pltpu.VMEM((ROWS, HALF // 2) if swapped else (8, LANES), jnp.float32),
        ],
        input_output_aliases={3 + len(pieces) + len(swapped): 0} if grows else {},
        compiler_params=PARAMS,
        cost_estimate=cost(names, HALF // 2),
        name="own_rows",
    )(core, left, *pieces, before, *swapped, after)


def other_kernel(names, n, start, left, *refs):
    pieces = halves(refs[:n])
    before, _, out = refs[n:]

    def step(i, carry):
        total = product(names, True, left, pieces, chunk(i, start=start)) + before[:, chunk(i, start=start)]
        out[:, chunk(i)] = total.astype(jnp.bfloat16)
        return carry

    lax.fori_loop(0, 2, step, 0)


def other_rows(names, start, left, pieces, before, tie):
    return pl.pallas_call(
        functools.partial(other_kernel, names, len(pieces), start),
        out_shape=pltpu.VMEM((ROWS, HALF // 2), jnp.bfloat16),
        in_specs=[VM] * (len(pieces) + 3),
        out_specs=VM,
        compiler_params=PARAMS,
        cost_estimate=cost(names, HALF // 2),
        name="other_rows",
    )(left, *pieces, before, tie)


def finish_kernel(core, row, _, out, wide, sem):
    def copy(j):
        at = pl.multiple_of(((4 + j) * 2 + 1 - core[0]) * ROWS, LANES)
        return pltpu.make_async_copy(
            wide.at[:, pl.ds(j * ROWS, ROWS)], out.at[:, pl.ds(at, ROWS)], sem.at[j]
        )

    for j in range(4):
        at = slice(j * ROWS, (j + 1) * ROWS)
        wide[:, at] = row[:, at].astype(jnp.float32)
        copy(j).start()
    for j in range(4):
        copy(j).wait()


def finish(core, row, out):
    return pl.pallas_call(
        finish_kernel,
        out_shape=jax.ShapeDtypeStruct((ROWS, NG), jnp.float32),
        in_specs=[SM, VM, HBM],
        out_specs=HBM,
        scratch_shapes=[pltpu.VMEM((ROWS, HALF // 2), jnp.float32), pltpu.SemaphoreType.DMA((4,))],
        input_output_aliases={2: 0},
        compiler_params=PARAMS,
        name="finish",
    )(core, row, out)


def in_vmem(a):
    return pltpu.with_memory_space_constraint(a, pltpu.VMEM)


def on_device(psi_val, psi_con, e_val, e_con, occ, omega, g_index):
    ga = lax.axis_index("ga")
    ba = lax.axis_index("ba")
    core = lax.rem(ga, 2).astype(jnp.int32)
    kinds = [[2 * i + c for i in range(8)] for c in range(2)]
    rows, *constants = payload(psi_val, psi_con)
    psi = lax.all_to_all(rows, "ga", 0, 0, tiled=True, axis_index_groups=kinds)
    psi_other = send(psi, core_pairs())

    delta = (lax.dynamic_slice(e_con, (ga * 4,), (4,))[None, :] - e_val[:, None]).reshape(PAIRS)
    taken = jnp.broadcast_to(occ.astype(jnp.float32)[:, None], (4, 4)).reshape(PAIRS)
    d1 = lax.reduce_precision(delta, 8, 7)
    d2 = lax.reduce_precision(delta - d1, 8, 7)
    d3 = delta - d1 - d2
    meta = jnp.stack([d1, d2, d3, taken], 1).astype(jnp.bfloat16)
    meta = jnp.pad(meta, ((0, 0), (0, LANES - 4)))

    kinds_of_rows = g_index.reshape(8, 2, ROWS).transpose(1, 0, 2).reshape(2, HALF)
    kept = lax.dynamic_slice(kinds_of_rows, (core, 0), (1, HALF))
    given = lax.dynamic_slice(kinds_of_rows, (1 - core, 0), (1, HALF))
    spec, give = rho_spectrum(core.reshape(1), psi, psi_other, given, meta, constants)
    swapped = send(give, core_pairs())
    keep = rho_pick(spec, kept, meta)

    a = join(level(join([keep, swapped]), NEAR))
    *sources, both = deal(level(a, EVEN))
    got = {(h, 0): m for h, m in enumerate(sources)}
    for h in range(2):
        for s in (1, 2):
            got[h, s] = send(sources[h], offset_pairs(STEP[s]))
    got["z"] = send(both, offset_pairs(STEP[3]))

    place = lax.div(ga, 2).astype(jnp.int32).reshape(1)
    mine_omega = lax.dynamic_slice(omega, (ba,), (1,))
    core = core.reshape(1)
    own = other = None
    tie = jnp.zeros(TIE.shape, TIE.dtype)
    groups = (((0, 0), (1, 0)), ((0, 1), (0, 2)), ((1, 1), (1, 2), (0, 3), (1, 3)))
    for names in groups:
        held = names if names is not groups[-1] else (*names[:2], "z")
        pieces = [in_vmem(got[name]) for name in held]
        left = weighted(place, mine_omega, pieces, tie)
        mirror = send(left, core_pairs())
        if names is not groups[-1]:
            own, tie = partial_rows(names, False, left, pieces, own, tie)
            other, tie = partial_rows(names, True, mirror, pieces, other, tie)
    out, tie = own_rows(names, 0, core, left, pieces, own, [], tie)
    rows = [send(other_rows(names, s, mirror, pieces, other, tie), core_pairs()) for s in (0, HALF // 2)]
    out, _ = own_rows(names, HALF // 2, core, left, pieces, own, rows[:1], out)
    return finish(core, rows[1], out)[None]


def solution(mesh):
    placed = (P("ba", "ga"), P(None, "ga"), P("ba"), P(), P("ba"), P(), P())
    return jax.shard_map(
        on_device, mesh=mesh, in_specs=placed, out_specs=P("ba", "ga", None), check_vma=False
    )
```
